32 devices in a mesh: dp: 4 (over y, x), fsdp: 8 (over z, core).
Axes of the slice: x: 2, y: 2, z: 4, core: 2. Of those that a mesh axis runs over, the one named last changes fastest.
Arguments:
- feats: bfloat16 [192, 196, 1024], P(('dp', 'fsdp')), may hold values from -6 to 6
- text: bfloat16 [192, 64, 768], P(('dp', 'fsdp')), may hold values from -6 to 6
- lengths: int32 [192], P(('dp', 'fsdp')), may hold values from 1 to 64, as said below
- cotangent: bfloat16 [192, 260, 768], P(('dp', 'fsdp')), may hold values from -6 to 6
- w_red: bfloat16 [1024, 256], P(('dp', 'fsdp')), may hold values from -0.1875 to 0.1875
- bn1_gain: bfloat16 [256], P(('dp', 'fsdp')), may hold values from 0.5 to 1.5
- bn1_bias: bfloat16 [256], P(('dp', 'fsdp')), may hold values from -3 to 3
- w_conv: bfloat16 [2304, 256], P(('dp', 'fsdp')), may hold values from -0.125 to 0.125
- bn2_gain: bfloat16 [256], P(('dp', 'fsdp')), may hold values from 0.5 to 1.5
- bn2_bias: bfloat16 [256], P(('dp', 'fsdp')), may hold values from -3 to 3
- w_exp: bfloat16 [256, 1024], P(('dp', 'fsdp')), may hold values from -0.375 to 0.375
- bn3_gain: bfloat16 [1024], P(('dp', 'fsdp')), may hold values from 0.5 to 1.5
- bn3_bias: bfloat16 [1024], P(('dp', 'fsdp')), may hold values from -3 to 3
- w_patch: bfloat16 [1024, 768], P(('dp', 'fsdp')), may hold values from -0.1875 to 0.1875
- b_patch: bfloat16 [768], P(('dp', 'fsdp')), may hold values from -3 to 3
- ln1_gain: bfloat16 [768], P(('dp', 'fsdp')), may hold values from 0.25 to 1.75
- ln1_bias: bfloat16 [768], P(('dp', 'fsdp')), may hold values from -2 to 2
- w_qkv: bfloat16 [768, 2304], P(('dp', 'fsdp')), may hold values from -0.21875 to 0.21875
- b_qv: bfloat16 [1536], P(('dp', 'fsdp')), may hold values from -2 to 2
- w_out: bfloat16 [768, 768], P(('dp', 'fsdp')), may hold values from -0.625 to 0.625
- b_out: bfloat16 [768], P(('dp', 'fsdp')), may hold values from -2 to 2
- ln2_gain: bfloat16 [768], P(('dp', 'fsdp')), may hold values from 0.25 to 1.75
- ln2_bias: bfloat16 [768], P(('dp', 'fsdp')), may hold values from -2 to 2
- w_up: bfloat16 [768, 3072], P(('dp', 'fsdp')), may hold values from -0.21875 to 0.21875
- b_up: bfloat16 [3072], P(('dp', 'fsdp')), may hold values from -3 to 3
- w_down: bfloat16 [3072, 768], P(('dp', 'fsdp')), may hold values from -0.109375 to 0.109375
- b_down: bfloat16 [768], P(('dp', 'fsdp')), may hold values from -2 to 2
Outputs:
- output: bfloat16 [192, 260, 768], P(('dp', 'fsdp'))
- grad_feats: bfloat16 [192, 196, 1024], P(('dp', 'fsdp'))
- grad_text: bfloat16 [192, 64, 768], P(('dp', 'fsdp'))
- grad_w_red: float32 [1024, 256], P(('dp', 'fsdp'))
- grad_bn1_gain: float32 [256], P(('dp', 'fsdp'))
- grad_bn1_bias: float32 [256], P(('dp', 'fsdp'))
- grad_w_conv: float32 [2304, 256], P(('dp', 'fsdp'))
- grad_bn2_gain: float32 [256], P(('dp', 'fsdp'))
- grad_bn2_bias: float32 [256], P(('dp', 'fsdp'))
- grad_w_exp: float32 [256, 1024], P(('dp', 'fsdp'))
- grad_bn3_gain: float32 [1024], P(('dp', 'fsdp'))
- grad_bn3_bias: float32 [1024], P(('dp', 'fsdp'))
- grad_w_patch: float32 [1024, 768], P(('dp', 'fsdp'))
- grad_b_patch: float32 [768], P(('dp', 'fsdp'))
- grad_ln1_gain: float32 [768], P(('dp', 'fsdp'))
- grad_ln1_bias: float32 [768], P(('dp', 'fsdp'))
- grad_w_qkv: float32 [768, 2304], P(('dp', 'fsdp'))
- grad_b_qv: float32 [1536], P(('dp', 'fsdp'))
- grad_w_out: float32 [768, 768], P(('dp', 'fsdp'))
- grad_b_out: float32 [768], P(('dp', 'fsdp'))
- grad_ln2_gain: float32 [768], P(('dp', 'fsdp'))
- grad_ln2_bias: float32 [768], P(('dp', 'fsdp'))
- grad_w_up: float32 [768, 3072], P(('dp', 'fsdp'))
- grad_b_up: float32 [3072], P(('dp', 'fsdp'))
- grad_w_down: float32 [3072, 768], P(('dp', 'fsdp'))
- grad_b_down: float32 [768], P(('dp', 'fsdp'))
The draws below stay inside these ranges and needn't reach their ends.
Inputs may be any that keep to these rules, and one draw needn't show every extreme that they name: `lengths`: each example has 1 to 64 text tokens; some example has 64.
All inputs are finite; a program needn't handle non-finite values.
Results may differ from the reference program's by a relative error of at most 0.019.
Values may be sent and summed in bfloat16 or wider, within the bound.
A program may use at most 320 MiB of HBM per device.

```python
import jax
import jax.numpy as jnp
from jax import lax

D = 768
FF = 3072
HEADS = 12
HEAD_DIM = 64
CS = 1024
WB = 256
GRID = 14
TEXT = 64
PATCHES = 196
SEQ = 260
EXAMPLES = 192


def draw_lengths(key, part):
    key = jax.random.fold_in(key, 11)
    first_key, second_key, third_key, place_key = jax.random.split(key, 4)
    first_draw = jax.random.randint(first_key, (EXAMPLES,), 1, TEXT + 1)
    second_draw = jax.random.randint(second_key, (EXAMPLES,), 1, TEXT + 1)
    third_draw = jax.random.randint(third_key, (EXAMPLES,), 1, TEXT + 1)
    counts = jnp.maximum(first_draw * second_draw * third_draw // (TEXT * TEXT), 1)
    position = jax.random.randint(place_key, (), 0, EXAMPLES)
    counts = jnp.where(jnp.arange(EXAMPLES, dtype=jnp.int32) == position, TEXT, counts)
    return counts.astype(jnp.int32)


def level_of(own_key, extent, shards, low, high):
    level, own = 1.0, jax.random.fold_in(own_key, 6)
    for dim, blocks in shards:
        heights = jnp.exp(jax.random.uniform(jax.random.fold_in(own, dim), (blocks,), jnp.float32, low / len(shards), high / len(shards)))
        level = level * jnp.repeat(heights, extent[dim] // blocks).reshape([-1 if axis == dim else 1 for axis in range(len(extent))])
    return level


def normal_values(own_key, shape, deviation, reach, cuts=(), kind=jnp.bfloat16):
    drawn = jax.random.normal(own_key, shape, jnp.float32) * deviation
    if len(cuts) > 0:
        drawn = level_of(own_key, shape, cuts, -0.22, 0.18) * drawn
    return jnp.clip(drawn, min=-reach, max=reach).astype(kind)


def setup_inputs(seed: int = 0) -> dict:
    keys = jax.random.split(jax.random.key(seed), 28)
    feats = normal_values(keys[0], (EXAMPLES, PATCHES, CS), 1.0, 6.0, ((0, 32),))
    text = normal_values(keys[1], (EXAMPLES, TEXT, D), 1.0, 6.0, ((0, 32),))
    lengths = draw_lengths(jax.random.fold_in(keys[27], 71), 0)
    cotangent = normal_values(keys[3], (EXAMPLES, SEQ, D), 1.0, 6.0, ((0, 32),))
    w_red = normal_values(keys[4], (CS, WB), CS ** -0.5, 0.1875, ((0, 32),))
    bn1_gain = jnp.clip(1.0 + 0.1 * jax.random.normal(keys[5], (WB,), jnp.float32), 0.5, 1.5).astype(jnp.bfloat16)
    bn1_bias = normal_values(keys[6], (WB,), 0.5, 3.0, ((0, 32),))
    w_conv = normal_values(keys[7], (9 * WB, WB), (9 * WB) ** -0.5, 0.125, ((0, 32),))
    bn2_gain = jnp.clip(1.0 + 0.1 * jax.random.normal(keys[8], (WB,), jnp.float32), 0.5, 1.5).astype(jnp.bfloat16)
    bn2_bias = normal_values(keys[9], (WB,), 0.5, 3.0, ((0, 32),))
    w_exp = normal_values(keys[10], (WB, CS), WB ** -0.5, 0.375, ((0, 32),))
    bn3_gain = jnp.clip(1.0 + 0.1 * jax.random.normal(keys[11], (CS,), jnp.float32), 0.5, 1.5).astype(jnp.bfloat16)
    bn3_bias = normal_values(keys[12], (CS,), 0.5, 3.0, ((0, 32),))
    w_patch = normal_values(keys[13], (CS, D), CS ** -0.5, 0.1875, ((0, 32),))
    b_patch = normal_values(keys[14], (D,), 0.5, 3.0, ((0, 32),))
    ln1_gain = jnp.clip(1.0 + 0.15 * jax.random.normal(keys[15], (D,), jnp.float32), 0.25, 1.75).astype(jnp.bfloat16)
    ln1_bias = normal_values(keys[16], (D,), 0.3, 2.0, ((0, 32),))
    w_qkv = normal_values(keys[17], (D, 3 * D), D ** -0.5, 0.21875, ((0, 32),))
    b_qv = normal_values(keys[18], (2 * D,), 0.3, 2.0, ((0, 32),))
    w_out = normal_values(keys[19], (D, D), (D // 8) ** -0.5, 0.625, ((0, 32),))
    b_out = normal_values(keys[20], (D,), 0.3, 2.0, ((0, 32),))
    ln2_gain = jnp.clip(1.0 + 0.15 * jax.random.normal(keys[21], (D,), jnp.float32), 0.25, 1.75).astype(jnp.bfloat16)
    ln2_bias = normal_values(keys[22], (D,), 0.3, 2.0, ((0, 32),))
    w_up = normal_values(keys[23], (D, FF), D ** -0.5, 0.21875, ((0, 32),))
    b_up = normal_values(keys[24], (FF,), 0.5, 3.0, ((0, 32),))
    w_down = normal_values(keys[25], (FF, D), FF ** -0.5, 0.109375, ((0, 32),))
    b_down = normal_values(keys[26], (D,), 0.3, 2.0, ((0, 32),))
    return {"feats": feats, "text": text, "lengths": lengths, "cotangent": cotangent, "w_red": w_red, "bn1_gain": bn1_gain, "bn1_bias": bn1_bias, "w_conv": w_conv, "bn2_gain": bn2_gain, "bn2_bias": bn2_bias, "w_exp": w_exp, "bn3_gain": bn3_gain, "bn3_bias": bn3_bias, "w_patch": w_patch, "b_patch": b_patch, "ln1_gain": ln1_gain, "ln1_bias": ln1_bias, "w_qkv": w_qkv, "b_qv": b_qv, "w_out": w_out, "b_out": b_out, "ln2_gain": ln2_gain, "ln2_bias": ln2_bias, "w_up": w_up, "b_up": b_up, "w_down": w_down, "b_down": b_down}


ln_eps = 1e-06
bn_eps = 1e-05
gelu_coef = 0.7978845608028654

@jax.custom_vjp
def low(v):
    return lax.optimization_barrier(v.astype(jnp.bfloat16)).astype(jnp.float32)

@jax.custom_vjp
def low_back(v):
    return v

def low_keep(v):
    return (low(v), None)

def low_pass(kept, grad):
    return (grad,)

def back_keep(v):
    return (v, None)

def back_low(kept, grad):
    return (low(grad),)
low.defvjp(low_keep, low_pass)
low_back.defvjp(back_keep, back_low)

def smooth(values):
    return 0.5 * values * (1.0 + jnp.tanh(gelu_coef * (values + 0.044715 * values * values * values)))

def normed(values, gain_vec, shift_vec):
    center = values - lax.optimization_barrier(jnp.mean(values, -1, keepdims=True))
    return center * lax.rsqrt(lax.optimization_barrier(jnp.mean(center * center, -1, keepdims=True)) + ln_eps) * gain_vec + shift_vec

def batch_normed(values, gain_vec, shift_vec):
    center = values - lax.optimization_barrier(jnp.mean(values, 0))
    return center * lax.rsqrt(lax.optimization_barrier(jnp.mean(center * center, 0)) + bn_eps) * gain_vec + shift_vec

def unfold(maps):
    grid_size = maps.shape[1]
    padded = jnp.pad(maps, ((0, 0), (1, 1), (1, 1), (0, 0)))
    pieces = [padded[:, row_off:row_off + grid_size, col_off:col_off + grid_size, :] for row_off in range(3) for col_off in range(3)]
    return jnp.concatenate(pieces, -1).reshape(-1, 9 * maps.shape[3])

def matmul(left, right):
    return jnp.dot(left, right, precision=lax.Precision.HIGHEST, preferred_element_type=jnp.float32)

def attend(inputs):
    query, key_part, value_part, valid = inputs
    scores = low_back(jnp.einsum('qhd,khd->hqk', query, key_part, precision=lax.Precision.HIGHEST) * HEAD_DIM ** (-0.5))
    scores = jnp.where(valid[None, None, :] > 0.5, scores, -1e+30)
    top_score = lax.optimization_barrier(jnp.max(scores, -1, keepdims=True))
    expo_scores = jnp.exp(scores - top_score)
    probs = low(expo_scores / lax.optimization_barrier(jnp.sum(expo_scores, -1, keepdims=True)))
    return jnp.einsum('hqk,khd->qhd', probs, value_part, precision=lax.Precision.HIGHEST)

def forward(feats, text, keep, weights):
    w_red, bn1_gain, bn1_bias, w_conv, bn2_gain, bn2_bias, w_exp, bn3_gain, bn3_bias, w_patch, b_patch, ln1_gain, ln1_bias, w_qkv, b_qv, w_out, b_out, ln2_gain, ln2_bias, w_up, b_up, w_down, b_down = weights
    examples = feats.shape[0]
    feat_rows = feats.reshape(-1, CS)
    red_pre = low_back(matmul(feat_rows, w_red))
    red_act = low(smooth(batch_normed(red_pre, bn1_gain, bn1_bias)))
    columns = unfold(red_act.reshape(examples, GRID, GRID, WB))
    conv_pre = low_back(matmul(columns, w_conv))
    conv_act = low(smooth(batch_normed(conv_pre, bn2_gain, bn2_bias)))
    expand_pre = low_back(matmul(conv_act, w_exp))
    stem_act = low(smooth(batch_normed(expand_pre, bn3_gain, bn3_bias) + feat_rows))
    patch = low_back(matmul(stem_act, w_patch) + b_patch).reshape(examples, PATCHES, D)
    valid = jnp.concatenate([jnp.ones((examples, PATCHES), jnp.float32), keep], 1)
    stream = jnp.concatenate([patch, text * keep[:, :, None]], 1).reshape(-1, D)
    first_norm = low(normed(stream, ln1_gain, ln1_bias))
    qkv_bias = jnp.concatenate([b_qv[:D], jnp.zeros((D,), jnp.float32), b_qv[D:]])
    qkv = low(low_back(matmul(first_norm, w_qkv) + qkv_bias)).reshape(examples, SEQ, 3, HEADS, HEAD_DIM)
    mixed = lax.map(jax.checkpoint(attend), (qkv[:, :, 0], qkv[:, :, 1], qkv[:, :, 2], valid))
    mixed = low(low_back(mixed.reshape(-1, D)))
    second = stream + low_back(matmul(mixed, w_out) + b_out)
    second_norm = low(normed(second, ln2_gain, ln2_bias))
    hidden = low(smooth(low_back(matmul(second_norm, w_up) + b_up)))
    result = second + low_back(matmul(hidden, w_down) + b_down)
    return result.reshape(examples, SEQ, D) * valid[:, :, None]

def reference(feats, text, lengths, cotangent, w_red, bn1_gain, bn1_bias, w_conv, bn2_gain, bn2_bias, w_exp, bn3_gain, bn3_bias, w_patch, b_patch, ln1_gain, ln1_bias, w_qkv, b_qv, w_out, b_out, ln2_gain, ln2_bias, w_up, b_up, w_down, b_down):
    keep = (jnp.arange(TEXT, dtype=jnp.int32)[None, :] < lengths[:, None]).astype(jnp.float32)
    weights = tuple((weight_arg.astype(jnp.float32) for weight_arg in (w_red, bn1_gain, bn1_bias, w_conv, bn2_gain, bn2_bias, w_exp, bn3_gain, bn3_bias, w_patch, b_patch, ln1_gain, ln1_bias, w_qkv, b_qv, w_out, b_out, ln2_gain, ln2_bias, w_up, b_up, w_down, b_down)))

    def run(feat_values, text_values, weight_values):
        return forward(feat_values, text_values, keep, weight_values)
    output, backward = jax.vjp(run, feats.astype(jnp.float32), text.astype(jnp.float32), weights)
    grad_feats, grad_text, grad_weights = backward(cotangent.astype(jnp.float32))
    return (output.astype(jnp.bfloat16), grad_feats.astype(jnp.bfloat16), grad_text.astype(jnp.bfloat16)) + tuple(grad_weights)
```

```python
import functools

import jax
import jax.numpy as jnp
from jax import lax
from jax.experimental import pallas as pl
from jax.experimental.pallas import tpu as pltpu
from jax.sharding import PartitionSpec as P

HEAD_DIM = 64
GRID = 14


ln_eps = 1e-06
bn_eps = 1e-05
gelu_coef = 0.7978845608028654


MESH = pl.DeviceIdType.MESH
DMA = pltpu.SemaphoreType.DMA


def rcopy(src, dst, send, recv, dev):
    return pltpu.make_async_remote_copy(
        src_ref=src, dst_ref=dst, send_sem=send, recv_sem=recv, device_id=dev, device_id_type=MESH
    )


class Place:
    def __init__(self, A, B):
        self.A, self.B, self.A2, self.Z = A, B, A // 2, B // 2
        a, b = lax.axis_index("dp"), lax.axis_index("fsdp")
        self.a, self.b = a, b
        self.y, self.x = a // 2, lax.rem(a, 2)
        self.z, self.c = b // 2, lax.rem(b, 2)
        self.zs = [lax.rem(self.z + k, self.Z) for k in range(1, self.Z)]
        self.ys = [lax.rem(self.y + k, self.A2) for k in range(1, self.A2)]
        self.zfrom = [lax.rem(self.z + self.Z - k, self.Z) for k in range(1, self.Z)]
        self.yfrom = [lax.rem(self.y + self.A2 - k, self.A2) for k in range(1, self.A2)]
        self.me = (a, b)
        self.core = (a, self.z * 2 + 1 - self.c)
        self.xpeer = (self.y * 2 + 1 - self.x, b)
        self.zpeers = [(a, zz * 2 + self.c) for zz in self.zs]
        self.ypeers = [(yy * 2 + self.x, b) for yy in self.ys]

    def greet(self):
        peers = self.zpeers + self.ypeers + [self.xpeer, self.core]
        bar = pltpu.get_barrier_semaphore()
        for p in peers:
            pl.semaphore_signal(bar, inc=1, device_id=p, device_id_type=MESH)
        pl.semaphore_wait(bar, len(peers))


class GatherItem:
    def __init__(self, pc, i, cols, order, src, out, sems):
        self.pc, self.order, self.src = pc, order, src
        self.o = out if cols is None else out.at[:, :, :, :, :, pl.ds(*cols)]
        if cols is not None:
            self.src = src.at[:, pl.ds(*cols)]
        self.loc, self.s1, self.r1, self.s2, self.r2, self.s3, self.r3, self.sc, self.rc = [s.at[i] for s in sems]
        self.sends, self.corew = [], []

    def go(self, d):
        d.start()
        self.sends.append(d)

    def core(self, j, got, mirror):
        self.go(rcopy(got, got, self.sc.at[j], self.rc.at[j], self.pc.core))
        self.corew.append((j, mirror))

    def start(self):
        p = self.pc
        mine = self.o.at[p.y, p.x, p.z, p.c]
        self.local = pltpu.make_async_copy(self.src, mine, self.loc)
        self.local.start()
        for k, dev in enumerate(p.zpeers):
            self.go(rcopy(self.src, mine, self.s1.at[k], self.r1.at[k], dev))

    def second(self):
        p = self.pc
        self.local.wait()
        for k, zz in enumerate(p.zfrom):
            got = self.o.at[p.y, p.x, zz, p.c]
            rcopy(got, got, self.s1.at[k], self.r1.at[k], p.me).wait_recv()
        col = self.o.at[p.y, p.x, :, p.c]
        for k, dev in enumerate([p.xpeer] if self.order == 0 else p.ypeers):
            self.go(rcopy(col, col, self.s2.at[k], self.r2.at[k], dev))
        self.core(0, col, self.o.at[p.y, p.x, :, 1 - p.c])

    def third(self):
        p, o = self.pc, self.o
        froms = [(p.y, 1 - p.x)] if self.order == 0 else [(yy, p.x) for yy in p.yfrom]
        blk = o.at[p.y, :, :, p.c] if self.order == 0 else o.at[:, p.x, :, p.c]
        for k, (yy, xx) in enumerate(froms):
            got = o.at[yy, xx, :, p.c]
            rcopy(got, got, self.s2.at[k], self.r2.at[k], p.me).wait_recv()
        for k, dev in enumerate(p.ypeers if self.order == 0 else [p.xpeer]):
            self.go(rcopy(blk, blk, self.s3.at[k], self.r3.at[k], dev))
        for k, (yy, xx) in enumerate(froms):
            self.core(1 + k, o.at[yy, xx, :, p.c], o.at[yy, xx, :, 1 - p.c])

    def fourth(self):
        p, o = self.pc, self.o
        base = 1 + (1 if self.order == 0 else p.A2 - 1)
        froms = [((yy, slice(None)),) for yy in p.yfrom] if self.order == 0 else [None]
        if self.order == 0:
            gots = [(o.at[yy, :, :, p.c], o.at[yy, :, :, 1 - p.c]) for yy in p.yfrom]
        else:
            gots = [(o.at[:, 1 - p.x, :, p.c], o.at[:, 1 - p.x, :, 1 - p.c])]
        for k, (got, mirror) in enumerate(gots):
            rcopy(got, got, self.s3.at[k], self.r3.at[k], p.me).wait_recv()
            self.core(base + k, got, mirror)

    def arrived(self):
        for j, got in self.corew:
            rcopy(got, got, self.sc.at[j], self.rc.at[j], self.pc.me).wait_recv()

    def drain(self):
        for d in self.sends:
            d.wait_send()


def gather_sems(A, B, n):
    A2, Z = A // 2, B // 2
    m = max(A2 - 1, 1)
    return [DMA((n,)), DMA((n, Z - 1)), DMA((n, Z - 1)), DMA((n, m)), DMA((n, m)), DMA((n, m)), DMA((n, m)), DMA((n, A2 + 1)), DMA((n, A2 + 1))]


def wave(items, lags, stages):
    last = len(items) + lags[-1]
    for t in range(last):
        for lag, stage in zip(reversed(lags), reversed(stages)):
            if 0 <= t - lag < len(items):
                getattr(items[t - lag], stage)()


def gather_kernel(A, B, items, n, lags, *refs):
    ins, outs, sems = refs[:n], refs[n : 2 * n], refs[2 * n :]
    pc = Place(A, B)
    pc.greet()
    moves = [GatherItem(pc, j, cols, order, ins[i], outs[i], sems) for j, (i, cols, order) in enumerate(items)]
    wave(moves, lags, ["start", "second", "third", "fourth"])
    for m in moves:
        m.arrived()
    for m in moves:
        m.drain()


def cut(widths_parts):
    items, order = [], 0
    for i, (width, parts) in enumerate(widths_parts):
        for q in range(parts):
            items.append((i, None if parts == 1 else (q * (width // parts), width // parts), order))
            order = 1 - order
    return items


def gather(A, B, shards, parts, cid, lags=(0, 2, 4, 6)):
    n = len(shards)
    A2, Z = A // 2, B // 2
    items = cut([(s.shape[1], q) for s, q in zip(shards, parts)])
    return pl.pallas_call(
        functools.partial(gather_kernel, A, B, items, n, lags),
        out_shape=[jax.ShapeDtypeStruct((A2, 2, Z, 2) + s.shape, s.dtype) for s in shards],
        in_specs=[pl.BlockSpec(memory_space=pl.ANY)] * n,
        out_specs=[pl.BlockSpec(memory_space=pl.ANY)] * n,
        scratch_shapes=gather_sems(A, B, len(items)),
        compiler_params=pltpu.CompilerParams(collective_id=cid, has_side_effects=True),
        name="gather",
    )(*shards)


class ScatterItem:
    def __init__(self, pc, i, order, src, out, own, r0, r1, r2, r3, sems):
        self.pc, self.order, self.src, self.out = pc, order, src, out
        self.own, self.r0, self.r1, self.r2, self.r3 = own, r0, r1, r2, r3
        self.loc, self.s0, self.q0, self.s1, self.q1, self.s2, self.q2, self.s3, self.q3 = [s.at[i] for s in sems]
        self.sends = []

    def go(self, d):
        d.start()
        self.sends.append(d)

    def start(self):
        p = self.pc
        self.go(rcopy(self.src.at[:, :, :, 1 - p.c], self.r0, self.s0, self.q0, p.core))
        self.local = pltpu.make_async_copy(self.src.at[:, :, :, p.c], self.own, self.loc)
        self.local.start()

    def add(self, dst, others, lead):
        total = 1
        for d in lead:
            total *= d

        def body(t, _):
            idx, rest = [], t
            for d in reversed(lead):
                idx.append(lax.rem(rest, d))
                rest = rest // d
            idx = tuple(reversed(idx))
            v = dst[idx].astype(jnp.float32)
            for o in others:
                v = v + o[idx].astype(jnp.float32)
            dst[idx] = v.astype(jnp.bfloat16)
            return 0

        lax.fori_loop(0, total, body, 0)

    def second(self):
        p = self.pc
        self.local.wait()
        rcopy(self.r0, self.r0, self.s0, self.q0, p.me).wait_recv()
        self.add(self.own, [self.r0], (p.A2, 2, p.Z))
        if self.order == 0:
            self.go(rcopy(self.own.at[:, 1 - p.x], self.r1.at[0], self.s1.at[0], self.q1.at[0], p.xpeer))
        else:
            for k, yy in enumerate(p.ys):
                self.go(rcopy(self.own.at[yy], self.r1.at[k], self.s1.at[k], self.q1.at[k], p.ypeers[k]))

    def third(self):
        p = self.pc
        n1 = 1 if self.order == 0 else p.A2 - 1
        for k in range(n1):
            rcopy(self.r1.at[k], self.r1.at[k], self.s1.at[k], self.q1.at[k], p.me).wait_recv()
        mine = self.own.at[:, p.x] if self.order == 0 else self.own.at[p.y]
        self.add(mine, [self.r1.at[k] for k in range(n1)], (p.A2 if self.order == 0 else 2, p.Z))
        if self.order == 0:
            for k, yy in enumerate(p.ys):
                self.go(rcopy(self.own.at[yy, p.x], self.r2.at[k], self.s2.at[k], self.q2.at[k], p.ypeers[k]))
        else:
            self.go(rcopy(self.own.at[p.y, 1 - p.x], self.r2.at[0], self.s2.at[0], self.q2.at[0], p.xpeer))

    def fourth(self):
        p = self.pc
        n2 = p.A2 - 1 if self.order == 0 else 1
        for k in range(n2):
            rcopy(self.r2.at[k], self.r2.at[k], self.s2.at[k], self.q2.at[k], p.me).wait_recv()
        self.add(self.own.at[p.y, p.x], [self.r2.at[k] for k in range(n2)], (p.Z,))
        for k, zz in enumerate(p.zs):
            self.go(rcopy(self.own.at[p.y, p.x, zz], self.r3.at[k], self.s3.at[k], self.q3.at[k], p.zpeers[k]))

    def arrived(self):
        p = self.pc
        for k in range(p.Z - 1):
            rcopy(self.r3.at[k], self.r3.at[k], self.s3.at[k], self.q3.at[k], p.me).wait_recv()
        v = self.own[p.y, p.x, p.z].astype(jnp.float32)
        for k in range(p.Z - 1):
            v = v + self.r3[k].astype(jnp.float32)
        self.out[...] = v

    def drain(self):
        for d in self.sends:
            d.wait_send()


def scatter_sems(A, B, n):
    m, Z = max(A // 2 - 1, 1), B // 2
    return [DMA((n,)), DMA((n,)), DMA((n,)), DMA((n, m)), DMA((n, m)), DMA((n, m)), DMA((n, m)), DMA((n, Z - 1)), DMA((n, Z - 1))]


def scatter_scratch(A, B, shape, order):
    A2, Z = A // 2, B // 2
    n1 = (1, A2, Z) if order == 0 else (A2 - 1, 2, Z)
    n2 = (A2 - 1, Z) if order == 0 else (1, Z)
    return [pltpu.VMEM(s + shape, jnp.bfloat16) for s in ((A2, 2, Z), (A2, 2, Z), n1, n2, (Z - 1,))]


def scatter_kernel(A, B, orders, lags, n, *refs):
    ins, outs, bufs, sems = refs[:n], refs[n : 2 * n], refs[2 * n : 7 * n], refs[7 * n :]
    pc = Place(A, B)
    pc.greet()
    moves = [ScatterItem(pc, i, orders[i], ins[i], outs[i], *bufs[5 * i : 5 * i + 5], sems) for i in range(n)]
    wave(moves, lags, ["start", "second", "third", "fourth", "arrived"])
    for m in moves:
        m.drain()


def scatter(A, B, grads, cid, lags=(0, 1, 3, 5, 7)):
    n = len(grads)
    A2, Z = A // 2, B // 2
    shapes = [(g.shape[0] // (A * B), g.shape[1]) for g in grads]
    orders = [i % 2 for i in range(n)]
    scratch = []
    for s, o in zip(shapes, orders):
        scratch += scatter_scratch(A, B, s, o)
    return pl.pallas_call(
        functools.partial(scatter_kernel, A, B, orders, lags, n),
        out_shape=[jax.ShapeDtypeStruct(s, jnp.float32) for s in shapes],
        in_specs=[pl.BlockSpec(memory_space=pl.ANY)] * n,
        out_specs=[pl.BlockSpec(memory_space=pltpu.VMEM)] * n,
        scratch_shapes=scratch + scatter_sems(A, B, n),
        compiler_params=pltpu.CompilerParams(collective_id=cid, has_side_effects=True, vmem_limit_bytes=56 << 20),
        name="scatter",
    )(*[g.reshape((A2, 2, Z, 2) + s) for g, s in zip(grads, shapes)])


def flips(A, B):
    a, b = lax.axis_index("dp"), lax.axis_index("fsdp")
    out = []
    bit = 1
    while bit < B:
        out.append((a, b + bit - 2 * bit * lax.rem(b // bit, 2)))
        bit *= 2
    bit = 1
    while bit < A:
        out.append((a + bit - 2 * bit * lax.rem(a // bit, 2), b))
        bit *= 2
    return out


def total_kernel(A, B, x_ref, o_ref, out_buf, in_buf, ssem, rsem):
    peers = flips(A, B)
    bar = pltpu.get_barrier_semaphore()
    for p in peers:
        pl.semaphore_signal(bar, inc=1, device_id=p, device_id_type=MESH)
    pl.semaphore_wait(bar, len(peers))
    v = x_ref[...]
    sends = []
    for k, p in enumerate(peers):
        out_buf[k] = v
        d = rcopy(out_buf.at[k], in_buf.at[k], ssem.at[k], rsem.at[k], p)
        d.start()
        sends.append(d)
        d.wait_recv()
        v = v + in_buf[k]
    o_ref[...] = v
    for d in sends:
        d.wait_send()


def total(A, B, x, cid):
    h = (A.bit_length() - 1) + (B.bit_length() - 1)
    vm = pl.BlockSpec(memory_space=pltpu.VMEM)
    return pl.pallas_call(
        functools.partial(total_kernel, A, B),
        out_shape=jax.ShapeDtypeStruct(x.shape, x.dtype),
        in_specs=[vm],
        out_specs=vm,
        scratch_shapes=[pltpu.VMEM((h,) + x.shape, x.dtype), pltpu.VMEM((h,) + x.shape, x.dtype), DMA((h,)), DMA((h,))],
        compiler_params=pltpu.CompilerParams(collective_id=cid, has_side_effects=True),
        name="total",
    )(x)


def smooth(values):
    return (
        0.5 * values * (1.0 + jnp.tanh(gelu_coef * (values + 0.044715 * values * values * values)))
    )


def normed(values, gain_vec, shift_vec):
    center = values - jnp.mean(values, -1, keepdims=True)
    return (
        center * lax.rsqrt(jnp.mean(center * center, -1, keepdims=True) + ln_eps) * gain_vec
        + shift_vec
    )


def unfold(maps):
    grid_size = maps.shape[1]
    padded = jnp.pad(maps, ((0, 0), (1, 1), (1, 1), (0, 0)))
    pieces = [
        padded[:, row_off : row_off + grid_size, col_off : col_off + grid_size, :]
        for row_off in range(3)
        for col_off in range(3)
    ]
    return jnp.concatenate(pieces, -1).reshape(-1, 9 * maps.shape[3])


def matmul(left, right):
    return jnp.dot(left, right, preferred_element_type=jnp.float32)


def left_product(left, right):
    return lax.dot_general(
        left, right, (((0,), (0,)), ((), ())), preferred_element_type=jnp.float32
    )


def right_product(left, right):
    return lax.dot_general(
        left, right, (((1,), (1,)), ((), ())), preferred_element_type=jnp.float32
    )


def summed(first, second):
    A, B = lax.axis_size("dp"), lax.axis_size("fsdp")
    width = first.shape[0]
    if width < 1024:
        first, second = (jnp.pad(v, (0, 1024 - width)) for v in (first, second))
    both = total(A, B, jnp.pad(jnp.stack([first, second]), ((0, 6), (0, 0))), 2)
    return both[0, :width], both[1, :width]


def vectors_summed(vectors):
    A, B = lax.axis_size("dp"), lax.axis_size("fsdp")
    flat = jnp.concatenate(vectors)
    wide = total(A, B, flat.reshape(-1, 128), 3).reshape(-1)
    out, at = [], 0
    for v in vectors:
        out.append(wide[at : at + v.shape[0]])
        at += v.shape[0]
    return out


def gather_all(matrices, vectors):
    A, B = lax.axis_size("dp"), lax.axis_size("fsdp")
    pack = jnp.pad(jnp.stack([jnp.pad(v, (0, 128 - v.shape[0])) for v in vectors]), ((0, 32 - len(vectors)), (0, 0)))
    parts = (1, 1, 1, 1, 1, 3, 1, 4, 3)
    got = gather(A, B, [pack] + list(matrices), parts, 0)
    whole = [g.reshape((-1,) + g.shape[-1:]) for g in got[1:]]
    table = got[0].reshape(-1, 32, 128)
    return whole, [table[:, i, : v.shape[0]].reshape(-1) for i, v in enumerate(vectors)]


def batch_forward(pre_values, gain_vec, shift_vec):
    column_sum, column_squares = summed(jnp.sum(pre_values, 0), jnp.sum(pre_values * pre_values, 0))
    total_rows = pre_values.shape[0] * lax.axis_size(("dp", "fsdp"))
    batch_mean = column_sum / total_rows
    inv_std = lax.rsqrt(column_squares / total_rows - batch_mean * batch_mean + bn_eps)
    norm_part = (pre_values - batch_mean) * inv_std
    return (
        norm_part * gain_vec.astype(jnp.float32) + shift_vec.astype(jnp.float32),
        norm_part,
        inv_std,
    )


def batch_backward(grad_shift, norm_part, inv_std, gain_vec):
    total_rows = grad_shift.shape[0] * lax.axis_size(("dp", "fsdp"))
    total_bias, total_gain = summed(jnp.sum(grad_shift, 0), jnp.sum(grad_shift * norm_part, 0))
    grad_pre = (
        inv_std
        * gain_vec.astype(jnp.float32)
        * (grad_shift - total_bias / total_rows - norm_part * total_gain / total_rows)
    )
    return (grad_pre.astype(jnp.bfloat16), total_gain, total_bias)


def own_share(whole, share):
    return lax.dynamic_slice_in_dim(whole, lax.axis_index(("dp", "fsdp")) * share, share, 0)


def smooth_grad(point, grad_out):
    _, smooth_back = jax.vjp(smooth, point)
    return smooth_back(grad_out)[0]


def forward_pass(feats, text, lengths, weights):
    (
        w_red,
        bn1_gain,
        bn1_bias,
        w_conv,
        bn2_gain,
        bn2_bias,
        w_exp,
        bn3_gain,
        bn3_bias,
        w_patch,
        b_patch,
        ln1_gain,
        ln1_bias,
        w_qkv,
        b_qv,
        w_out,
        b_out,
        ln2_gain,
        ln2_bias,
        w_up,
        b_up,
        w_down,
        b_down,
    ) = weights
    examples, patches, channels = feats.shape
    grid_size = GRID
    bottleneck = w_red.shape[1]
    text_slots = text.shape[1]
    model_width = text.shape[2]
    head_count = model_width // HEAD_DIM
    seq_len = patches + text_slots
    feat_rows = feats.reshape(-1, channels)
    red_pre = matmul(feat_rows, w_red)
    red_shift, red_norm, red_inv = batch_forward(red_pre, bn1_gain, bn1_bias)
    red_act = smooth(red_shift).astype(jnp.bfloat16)
    columns = unfold(red_act.reshape(examples, grid_size, grid_size, bottleneck))
    conv_pre = matmul(columns, w_conv)
    conv_shift, conv_norm, conv_inv = batch_forward(conv_pre, bn2_gain, bn2_bias)
    conv_act = smooth(conv_shift).astype(jnp.bfloat16)
    expand_pre = matmul(conv_act, w_exp)
    expand_shift, expand_norm, expand_inv = batch_forward(expand_pre, bn3_gain, bn3_bias)
    joined = expand_shift + feat_rows.astype(jnp.float32)
    stem_act = smooth(joined).astype(jnp.bfloat16)
    patch = matmul(stem_act, w_patch) + b_patch.astype(jnp.float32)
    keep = (jnp.arange(text_slots, dtype=jnp.int32)[None, :] < lengths[:, None]).astype(jnp.float32)
    valid = jnp.concatenate([jnp.ones((examples, patches), jnp.float32), keep], 1)
    stream = jnp.concatenate(
        [
            patch.reshape(examples, patches, model_width),
            text.astype(jnp.float32) * keep[:, :, None],
        ],
        1,
    ).reshape(-1, model_width)
    first_norm = normed(stream, ln1_gain.astype(jnp.float32), ln1_bias.astype(jnp.float32)).astype(
        jnp.bfloat16
    )
    qkv_bias = jnp.concatenate(
        [b_qv[:model_width], jnp.zeros((model_width,), jnp.bfloat16), b_qv[model_width:]]
    ).astype(jnp.float32)
    qkv = (matmul(first_norm, w_qkv) + qkv_bias).astype(jnp.bfloat16)
    qkv = qkv.reshape(examples, seq_len, 3, head_count, HEAD_DIM)
    query = qkv[:, :, 0]
    key_part = qkv[:, :, 1]
    value_part = qkv[:, :, 2]
    scores = jnp.einsum(
        "eqhd,ekhd->ehqk", query, key_part, preferred_element_type=jnp.float32
    ) * HEAD_DIM ** (-0.5)
    scores = jnp.where(valid[:, None, None, :] > 0.5, scores, -1e30)
    top_score = jnp.max(scores, -1, keepdims=True)
    expo_scores = jnp.exp(scores - top_score)
    probs = expo_scores / jnp.sum(expo_scores, -1, keepdims=True)
    probs_low = probs.astype(jnp.bfloat16)
    mixed = jnp.einsum("ehqk,ekhd->eqhd", probs_low, value_part, preferred_element_type=jnp.float32)
    mixed = mixed.astype(jnp.bfloat16).reshape(-1, model_width)
    second = stream + matmul(mixed, w_out) + b_out.astype(jnp.float32)
    second_norm = normed(second, ln2_gain.astype(jnp.float32), ln2_bias.astype(jnp.float32)).astype(
        jnp.bfloat16
    )
    upper = matmul(second_norm, w_up) + b_up.astype(jnp.float32)
    hidden = smooth(upper).astype(jnp.bfloat16)
    result = second + matmul(hidden, w_down) + b_down.astype(jnp.float32)
    output = (result.reshape(examples, seq_len, model_width) * valid[:, :, None]).astype(
        jnp.bfloat16
    )
    saved = dict(
        feat_rows=feat_rows,
        red_shift=red_shift,
        red_norm=red_norm,
        red_inv=red_inv,
        red_act=red_act,
        columns=columns,
        conv_shift=conv_shift,
        conv_norm=conv_norm,
        conv_inv=conv_inv,
        conv_act=conv_act,
        expand_norm=expand_norm,
        expand_inv=expand_inv,
        joined=joined,
        stem_act=stem_act,
        keep=keep,
        valid=valid,
        stream=stream,
        first_norm=first_norm,
        query=query,
        key_part=key_part,
        value_part=value_part,
        probs=probs,
        probs_low=probs_low,
        mixed=mixed,
        second=second,
        second_norm=second_norm,
        upper=upper,
        hidden=hidden,
    )
    return (output, saved)


def local(
    feats,
    text,
    lengths,
    cotangent,
    w_red,
    bn1_gain,
    bn1_bias,
    w_conv,
    bn2_gain,
    bn2_bias,
    w_exp,
    bn3_gain,
    bn3_bias,
    w_patch,
    b_patch,
    ln1_gain,
    ln1_bias,
    w_qkv,
    b_qv,
    w_out,
    b_out,
    ln2_gain,
    ln2_bias,
    w_up,
    b_up,
    w_down,
    b_down,
):
    mats, vecs = gather_all((w_red, w_conv, w_exp, w_patch, w_qkv, w_out, w_up, w_down), (bn1_gain, bn1_bias, bn2_gain, bn2_bias, bn3_gain, bn3_bias, b_patch, ln1_gain, ln1_bias, b_qv, b_out, ln2_gain, ln2_bias, b_up, b_down))
    gathered = (mats[0], vecs[0], vecs[1], mats[1], vecs[2], vecs[3], mats[2], vecs[4], vecs[5], mats[3], vecs[6], vecs[7], vecs[8], mats[4], vecs[9], mats[5], vecs[10], vecs[11], vecs[12], mats[6], vecs[13], mats[7], vecs[14])
    output, saved = forward_pass(feats, text, lengths, gathered)
    weights = gathered
    (
        full_red,
        full_bn1_gain,
        full_bn1_bias,
        full_conv,
        full_bn2_gain,
        full_bn2_bias,
        full_exp,
        full_bn3_gain,
        full_bn3_bias,
        full_patch,
        full_b_patch,
        full_ln1_gain,
        full_ln1_bias,
        full_qkv,
        full_b_qv,
        full_out,
        full_b_out,
        full_ln2_gain,
        full_ln2_bias,
        full_up,
        full_b_up,
        full_down,
        full_b_down,
    ) = weights
    examples, patches, channels = feats.shape
    bottleneck = w_red.shape[1]
    model_width = text.shape[2]
    head_count = model_width // HEAD_DIM
    seq_len = cotangent.shape[1]
    scale_factor = HEAD_DIM ** (-0.5)
    grad_rows = (cotangent.astype(jnp.float32) * saved["valid"][:, :, None]).reshape(
        -1, model_width
    )
    grad_low = grad_rows.astype(jnp.bfloat16)
    g_down = left_product(saved["hidden"], grad_low)
    g_b_down = jnp.sum(grad_rows, 0)
    g_hidden = right_product(grad_low, full_down)
    g_upper = smooth_grad(saved["upper"], g_hidden).astype(jnp.bfloat16)
    g_up = left_product(saved["second_norm"], g_upper)
    g_b_up = jnp.sum(g_upper.astype(jnp.float32), 0)
    g_second_norm = right_product(g_upper, full_up)
    _, norm_back = jax.vjp(
        normed,
        saved["second"],
        full_ln2_gain.astype(jnp.float32),
        full_ln2_bias.astype(jnp.float32),
    )
    g_second, g_ln2_gain, g_ln2_bias = norm_back(g_second_norm)
    g_second = g_second + grad_rows
    g_branch = g_second.astype(jnp.bfloat16)
    g_out = left_product(saved["mixed"], g_branch)
    g_b_out = jnp.sum(g_branch.astype(jnp.float32), 0)
    g_mixed = (
        right_product(g_branch, full_out)
        .astype(jnp.bfloat16)
        .reshape(examples, seq_len, head_count, HEAD_DIM)
    )
    g_value = jnp.einsum(
        "ehqk,eqhd->ekhd", saved["probs_low"], g_mixed, preferred_element_type=jnp.float32
    )
    g_probs = jnp.einsum(
        "eqhd,ekhd->ehqk", g_mixed, saved["value_part"], preferred_element_type=jnp.float32
    )
    probs = saved["probs"]
    g_scores = (probs * (g_probs - jnp.sum(probs * g_probs, -1, keepdims=True))).astype(
        jnp.bfloat16
    )
    g_query = (
        jnp.einsum(
            "ehqk,ekhd->eqhd", g_scores, saved["key_part"], preferred_element_type=jnp.float32
        )
        * scale_factor
    )
    g_key = (
        jnp.einsum("ehqk,eqhd->ekhd", g_scores, saved["query"], preferred_element_type=jnp.float32)
        * scale_factor
    )
    g_qkv_rows = (
        jnp.stack([g_query, g_key, g_value], 2).astype(jnp.bfloat16).reshape(-1, 3 * model_width)
    )
    g_qkv = left_product(saved["first_norm"], g_qkv_rows)
    qkv_sums = jnp.sum(g_qkv_rows.astype(jnp.float32), 0)
    g_b_qv = jnp.concatenate([qkv_sums[:model_width], qkv_sums[2 * model_width :]])
    g_first_norm = right_product(g_qkv_rows, full_qkv)
    _, first_back = jax.vjp(
        normed,
        saved["stream"],
        full_ln1_gain.astype(jnp.float32),
        full_ln1_bias.astype(jnp.float32),
    )
    g_stream, g_ln1_gain, g_ln1_bias = first_back(g_first_norm)
    g_stream = (g_stream + g_second).reshape(examples, seq_len, model_width)
    grad_text = (g_stream[:, patches:] * saved["keep"][:, :, None]).astype(jnp.bfloat16)
    g_patch_rows = g_stream[:, :patches].reshape(-1, model_width).astype(jnp.bfloat16)
    g_patch = left_product(saved["stem_act"], g_patch_rows)
    g_b_patch = jnp.sum(g_patch_rows.astype(jnp.float32), 0)
    g_act = right_product(g_patch_rows, full_patch)
    g_joined = smooth_grad(saved["joined"], g_act)
    g_expand_low, t_bn3_gain, t_bn3_bias = batch_backward(
        g_joined, saved["expand_norm"], saved["expand_inv"], full_bn3_gain
    )
    g_exp = left_product(saved["conv_act"], g_expand_low)
    g_conv_act = right_product(g_expand_low, full_exp)
    g_conv_shift = smooth_grad(saved["conv_shift"], g_conv_act)
    g_conv_low, t_bn2_gain, t_bn2_bias = batch_backward(
        g_conv_shift, saved["conv_norm"], saved["conv_inv"], full_bn2_gain
    )
    g_conv = left_product(saved["columns"], g_conv_low)
    g_columns = right_product(g_conv_low, full_conv)
    _, fold_back = jax.vjp(unfold, jnp.zeros((examples, GRID, GRID, bottleneck), jnp.float32))
    g_red_act = fold_back(g_columns)[0].reshape(-1, bottleneck)
    g_red_shift = smooth_grad(saved["red_shift"], g_red_act)
    g_red_low, t_bn1_gain, t_bn1_bias = batch_backward(
        g_red_shift, saved["red_norm"], saved["red_inv"], full_bn1_gain
    )
    g_red = left_product(saved["feat_rows"], g_red_low)
    grad_feats = (
        (g_joined + right_product(g_red_low, full_red))
        .astype(jnp.bfloat16)
        .reshape(examples, patches, channels)
    )
    A, B = lax.axis_size("dp"), lax.axis_size("fsdp")
    (s_red, s_conv, s_exp, s_patch, s_qkv, s_out, s_up, s_down) = scatter(A, B, [w.astype(jnp.bfloat16) for w in (g_red, g_conv, g_exp, g_patch, g_qkv, g_out, g_up, g_down)], 1)
    small = (g_b_patch, g_ln1_gain, g_ln1_bias, g_b_qv, g_b_out, g_ln2_gain, g_ln2_bias, g_b_up, g_b_down)
    sizes = (b_patch.shape[0], ln1_gain.shape[0], ln1_bias.shape[0], b_qv.shape[0], b_out.shape[0], ln2_gain.shape[0], ln2_bias.shape[0], b_up.shape[0], b_down.shape[0])
    (s_b_patch, s_ln1_gain, s_ln1_bias, s_b_qv, s_b_out, s_ln2_gain, s_ln2_bias, s_b_up, s_b_down) = [own_share(w, n) for w, n in zip(vectors_summed(small), sizes)]
    narrow = bn1_gain.shape[0]
    broad = bn3_gain.shape[0]
    return (
        output,
        grad_feats,
        grad_text,
        s_red,
        own_share(t_bn1_gain, narrow),
        own_share(t_bn1_bias, narrow),
        s_conv,
        own_share(t_bn2_gain, narrow),
        own_share(t_bn2_bias, narrow),
        s_exp,
        own_share(t_bn3_gain, broad),
        own_share(t_bn3_bias, broad),
        s_patch,
        s_b_patch,
        s_ln1_gain,
        s_ln1_bias,
        s_qkv,
        s_b_qv,
        s_out,
        s_b_out,
        s_ln2_gain,
        s_ln2_bias,
        s_up,
        s_b_up,
        s_down,
        s_b_down,
    )


def solution(mesh):
    return jax.shard_map(
        local,
        mesh=mesh,
        in_specs=(
            P(("dp", "fsdp"), None, None),
            P(("dp", "fsdp"), None, None),
            P(("dp", "fsdp")),
            P(("dp", "fsdp"), None, None),
            P(("dp", "fsdp"), None),
            P(("dp", "fsdp")),
            P(("dp", "fsdp")),
            P(("dp", "fsdp"), None),
            P(("dp", "fsdp")),
            P(("dp", "fsdp")),
            P(("dp", "fsdp"), None),
            P(("dp", "fsdp")),
            P(("dp", "fsdp")),
            P(("dp", "fsdp"), None),
            P(("dp", "fsdp")),
            P(("dp", "fsdp")),
            P(("dp", "fsdp")),
            P(("dp", "fsdp"), None),
            P(("dp", "fsdp")),
            P(("dp", "fsdp"), None),
            P(("dp", "fsdp")),
            P(("dp", "fsdp")),
            P(("dp", "fsdp")),
            P(("dp", "fsdp"), None),
            P(("dp", "fsdp")),
            P(("dp", "fsdp"), None),
            P(("dp", "fsdp")),
        ),
        out_specs=(
            P(("dp", "fsdp"), None, None),
            P(("dp", "fsdp"), None, None),
            P(("dp", "fsdp"), None, None),
            P(("dp", "fsdp"), None),
            P(("dp", "fsdp")),
            P(("dp", "fsdp")),
            P(("dp", "fsdp"), None),
            P(("dp", "fsdp")),
            P(("dp", "fsdp")),
            P(("dp", "fsdp"), None),
            P(("dp", "fsdp")),
            P(("dp", "fsdp")),
            P(("dp", "fsdp"), None),
            P(("dp", "fsdp")),
            P(("dp", "fsdp")),
            P(("dp", "fsdp")),
            P(("dp", "fsdp"), None),
            P(("dp", "fsdp")),
            P(("dp", "fsdp"), None),
            P(("dp", "fsdp")),
            P(("dp", "fsdp")),
            P(("dp", "fsdp")),
            P(("dp", "fsdp"), None),
            P(("dp", "fsdp")),
            P(("dp", "fsdp"), None),
            P(("dp", "fsdp")),
        ),
        check_vma=False,
    )
```

```python
import functools

import jax
import jax.numpy as jnp
from jax import lax
from jax.experimental import pallas as pl
from jax.experimental.pallas import tpu as pltpu
from jax.sharding import PartitionSpec as P
MESH = pl.DeviceIdType.MESH
DMA = pltpu.SemaphoreType.DMA


def rcopy(src, dst, send, recv, dev):
    return pltpu.make_async_remote_copy(
        src_ref=src, dst_ref=dst, send_sem=send, recv_sem=recv, device_id=dev, device_id_type=MESH
    )


class Place:
    def __init__(self, A, B):
        self.A, self.B, self.A2, self.Z = A, B, A // 2, B // 2
        a, b = lax.axis_index("dp"), lax.axis_index("fsdp")
        self.a, self.b = a, b
        self.y, self.x = a // 2, lax.rem(a, 2)
        self.z, self.c = b // 2, lax.rem(b, 2)
        self.zs = [lax.rem(self.z + k, self.Z) for k in range(1, self.Z)]
        self.ys = [lax.rem(self.y + k, self.A2) for k in range(1, self.A2)]
        self.zfrom = [lax.rem(self.z + self.Z - k, self.Z) for k in range(1, self.Z)]
        self.yfrom = [lax.rem(self.y + self.A2 - k, self.A2) for k in range(1, self.A2)]
        self.me = (a, b)
        self.core = (a, self.z * 2 + 1 - self.c)
        self.xpeer = (self.y * 2 + 1 - self.x, b)
        self.c1, self.x1 = 1 - self.c, 1 - self.x
        self.dpeers = [(lax.rem(a + k, A), b) for k in range(1, A)]
        self.zpeers = [(a, zz * 2 + self.c) for zz in self.zs]
        self.ypeers = [(yy * 2 + self.x, b) for yy in self.ys]

        self.bpeers = [(a, lax.rem(b + k, B)) for k in range(1, B)]

    def greet(self, totals=True):
        peers = self.dpeers + self.bpeers if totals else self.zpeers + self.ypeers + [self.xpeer, self.core]
        bar = pltpu.get_barrier_semaphore()
        for p in peers:
            pl.semaphore_signal(bar, inc=1, device_id=p, device_id_type=MESH)
        pl.semaphore_wait(bar, len(peers))


class GatherItem:
    def __init__(self, pc, i, cols, order, src, out, sems):
        self.pc, self.order, self.src_ref, self.out = pc, order, src, out
        self.cols = slice(None) if cols is None else pl.ds(*cols)
        self.loc, self.s1, self.r1, self.s2, self.r2, self.s3, self.r3, self.sc, self.rc = [s.at[i] for s in sems]
        self.here = False
        p = pc
        every = slice(None)
        self.got2 = [(p.y, p.x1)] if order == 0 else [(yy, p.x) for yy in p.yfrom]
        self.got3 = [(yy, every) for yy in p.yfrom] if order == 0 else [(every, p.x1)]
        self.to2 = [p.xpeer] if order == 0 else p.ypeers
        self.to3 = p.ypeers if order == 0 else [p.xpeer]
        self.crossed = [(p.y, p.x)] + self.got2 + self.got3

    def src(self):
        return self.src_ref.at[:, self.cols]

    def block(self, y, x, z, c):
        return self.out.at[y, x, z, c, :, self.cols]

    def local(self):
        p = self.pc
        return pltpu.make_async_copy(self.src(), self.block(p.y, p.x, p.z, p.c), self.loc)

    def send1(self, k):
        p = self.pc
        return rcopy(self.src(), self.block(p.y, p.x, p.z, p.c), self.s1.at[k], self.r1.at[k], p.zpeers[k])

    def send2(self, k):
        p = self.pc
        col = self.block(p.y, p.x, slice(None), p.c)
        return rcopy(col, col, self.s2.at[k], self.r2.at[k], self.to2[k])

    def send3(self, k):
        p, every = self.pc, slice(None)
        blk = self.block(p.y, every, every, p.c) if self.order == 0 else self.block(every, p.x, every, p.c)
        return rcopy(blk, blk, self.s3.at[k], self.r3.at[k], self.to3[k])

    def cross(self, j, c):
        blk = self.block(*self.crossed[j], slice(None), c)
        return rcopy(blk, blk, self.sc.at[j], self.rc.at[j], self.pc.core)

    def wait(self, got, send, recv):
        rcopy(got, got, send, recv, self.pc.me).wait_recv()

    def start(self):
        self.local().start()
        for k in range(len(self.pc.zpeers)):
            self.send1(k).start()

    def second(self):
        p = self.pc
        self.local().wait()
        for k, zz in enumerate(p.zfrom):
            self.wait(self.block(p.y, p.x, zz, p.c), self.s1.at[k], self.r1.at[k])
        for k in range(len(self.to2)):
            self.send2(k).start()
        self.cross(0, p.c).start()

    def third(self):
        p = self.pc
        for k, (yy, xx) in enumerate(self.got2):
            self.wait(self.block(yy, xx, slice(None), p.c), self.s2.at[k], self.r2.at[k])
        for k in range(len(self.to3)):
            self.send3(k).start()
        for k in range(len(self.got2)):
            self.cross(1 + k, p.c).start()

    def fourth(self):
        p = self.pc
        for k, (yy, xx) in enumerate(self.got3):
            self.wait(self.block(yy, xx, slice(None), p.c), self.s3.at[k], self.r3.at[k])
            self.cross(1 + len(self.got2) + k, p.c).start()

    def arrived(self):
        if self.here:
            return
        self.here = True
        for j in range(len(self.crossed)):
            self.cross(j, self.pc.c1).wait_recv()

    def drain(self):
        for k in range(len(self.pc.zpeers)):
            self.send1(k).wait_send()
        for k in range(len(self.to2)):
            self.send2(k).wait_send()
        for k in range(len(self.to3)):
            self.send3(k).wait_send()
        for j in range(len(self.crossed)):
            self.cross(j, self.pc.c).wait_send()


def gather_sems(A, B, n):
    A2, Z = A // 2, B // 2
    m = max(A2 - 1, 1)
    return [DMA((n,)), DMA((n, Z - 1)), DMA((n, Z - 1)), DMA((n, m)), DMA((n, m)), DMA((n, m)), DMA((n, m)), DMA((n, A2 + 1)), DMA((n, A2 + 1))]


def wave(items, lags, stages, hooks=None):
    hooks = hooks or {}
    last = max([len(items) + lags[-1]] + [t + 1 for t in hooks])
    for t in range(last):
        for lag, stage in zip(reversed(lags), reversed(stages)):
            if 0 <= t - lag < len(items):
                getattr(items[t - lag], stage)()
        for hook in hooks.get(t, ()):
            hook()


def wave_stages(items, lags, stages):
    out = []
    for t in range(len(items) + lags[-1]):
        for lag, stage in zip(reversed(lags), reversed(stages)):
            if 0 <= t - lag < len(items):
                out.append(getattr(items[t - lag], stage))
    return out


def cut(widths_parts):
    items, order = [], 0
    for i, (width, parts) in enumerate(widths_parts):
        for q in range(parts):
            items.append((i, None if parts == 1 else (q * (width // parts), width // parts), order))
            order = 1 - order
    return items


class ScatterItem:
    def __init__(self, pc, i, order, src, out, own, r0, r1, r2, r3, sems, cols=None):
        self.pc, self.order, self.src, self.out = pc, order, src, out
        self.cols = slice(None) if cols is None else pl.ds(*cols)
        self.own, self.r0, self.r1, self.r2, self.r3 = own, r0, r1, r2, r3
        self.loc, self.s0, self.q0, self.s1, self.q1, self.s2, self.q2, self.s3, self.q3 = [s.at[i] for s in sems]
        self.sends = []

    def go(self, copy):
        copy().start()
        self.sends.append(copy)

    def start(self):
        p = self.pc
        self.go(lambda: rcopy(self.src.at[:, :, :, p.c1, :, self.cols], self.r0, self.s0, self.q0, p.core))
        self.local().start()

    def local(self):
        return pltpu.make_async_copy(self.src.at[:, :, :, self.pc.c, :, self.cols], self.own, self.loc)

    def add(self, dst, others, lead):
        total = 1
        for d in lead:
            total *= d

        def body(t, _):
            idx, rest = [], t
            for d in reversed(lead):
                idx.append(lax.rem(rest, d))
                rest = rest // d
            idx = tuple(reversed(idx))
            v = dst[idx].astype(jnp.float32)
            for o in others:
                v = v + o[idx].astype(jnp.float32)
            dst[idx] = v.astype(jnp.bfloat16)
            return 0

        lax.fori_loop(0, total, body, 0)

    def second(self):
        p = self.pc
        self.local().wait()
        rcopy(self.r0, self.r0, self.s0, self.q0, p.me).wait_recv()
        self.add(self.own, [self.r0], (p.A2, 2, p.Z))
        if self.order == 0:
            self.go(lambda: rcopy(self.own.at[:, p.x1], self.r1.at[0], self.s1.at[0], self.q1.at[0], p.xpeer))
        else:
            for k, yy in enumerate(p.ys):
                self.go(lambda k=k, yy=yy: rcopy(self.own.at[yy], self.r1.at[k], self.s1.at[k], self.q1.at[k], p.ypeers[k]))

    def third(self):
        p = self.pc
        n1 = 1 if self.order == 0 else p.A2 - 1
        for k in range(n1):
            rcopy(self.r1.at[k], self.r1.at[k], self.s1.at[k], self.q1.at[k], p.me).wait_recv()
        mine = self.own.at[:, p.x] if self.order == 0 else self.own.at[p.y]
        self.add(mine, [self.r1.at[k] for k in range(n1)], (p.A2 if self.order == 0 else 2, p.Z))
        if self.order == 0:
            for k, yy in enumerate(p.ys):
                self.go(lambda k=k, yy=yy: rcopy(self.own.at[yy, p.x], self.r2.at[k], self.s2.at[k], self.q2.at[k], p.ypeers[k]))
        else:
            self.go(lambda: rcopy(self.own.at[p.y, p.x1], self.r2.at[0], self.s2.at[0], self.q2.at[0], p.xpeer))

    def fourth(self):
        p = self.pc
        n2 = p.A2 - 1 if self.order == 0 else 1
        for k in range(n2):
            rcopy(self.r2.at[k], self.r2.at[k], self.s2.at[k], self.q2.at[k], p.me).wait_recv()
        self.add(self.own.at[p.y, p.x], [self.r2.at[k] for k in range(n2)], (p.Z,))
        for k, zz in enumerate(p.zs):
            self.go(lambda k=k, zz=zz: rcopy(self.own.at[p.y, p.x, zz], self.r3.at[k], self.s3.at[k], self.q3.at[k], p.zpeers[k]))

    def arrived(self):
        p = self.pc
        for k in range(p.Z - 1):
            rcopy(self.r3.at[k], self.r3.at[k], self.s3.at[k], self.q3.at[k], p.me).wait_recv()
        v = self.own[p.y, p.x, p.z].astype(jnp.float32)
        for k in range(p.Z - 1):
            v = v + self.r3[k].astype(jnp.float32)
        self.out[:, self.cols] = v[: self.out.shape[0]]

    def drain(self):
        for copy in self.sends:
            copy().wait_send()


def scatter_sems(A, B, n):
    m, Z = max(A // 2 - 1, 1), B // 2
    return [DMA((n,)), DMA((n,)), DMA((n,)), DMA((n, m)), DMA((n, m)), DMA((n, m)), DMA((n, m)), DMA((n, Z - 1)), DMA((n, Z - 1))]


def scatter_scratch(A, B, shape, order):
    A2, Z = A // 2, B // 2
    n1 = (1, A2, Z) if order == 0 else (A2 - 1, 2, Z)
    n2 = (A2 - 1, Z) if order == 0 else (1, Z)
    return [pltpu.VMEM(s + shape, jnp.bfloat16) for s in ((A2, 2, Z), (A2, 2, Z), n1, n2, (Z - 1,))]


def scatter_items(pc, cuts, srcs, outs, bufs, sems, base=0):
    return [ScatterItem(pc, base + j, o, srcs[i], outs[i], *bufs[5 * j : 5 * j + 5], sems, cols) for j, (i, cols, o) in enumerate(cuts)]


def scatter_buffers(A, B, cuts, shapes):
    out = []
    for i, cols, order in cuts:
        out += scatter_scratch(A, B, (shapes[i][0], shapes[i][1] if cols is None else cols[1]), order)
    return out


def split_rows(A, B, g):
    return g.reshape((A // 2, 2, B // 2, 2, g.shape[0] // (A * B), g.shape[1]))


HEAD_DIM = 64
GRID = 14
ln_eps = 1e-06
bn_eps = 1e-05
gelu_coef = 0.7978845608028654
gelu_cube = gelu_coef * 0.044715
bf16, f32 = jnp.bfloat16, jnp.float32
PATCH_PAD = 208


def dot(left, right):
    return jnp.dot(left, right, preferred_element_type=f32)


def dot_nt(left, right):
    return lax.dot_general(left, right, (((1,), (1,)), ((), ())), preferred_element_type=f32)


def dot_tn(left, right):
    return lax.dot_general(left, right, (((0,), (0,)), ((), ())), preferred_element_type=f32)


def smooth(v):
    return (0.5 * v) * (1.0 + jnp.tanh(v * (gelu_coef + gelu_cube * (v * v))))


def smooth_both(v):
    sq = v * v
    t = jnp.tanh(v * (gelu_coef + gelu_cube * sq))
    half = 0.5 * v
    up = 1.0 + t
    return half * up, 0.5 * up + half * ((1.0 - t * t) * (gelu_coef + 3.0 * gelu_cube * sq))


def ln_parts(v):
    center = v - jnp.mean(v, -1, keepdims=True)
    inv = lax.rsqrt(jnp.mean(center * center, -1, keepdims=True) + ln_eps)
    return center * inv, inv


def ln_back(dy, hat, inv, gain):
    dh = dy * gain
    return inv * (dh - jnp.mean(dh, -1, keepdims=True) - hat * jnp.mean(dh * hat, -1, keepdims=True))


def colsum(v):
    return jnp.sum(v, 0, keepdims=True)


def iota(shape, dim):
    return lax.broadcasted_iota(jnp.int32, shape, dim)


def valid_of(position, length, patches):
    text = position - PATCH_PAD
    return jnp.where((position < patches) | ((text >= 0) & (text < length)), 1.0, 0.0).astype(f32)


def spread(rows, patches, seq):
    i, j = iota((rows, seq), 0), iota((rows, seq), 1)
    hit = ((i < patches) & (j == i)) | ((i >= PATCH_PAD) & (j == i - (PATCH_PAD - patches)))
    return jnp.where(hit, 1.0, 0.0).astype(bf16)


def gather_rows(seq, rows, patches):
    j, i = iota((seq, rows), 0), iota((seq, rows), 1)
    hit = ((i < patches) & (j == i)) | ((i >= PATCH_PAD) & (j == i - (PATCH_PAD - patches)))
    return jnp.where(hit, 1.0, 0.0).astype(bf16)


def lane_masks(width):
    lane = iota((1, 2 * width), 1)
    low = jnp.where(lane < width, 1.0, 0.0).astype(bf16)
    return low, (1.0 - low.astype(f32)).astype(bf16)


class Plan:
    def __init__(self, step, steps, points, stages):
        self.step, self.steps, self.points = step, steps, points
        total, n = steps * points, len(stages)
        self.due = [stages[n * q // total : n * (q + 1) // total] for q in range(total)]

    def __call__(self, point):
        for s in range(self.steps):
            stages = self.due[s * self.points + point]
            if stages:

                @pl.when(self.step == s)
                def _():
                    for stage in stages:
                        stage()


def attend_kernel(n, patches, len_ref, act, text, wp, wqkv, wout, params, x_o, h1_o, qkv_o, o_o, x2_o, h2_o):
    width = text.shape[2]
    slots = text.shape[1]
    rows = PATCH_PAD + slots
    step = pl.program_id(0)
    lows = lane_masks(HEAD_DIM)
    bp, g1, b1, bo, g2, b2 = (params[v : v + 1, :width] for v in (6, 7, 8, 10, 11, 12))
    bqkv = jnp.concatenate([params[9:10, :width], jnp.zeros((1, width), f32), params[9:10, width : 2 * width]], 1)
    patch = dot(act[...].reshape(n * PATCH_PAD, act.shape[2]), wp[...]) + bp
    for i in range(n):
        length = len_ref[step * n + i]
        keep = jnp.where(iota((slots, 1), 0) < length, 1.0, 0.0).astype(f32)
        x_o[i * rows : i * rows + PATCH_PAD] = patch[i * PATCH_PAD : (i + 1) * PATCH_PAD]
        x_o[i * rows + PATCH_PAD : (i + 1) * rows] = text[i].astype(f32) * keep
    hat, _ = ln_parts(x_o[...])
    h1 = (hat * g1 + b1).astype(bf16)
    h1_o[...] = h1
    qkv_o[...] = (dot(h1, wqkv[...]) + bqkv).astype(bf16)
    for i in range(n):
        at = slice(i * rows, (i + 1) * rows)
        bias = jnp.where(valid_of(iota((1, rows), 1), len_ref[step * n + i], patches) > 0.5, 0.0, -1e30)
        for j in range(width // (2 * HEAD_DIM)):
            cols = [slice(p * width + j * 128, p * width + (j + 1) * 128) for p in range(3)]
            q = qkv_o[at, cols[0]] * bf16(HEAD_DIM**-0.5)
            k, v = qkv_o[at, cols[1]], qkv_o[at, cols[2]]
            mixed = 0.0
            for low in lows:
                s = dot_nt(q * low, k) + bias
                e = jnp.exp(s - jnp.max(s, -1, keepdims=True))
                pr = (e * (1.0 / jnp.sum(e, -1, keepdims=True))).astype(bf16)
                mixed = mixed + dot(pr, v * low)
            o_o[at, cols[0]] = mixed.astype(bf16)
    x2 = x_o[...] + dot(o_o[...], wout[...]) + bo
    x2_o[...] = x2
    hat2, _ = ln_parts(x2)
    h2_o[...] = (hat2 * g2 + b2).astype(bf16)


def whole(shape):
    return pl.BlockSpec(shape, lambda *_: (0,) * len(shape), pipeline_mode=pl.Buffered(1))


def attend(lengths, act, text, wp, wqkv, wout, params, patches, n):
    examples, slots, width = text.shape
    rows = PATCH_PAD + slots
    steps = examples // n
    blk = lambda w: pl.BlockSpec((n * rows, w), lambda s: (s, 0))
    out = lambda w, t: jax.ShapeDtypeStruct((examples * rows, w), t)
    return pl.pallas_call(
        functools.partial(attend_kernel, n, patches),
        grid=(steps,),
        out_shape=[out(width, f32), out(width, bf16), out(3 * width, bf16), out(width, bf16), out(width, f32), out(width, bf16)],
        in_specs=[
            pl.BlockSpec(memory_space=pltpu.SMEM),
            pl.BlockSpec((n,) + act.shape[1:], lambda s: (s, 0, 0)),
            pl.BlockSpec((n,) + text.shape[1:], lambda s: (s, 0, 0)),
        ]
        + [whole(w.shape) for w in (wp, wqkv, wout, params)],
        out_specs=[blk(width), blk(width), blk(3 * width), blk(width), blk(width), blk(width)],
        compiler_params=pltpu.CompilerParams(vmem_limit_bytes=56 << 20),
        name="attend",
    )(lengths, act, text, wp, wqkv, wout, params)


def ffn_kernel(n, patches, len_ref, h2, x2_h, cot, wu, bu, wd, params, out_h, dx2_h, gup, gdown, gbu, small, g_s, h2t, acc, dh, m_s, du_s, x2, out, sems):
    c, last = pl.program_id(0), pl.num_programs(0) - 1
    examples, seq, width = cot.shape
    rows = PATCH_PAD + seq - patches
    blocks = examples // n
    load = pltpu.make_async_copy(x2_h, x2, sems.at[0, 0])

    def leave(i, at):
        return pltpu.make_async_copy(out.at[i], out_h.at[i], sems.at[1, i]), pltpu.make_async_copy(dh.at[at], dx2_h.at[at], sems.at[2, i])

    @pl.when(c == 0)
    def _():
        load.start()

        def body(i, _):
            at = pl.ds(pl.multiple_of(i * rows, 16), rows)
            valid = valid_of(iota((rows, 1), 0), len_ref[i], patches)
            g_s[at] = (dot(spread(rows, patches, seq), cot[i]) * valid).astype(bf16)
            acc[at] = jnp.zeros((rows, width), f32)
            dh[at] = jnp.zeros((rows, width), f32)
            return 0

        lax.fori_loop(0, examples, body, 0)
        h2t[...] = h2[...].T

    def block(r, sums):
        at = pl.ds(pl.multiple_of(r * (n * rows), 16), n * rows)
        m, slope = smooth_both(dot(h2[at], wu[...]) + bu[13:14])
        m = m.astype(bf16)
        m_s[at] = m
        acc[at] += dot(m, wd[...])
        du = dot_nt(g_s[at], wd[...]) * slope
        sums = sums + colsum(du)
        du = du.astype(bf16)
        du_s[at] = du
        dh[at] += dot_nt(du, wu[...])
        return sums

    gbu[...] = lax.fori_loop(0, blocks, block, jnp.zeros(gbu.shape, f32), unroll=True)
    gup[...] = dot(h2t[...], du_s[...]).astype(bf16)
    gdown[...] = dot_tn(m_s[...], g_s[...]).astype(bf16)

    @pl.when(c == last)
    def _():
        load.wait()

        def body(i, sums):
            at = pl.ds(pl.multiple_of(i * rows, 16), rows)
            valid = valid_of(iota((rows, 1), 0), len_ref[i], patches)
            result = (acc[at] + x2[at] + params[14:15, :width]) * valid
            out[i] = dot(gather_rows(seq, rows, patches), result.astype(bf16)).astype(bf16)
            hat, inv = ln_parts(x2[at])
            g = g_s[at].astype(f32)
            dy = dh[at]
            dh[at] = g + ln_back(dy, hat, inv, params[11:12, :width])
            for copy in leave(i, at):
                copy.start()
            return sums[0] + colsum(g), sums[1] + colsum(dy * hat), sums[2] + colsum(dy)

        zero = jnp.zeros((1, width), f32)
        a, b, d = lax.fori_loop(0, examples, body, (zero, zero, zero))
        small[0:1], small[1:2], small[2:3] = a, b, d
        small[3:8] = jnp.zeros((5, width), f32)

        def wait(i, _):
            for copy in leave(i, pl.ds(pl.multiple_of(i * rows, 16), rows)):
                copy.wait()
            return 0

        lax.fori_loop(0, examples, wait, 0)


def ffn(lengths, h2, x2, cot, wu, wd, params, patches, n, chunk):
    examples, seq, width = cot.shape
    total, hidden = h2.shape[0], wu.shape[1]
    col = lambda rows: pl.BlockSpec((rows, chunk), lambda c: (0, c))
    row = pl.BlockSpec((chunk, width), lambda c: (c, 0))
    return pl.pallas_call(
        functools.partial(ffn_kernel, n, patches),
        grid=(hidden // chunk,),
        out_shape=[
            jax.ShapeDtypeStruct(cot.shape, bf16),
            jax.ShapeDtypeStruct((total, width), f32),
            jax.ShapeDtypeStruct((width, hidden), bf16),
            jax.ShapeDtypeStruct((hidden, width), bf16),
            jax.ShapeDtypeStruct((1, hidden), f32),
            jax.ShapeDtypeStruct((8, width), f32),
        ],
        in_specs=[pl.BlockSpec(memory_space=pltpu.SMEM), whole(h2.shape), pl.BlockSpec(memory_space=pl.ANY), whole(cot.shape), col(width), col(params.shape[0]), row, whole(params.shape)],
        out_specs=[pl.BlockSpec(memory_space=pl.ANY), pl.BlockSpec(memory_space=pl.ANY), col(width), row, col(1), whole((8, width))],
        scratch_shapes=[
            pltpu.VMEM((total, width), bf16),
            pltpu.VMEM((width, total), bf16),
            pltpu.VMEM((total, width), f32),
            pltpu.VMEM((total, width), f32),
            pltpu.VMEM((total, chunk), bf16),
            pltpu.VMEM((total, chunk), bf16),
            pltpu.VMEM((total, width), f32),
            pltpu.VMEM(cot.shape, bf16),
            DMA((3, examples)),
        ],
        compiler_params=pltpu.CompilerParams(vmem_limit_bytes=60 << 20),
        name="ffn",
    )(lengths, h2, x2, cot, wu, params, wd, params)


def attend_back_kernel(A, B, n, patches, slots, cuts, n_sc, *refs):
    (len_ref, dx2, x, h1, qkv, o, act, wp, wqkv, wout, params), refs = refs[:11], refs[11:]
    srcs, refs = refs[:n_sc], refs[n_sc:]
    (dact, gtext, gqkv, gout, gpatch, small, small3), refs = refs[:7], refs[7:]
    sums, refs = refs[:n_sc], refs[n_sc:]
    (aqkv, aout, apatch, do_s, dq_s), refs = refs[:5], refs[5:]
    step, last = pl.program_id(0), pl.num_programs(0) - 1
    width = x.shape[1]
    g1 = params[7:8, :width]
    rows = PATCH_PAD + slots
    lows = lane_masks(HEAD_DIM)
    scale = bf16(HEAD_DIM**-0.5)

    @pl.when(step == 0)
    def _():
        for ref in (aqkv, aout, apatch, small, small3):
            ref[...] = jnp.zeros(ref.shape, f32)

    moves, stages = [], []
    if n_sc:
        pc = Place(A, B)
        pl.when(step == 0)(lambda: pc.greet(False))
        moves = scatter_items(pc, cuts, srcs, sums, refs[: 5 * len(cuts)], refs[5 * len(cuts) :])
        stages = wave_stages(moves, (0, 2, 5, 8, 11), ["start", "second", "third", "fourth", "arrived"])
    progress = Plan(step, 6, 3, stages)
    progress(0)
    db = dx2[...].astype(bf16)
    do_s[...] = dot_nt(db, wout[...]).astype(bf16)
    aout[...] += dot_tn(o[...], db)
    for i in range(n):
        at = slice(i * rows, (i + 1) * rows)
        bias = jnp.where(valid_of(iota((rows, 1), 0), len_ref[step * n + i], patches) > 0.5, 0.0, -1e30)
        for j in range(width // (2 * HEAD_DIM)):
            cols = [slice(p * width + j * 128, p * width + (j + 1) * 128) for p in range(3)]
            q, k, v = qkv[at, cols[0]] * scale, qkv[at, cols[1]], qkv[at, cols[2]]
            ks = k * scale
            do = do_s[at, cols[0]]
            dq = dk = dv = 0.0
            for low in lows:
                s = dot_nt(k * low, q) + bias
                e = jnp.exp(s - jnp.max(s, 0, keepdims=True))
                p = e * (1.0 / jnp.sum(e, 0, keepdims=True))
                dv = dv + dot(p.astype(bf16), do * low)
                dp = dot_nt(v * low, do)
                ds = (p * (dp - jnp.sum(p * dp, 0, keepdims=True))).astype(bf16)
                dk = dk + dot(ds, q * low)
                dq = dq + dot_tn(ds, ks * low)
            dq_s[at, cols[0]], dq_s[at, cols[1]], dq_s[at, cols[2]] = dq.astype(bf16), dk.astype(bf16), dv.astype(bf16)
    progress(1)
    aqkv[...] += dot_tn(h1[...], dq_s[...])
    dh1 = dot_nt(dq_s[...], wqkv[...])
    hat, inv = ln_parts(x[...])
    dx = dx2[...] + ln_back(dh1, hat, inv, g1)
    progress(2)
    dps = []
    for i in range(n):
        keep = jnp.where(iota((slots, 1), 0) < len_ref[step * n + i], 1.0, 0.0).astype(f32)
        gtext[i] = (dx[i * rows + PATCH_PAD : (i + 1) * rows] * keep).astype(bf16)
        inside = iota((PATCH_PAD, 1), 0) < patches
        dps.append(jnp.where(inside, dx[i * rows : i * rows + PATCH_PAD], 0.0).astype(bf16))
    dp = jnp.concatenate(dps, 0)
    dact[...] = dot_nt(dp, wp[...]).reshape(dact.shape)
    apatch[...] += dot_tn(act[...].reshape(n * PATCH_PAD, act.shape[2]), dp)
    small[0:1] += colsum(dh1 * hat)
    small[1:2] += colsum(dh1)
    small[2:3] += colsum(db.astype(f32))
    small[3:4] += colsum(dp.astype(f32))
    small3[0:1] += colsum(dq_s[...].astype(f32))

    @pl.when(step == last)
    def _():
        for m in moves:
            m.drain()
        gqkv[...], gout[...], gpatch[...] = aqkv[...].astype(bf16), aout[...].astype(bf16), apatch[...].astype(bf16)


def attend_back(A, B, lengths, dx2, x, h1, qkv, o, act, wp, wqkv, wout, params, grads, parts, slots, patches, n, cid):
    examples, _, channels = act.shape
    width = x.shape[1]
    rows = PATCH_PAD + slots
    blk = lambda w: pl.BlockSpec((n * rows, w), lambda s: (s, 0))
    assert examples == 6 * n
    cuts = cut([(g.shape[1], q) for g, q in zip(grads, parts)])
    shapes = [(g.shape[0] // (A * B), g.shape[1]) for g in grads]
    hbm = pl.BlockSpec(memory_space=pl.ANY)
    remote = dict(collective_id=cid, has_side_effects=True) if grads else {}
    cube = lambda a, b: pl.BlockSpec((n, a, b), lambda s: (s, 0, 0))
    return pl.pallas_call(
        functools.partial(attend_back_kernel, A, B, n, patches, slots, cuts, len(grads)),
        grid=(examples // n,),
        out_shape=[
            jax.ShapeDtypeStruct(act.shape, f32),
            jax.ShapeDtypeStruct((examples, slots, width), bf16),
            jax.ShapeDtypeStruct(wqkv.shape, bf16),
            jax.ShapeDtypeStruct(wout.shape, bf16),
            jax.ShapeDtypeStruct(wp.shape, bf16),
            jax.ShapeDtypeStruct((8, width), f32),
            jax.ShapeDtypeStruct((8, 3 * width), f32),
        ]
        + [jax.ShapeDtypeStruct(s, f32) for s in shapes],
        in_specs=[pl.BlockSpec(memory_space=pltpu.SMEM), blk(width), blk(width), blk(width), blk(3 * width), blk(width), cube(PATCH_PAD, channels)]
        + [whole(w.shape) for w in (wp, wqkv, wout, params)]
        + [hbm] * len(grads),
        out_specs=[cube(PATCH_PAD, channels), cube(slots, width)] + [whole(s) for s in (wqkv.shape, wout.shape, wp.shape, (8, width), (8, 3 * width), *shapes)],
        scratch_shapes=[pltpu.VMEM(wqkv.shape, f32), pltpu.VMEM(wout.shape, f32), pltpu.VMEM(wp.shape, f32), pltpu.VMEM((n * rows, width), bf16), pltpu.VMEM((n * rows, 3 * width), bf16)]
        + (scatter_buffers(A, B, cuts, shapes) + scatter_sems(A, B, len(cuts)) if grads else []),
        compiler_params=pltpu.CompilerParams(vmem_limit_bytes=62 << 20, **remote),
        name="attend_back",
    )(lengths, dx2, x, h1, qkv, o, act, wp, wqkv, wout, params, *[split_rows(A, B, g) for g in grads])


class Total:
    def __init__(self, pc, j, send, recv, ssem, rsem):
        self.pc, self.send, self.recv = pc, send.at[j], recv.at[j]
        self.ssem, self.rsem = ssem.at[j], rsem.at[j]
        groups = [pc.bpeers, pc.dpeers]
        self.groups, at = [], 0
        for g in groups:
            self.groups.append([(at + k, dev) for k, dev in enumerate(g)])
            at += len(g)

    def copy(self, step, k, dev):
        return rcopy(self.send.at[step], self.recv.at[k], self.ssem.at[k], self.rsem.at[k], dev)

    def put(self, step, v):
        self.send[step] = v
        for k, dev in self.groups[step]:
            self.copy(step, k, dev).start()

    def take(self, step):
        v = self.send[step]
        for k, dev in self.groups[step]:
            self.copy(step, k, dev).wait_recv()
            v = v + self.recv[k]
        return v

    def begin(self, v):
        self.put(0, v)

    def middle(self):
        self.put(1, self.take(0))

    def end(self):
        return self.take(1)

    def drain(self):
        for step in range(2):
            for k, dev in self.groups[step]:
                self.copy(step, k, dev).wait_send()


def total_scratch(A, B, count, shape):
    peers = (B - 1) + (A - 1)
    return [pltpu.VMEM((count, 2) + shape, f32), pltpu.VMEM((count, peers) + shape, f32), DMA((count, peers)), DMA((count, peers))]


def tile_rows(rows):
    return -(-rows // 16) * 16


def together(rows):
    n = 1
    while n * rows % 16:
        n += 1
    return n


def unpack(src, dst, rows):
    padded, cols = src.shape[-2:]
    shards = dst.shape[0] // rows
    flat = src[...].reshape(shards * padded, cols)
    if padded == rows:
        dst[...] = flat
        return
    n = together(rows)
    pick = turn_rows((n * rows, n * padded), rows, padded)
    for t in range(shards // n):
        dst[t * n * rows : (t + 1) * n * rows] = dot(pick, flat[t * n * padded : (t + 1) * n * padded]).astype(bf16)


def turn_rows(shape, rows, padded):
    out, pos = iota(shape, 0), iota(shape, 1)
    shard = jnp.floor((out.astype(f32) + 0.5) * (1.0 / rows)).astype(jnp.int32)
    return jnp.where(pos == out + shard * (padded - rows), 1.0, 0.0).astype(bf16)


def pack(src, dst, rows):
    padded, cols = dst.shape[-2:]
    shards = src.shape[0] // rows
    if padded == rows:
        dst[...] = src.reshape(dst.shape)
        return
    n = together(rows)
    shape = (n * padded, n * rows)
    out, pos = iota(shape, 0), iota(shape, 1)
    shard = jnp.floor((out.astype(f32) + 0.5) * (1.0 / padded)).astype(jnp.int32)
    pick = jnp.where((pos == out - shard * (padded - rows)) & (out - shard * padded < rows), 1.0, 0.0).astype(bf16)
    parts = [dot(pick, src[t * n * rows : (t + 1) * n * rows]).astype(bf16) for t in range(shards // n)]
    dst[...] = jnp.concatenate(parts, 0).reshape(dst.shape)


def unpack_vectors(tab, out, sizes):
    shards = tab.shape[0] * tab.shape[1] * tab.shape[2] * tab.shape[3]
    flat = tab[...].reshape(shards, tab.shape[-2], tab.shape[-1])[:, 0, :]
    out[...] = jnp.zeros(out.shape, f32)
    for v, n in enumerate(sizes):
        wide = n * shards
        lane = iota((128, wide), 1)
        block = jnp.floor((lane.astype(f32) + 0.5) * (1.0 / n)).astype(jnp.int32)
        spot = jnp.where(iota((128, wide), 0) == lane - block * n, 1.0, 0.0).astype(bf16)
        rows = dot(flat[:, 128 * v : 128 * (v + 1)].astype(bf16), spot)
        owner = jnp.where(iota((shards, wide), 0) == block[:shards] if shards <= 128 else block, rows, 0.0)
        out[v : v + 1, :wide] = colsum(owner)


def make_taps(taps, grid):
    places = grid * grid
    i, j = iota((places, places), 0), iota((places, places), 1)
    col = i - grid * jnp.floor((i.astype(f32) + 0.5) * (1.0 / grid)).astype(jnp.int32)
    for t in range(9):
        dr, dc = t // 3 - 1, t % 3 - 1
        hit = (j == i + grid * dr + dc) & (col + dc >= 0) & (col + dc < grid)
        taps[t] = jnp.where(hit, 1.0, 0.0).astype(bf16)


def rows_of(vectors):
    rows = []
    for v in vectors:
        rows += [v[:, q : q + 256] for q in range(0, v.shape[1], 256)]
    if len(rows) < 8:
        rows.append(jnp.zeros((8 - len(rows), 256), f32))
    return jnp.concatenate(rows, 0)


def vectors_of(block, width):
    per = width // 256
    take = lambda k: jnp.concatenate([block[k * per + q : k * per + q + 1] for q in range(per)], 1)
    return take(0), take(1)


VECTORS = ("bn1_gain", "bn1_bias", "bn2_gain", "bn2_bias", "bn3_gain", "bn3_bias", "b_patch", "ln1_gain", "ln1_bias", "b_q", "b_v", "b_out", "ln2_gain", "ln2_bias", "b_up", "b_down")


def moments(s1, s2, total_rows, gain, bias):
    mean = s1 / total_rows
    inv = lax.rsqrt(s2 / total_rows - mean * mean + bn_eps)
    return mean, inv


def stem_kernel(A, B, items, n_mats, sizes, shard_rows, total_rows, *refs):
    n_vec = len(sizes)
    feats, vecs, refs = refs[0], refs[1 : 1 + n_vec], refs[1 + n_vec :]
    near, far_in, refs = refs[:3], refs[3 : n_mats - 1], refs[n_mats - 1 :]
    n_far = n_mats - 4
    far, refs = refs[:n_far], refs[n_far:]
    (act_h, r_h, c_h, e_h, params, stats, w_red, w_conv, w_exp), refs = refs[:9], refs[9:]
    (act, r_o, c_o, e_o, out_sems), refs = refs[:5], refs[5:]
    (p_red, tab, p_conv, p_exp, taps, cols), refs = refs[:6], refs[6:]
    mine, refs = refs[:4], refs[4:]
    sums, sems = refs[:4], refs[4:]
    pc = Place(A, B)
    for src, dst in zip(near, (mine[0], mine[2], mine[3])):
        dst[...] = dot(jnp.where(iota((dst.shape[0], src.shape[0]), 0) == iota((dst.shape[0], src.shape[0]), 1), 1.0, 0.0).astype(bf16), src[...]).astype(bf16)
    mine[1][...] = jnp.zeros(mine[1].shape, f32)
    for v, ref in enumerate(vecs):
        mine[1][:, 128 * v : 128 * v + sizes[v]] = ref[...].astype(f32)
    shards = [*mine, *far_in]
    pc.greet()
    dsts = [p_red, tab, p_conv, p_exp, *far]
    moves = [GatherItem(pc, j, c, order, shards[i], dsts[i], sems) for j, (i, c, order) in enumerate(items)]
    adds = [Total(pc, j, *sums) for j in range(3)]
    examples, patches, channels = feats.shape
    grid = GRID
    vec = lambda v, width: params[v : v + 1, :width]

    def each(fn, width):
        zero = jnp.zeros((1, width), f32)

        def body(i, s):
            v = fn(i)
            return s[0] + colsum(v), s[1] + colsum(v * v)

        return lax.fori_loop(0, examples, body, (zero, zero))

    def norm(v, j, width):
        return (v - stats[2 * j : 2 * j + 1, :width]) * stats[2 * j + 1 : 2 * j + 2, :width] * vec(2 * j, width) + vec(2 * j + 1, width)

    def keep(j, width):
        s1, s2 = vectors_of(adds[j].end(), width)
        mean, inv = moments(s1, s2, total_rows, None, None)
        stats[2 * j : 2 * j + 1, :width] = mean
        stats[2 * j + 1 : 2 * j + 2, :width] = inv

    narrow = r_o.shape[2]

    def first():
        moves[0].arrived()
        unpack(p_red, w_red, shard_rows[0])

        def one(i):
            v = dot(feats[i], w_red[...])
            r_o[i] = v
            return v

        adds[0].begin(rows_of(each(one, narrow)))

    def vectors():
        moves[1].arrived()
        unpack_vectors(tab, params, sizes)

    def second():
        keep(0, narrow)

        def one(i):
            ra = smooth(norm(r_o[i], 0, narrow)).astype(bf16)
            for t in range(9):
                cols[:, t * narrow : (t + 1) * narrow] = dot(taps[t], ra).astype(bf16)
            v = dot(cols[...], w_conv[...])
            c_o[i] = v
            return v

        adds[1].begin(rows_of(each(one, narrow)))

    def third():
        keep(1, narrow)

        def one(i):
            ca = smooth(norm(c_o[i], 1, narrow)).astype(bf16)
            v = dot(ca, w_exp[...])
            e_o[i] = v
            return v

        adds[2].begin(rows_of(each(one, channels)))

    def act_copy(i):
        return pltpu.make_async_copy(act.at[i], act_h.at[i], out_sems.at[3 + i])

    def fourth():
        keep(2, channels)
        wide = spread(act.shape[1], patches, patches)

        def body(i, _):
            v = norm(e_o[i], 2, channels) + feats[i].astype(f32)
            act[i] = dot(wide, smooth(v).astype(bf16)).astype(bf16)
            act_copy(i).start()
            return 0

        lax.fori_loop(0, examples, body, 0)

    saved = [pltpu.make_async_copy(v, h, out_sems.at[k]) for k, (v, h) in enumerate(((r_o, r_h), (c_o, c_h), (e_o, e_h)))]
    make_taps(taps, grid)
    stats[...] = jnp.zeros(stats.shape, f32)

    def ready_conv():
        moves[2].arrived()
        unpack(p_conv, w_conv, shard_rows[1])
        vectors()

    def ready_exp():
        moves[3].arrived()
        unpack(p_exp, w_exp, shard_rows[2])

    hooks = {8: [first], 10: [adds[0].middle, saved[0].start, ready_conv], 12: [second], 14: [adds[1].middle, saved[1].start, ready_exp], 16: [third], 18: [adds[2].middle, saved[2].start], 20: [fourth]}
    wave(moves, (0, 2, 4, 6), ["start", "second", "third", "fourth"], hooks)
    for m in moves:
        m.arrived()
    for m in moves:
        m.drain()
    for t in adds:
        t.drain()
    for t in saved:
        t.wait()
    lax.fori_loop(0, examples, lambda i, _: (act_copy(i).wait(), 0)[1], 0)


def stem_forward(A, B, feats, vecs, mats, pad_rows, parts, cid):
    A2, Z, count = A // 2, B // 2, A * B
    examples, patches, channels = feats.shape
    near, far = mats[:3], mats[3:]
    sizes = [v.shape[0] for v in vecs]
    shard_rows = [m.shape[0] for m in near]
    pads = [jax.ShapeDtypeStruct((tile_rows(m.shape[0]), m.shape[1]), bf16) for m in near]
    shards = [pads[0], jax.ShapeDtypeStruct((1, 128 * len(vecs)), f32), pads[1], pads[2], *far]
    items = cut([(s.shape[1], q) for s, q in zip(shards, (1, 1, 1, 1) + parts)])
    shape = lambda s: (A2, 2, Z, 2) + s.shape
    narrow = near[0].shape[1]
    hbm, vm = pl.BlockSpec(memory_space=pl.ANY), pl.BlockSpec(memory_space=pltpu.VMEM)
    full = [(m.shape[0] * count, m.shape[1]) for m in near]
    outs = pl.pallas_call(
        functools.partial(stem_kernel, A, B, items, len(shards), sizes, shard_rows, float(examples * count * patches)),
        out_shape=[jax.ShapeDtypeStruct(shape(s), s.dtype) for s in far]
        + [
            jax.ShapeDtypeStruct((examples, pad_rows, channels), bf16),
            jax.ShapeDtypeStruct((examples, patches, narrow), f32),
            jax.ShapeDtypeStruct((examples, patches, narrow), f32),
            jax.ShapeDtypeStruct((examples, patches, channels), f32),
            jax.ShapeDtypeStruct((16, sizes[13] * count), f32),
            jax.ShapeDtypeStruct((8, channels), f32),
        ]
        + [jax.ShapeDtypeStruct(s, bf16) for s in full],
        in_specs=[vm] * (1 + len(vecs) + 3) + [hbm] * len(far),
        out_specs=[hbm] * (len(far) + 4) + [vm] * 5,
        scratch_shapes=[
            pltpu.VMEM((examples, pad_rows, channels), bf16),
            pltpu.VMEM((examples, patches, narrow), f32),
            pltpu.VMEM((examples, patches, narrow), f32),
            pltpu.VMEM((examples, patches, channels), f32),
            DMA((3 + examples,)),
        ]
        + [pltpu.VMEM(shape(s), s.dtype) for s in shards[:4]]
        + [pltpu.VMEM((9, patches, patches), bf16), pltpu.VMEM((patches, full[1][0]), bf16)]
        + [pltpu.VMEM(s.shape, s.dtype) for s in shards[:4]]
        + total_scratch(A, B, 3, (8, 256))
        + gather_sems(A, B, len(items)),
        compiler_params=pltpu.CompilerParams(collective_id=cid, has_side_effects=True, vmem_limit_bytes=60 << 20),
        name="stem",
    )(feats, *[v[None] for v in vecs], *near, *far)
    return [g.reshape(-1, g.shape[-1]) for g in outs[: len(far)]], outs[len(far) :]


class Run:
    pass


class Written:
    def __init__(self, out):
        self.out = out

    def second(self):
        pass

    third = fourth = arrived = second


def stem_back_kernel(A, B, cuts, near_rows, total_rows, sizes, n_far, inside, *refs):
    (dact_h, feats_h, red_h, conv_h, expand_h, params, stats, w_red, w_conv, w_exp, small_f, small_b, small_a, small_q), refs = refs[:14], refs[14:]
    far, refs = refs[:n_far], refs[n_far:]
    (gfeats_h, shares), refs = refs[:2], refs[2:]
    far_out, near_out, refs = refs[:n_far], refs[n_far : n_far + 3], refs[n_far + 3 :]
    (dact, feats, expand, red, conv, gfeats, ex_sems, in_sems), refs = refs[:8], refs[8:]
    (ds_s, dy_s, ca_s, taps, gred, gconv, gexp, k_red, k_conv, k_exp), refs = refs[:10], refs[10:]
    sums, vsum, refs = refs[:4], refs[4:8], refs[8:]
    bufs, sems = refs[: 5 * len(cuts)], refs[5 * len(cuts) :]
    def load(k, i):
        src, dst = ((dact_h, dact), (feats_h, feats), (expand_h, expand))[k]
        return pltpu.make_async_copy(src.at[i], dst.at[i], ex_sems.at[k, i])

    def leave_feats(i):
        return pltpu.make_async_copy(gfeats.at[i], gfeats_h.at[i], ex_sems.at[3, i])

    load_conv, load_red = (pltpu.make_async_copy(a, b, in_sems.at[k]) for k, (a, b) in enumerate(((conv_h, conv), (red_h, red))))
    for i in range(feats.shape[0]):
        for k in range(3):
            load(k, i).start()
    load_conv.start()
    load_red.start()
    pc = Place(A, B)
    pc.greet()
    moves = scatter_items(pc, cuts, [*far, k_exp, k_conv, k_red], [*far_out, near_out[2], near_out[1], near_out[0]], bufs, sems)
    big, late = (moves[:-3], moves[-3:]) if inside else (moves, [Written(o) for o in (near_out[2], near_out[1], near_out[0])])
    m_exp, m_conv, m_red = late

    def leave(move, grad, packed, rows):
        if inside:
            pack(grad[...].astype(bf16), packed, rows)
            move.start()
        else:
            move.out[...] = grad[...].astype(bf16)

    adds = [Total(pc, j, *sums) for j in range(3)]
    vec_sum = Total(pc, 0, *vsum)
    examples, patches, channels = feats.shape
    narrow, width = red.shape[2], small_a.shape[1]
    for m in big:
        m.start()
    rows = [small_a[3:4], small_a[0:1], small_a[1:2], small_q[0:1, :width], small_q[0:1, 2 * width :], small_a[2:3], small_f[1:2], small_f[2:3]]
    rows += [small_b[:, q : q + width] for q in range(0, small_b.shape[1], width)]
    rows += [small_f[0:1]]
    vec_sum.begin(jnp.concatenate(rows + [jnp.zeros((16 - len(rows), width), f32)], 0))
    make_taps(taps, GRID)

    def hat_of(ref, i, j, w):
        return (ref[i] - stats[2 * j : 2 * j + 1, :w]) * stats[2 * j + 1 : 2 * j + 2, :w]

    def point(hat, j, w):
        return hat * params[2 * j : 2 * j + 1, :w] + params[2 * j + 1 : 2 * j + 2, :w]

    def each(fn, w):
        zero = jnp.zeros((1, w), f32)

        def body(i, s):
            dy, hat = fn(i)
            return s[0] + colsum(dy), s[1] + colsum(dy * hat)

        return lax.fori_loop(0, examples, body, (zero, zero))

    def norm_back(dy, hat, j, w, totals):
        scale = stats[2 * j + 1 : 2 * j + 2, :w] * params[2 * j : 2 * j + 1, :w]
        return (scale * (dy - totals[0] * (1.0 / total_rows) - hat * (totals[1] * (1.0 / total_rows)))).astype(bf16)

    run = Run()

    def fifth():
        def one(i):
            for k in range(3):
                load(k, i).wait()
            hat = hat_of(expand, i, 2, channels)
            _, slope = smooth_both(point(hat, 2, channels) + feats[i].astype(f32))
            dy = dact[i, :patches] * slope
            ds_s[i] = dy
            return dy, hat

        adds[2].begin(rows_of(each(one, channels)))

    def sixth():
        load_conv.wait()
        run.t3 = vectors_of(adds[2].end(), channels)
        gexp[...] = jnp.zeros(gexp.shape, f32)

        def one(i):
            de = norm_back(ds_s[i], hat_of(expand, i, 2, channels), 2, channels, run.t3)
            hat = hat_of(conv, i, 1, narrow)
            ca, slope = smooth_both(point(hat, 1, narrow))
            gexp[...] += dot_tn(ca.astype(bf16), de)
            dy = dot_nt(de, w_exp[...]) * slope
            dy_s[i] = dy
            return dy, hat

        adds[1].begin(rows_of(each(one, narrow)))
        leave(m_exp, gexp, k_exp, near_rows[2])

    def seventh():
        load_red.wait()
        run.t2 = vectors_of(adds[1].end(), narrow)
        gconv[...] = jnp.zeros(gconv.shape, f32)

        def one(i):
            dc = norm_back(dy_s[i], hat_of(conv, i, 1, narrow), 1, narrow, run.t2)
            hat = hat_of(red, i, 0, narrow)
            ra, slope = smooth_both(point(hat, 0, narrow))
            turned = ra.T.astype(bf16)
            dra = jnp.zeros((patches, narrow), f32)
            for t in range(9):
                moved = dot(taps[8 - t], dc).astype(bf16)
                at = slice(t * narrow, (t + 1) * narrow)
                gconv[at] += dot(turned, moved)
                dra = dra + dot_nt(moved, w_conv[at])
            dy = dra * slope
            dy_s[i] = dy
            return dy, hat

        adds[0].begin(rows_of(each(one, narrow)))
        leave(m_conv, gconv, k_conv, near_rows[1])

    def eighth():
        run.t1 = vectors_of(adds[0].end(), narrow)
        gred[...] = jnp.zeros(gred.shape, f32)

        def body(i, _):
            dr = norm_back(dy_s[i], hat_of(red, i, 0, narrow), 0, narrow, run.t1)
            ca_s[i] = dr
            gred[...] += dot_tn(feats[i], dr)
            return 0

        lax.fori_loop(0, examples, body, 0)
        leave(m_red, gred, k_red, near_rows[0])

    def ninth(lo, hi):
        def body(i, _):
            gfeats[i] = (ds_s[i] + dot_nt(ca_s[i], w_red[...])).astype(bf16)
            leave_feats(i).start()
            return 0

        lax.fori_loop(lo, hi, body, 0)

    def finish():
        v = vec_sum.end()
        me = pc.a * B + pc.b
        one = lambda k: v[k : k + 1]
        rows = [run.t1[1], run.t1[0], run.t2[1], run.t2[0], run.t3[1], run.t3[0], one(0), one(1), one(2), jnp.concatenate([one(3), one(4)], 1)]
        rows += [one(5), one(6), one(7), jnp.concatenate([one(k) for k in range(8, 8 + small_b.shape[1] // width)], 1), one(8 + small_b.shape[1] // width)]
        for k, row in enumerate(rows):
            wide = row.shape[1]
            turn = lax.rem(wide - me * sizes[k], wide)
            shares[k : k + 1] = pltpu.roll(jnp.broadcast_to(row, (8, wide)), turn, 1)[0:1, :128]
        shares[15:16] = jnp.zeros((1, 128), f32)

    queue = wave_stages(big, (0, 2, 4, 6), ["second", "third", "fourth", "arrived"])

    def advance(count):
        for _ in range(min(count, len(queue))):
            queue.pop(0)()

    fifth()
    advance(2)
    adds[2].middle()
    vec_sum.middle()
    advance(4)
    sixth()
    advance(2)
    adds[1].middle()
    m_exp.second()
    advance(4)
    seventh()
    m_exp.third()
    advance(2)
    adds[0].middle()
    m_conv.second()
    m_exp.fourth()
    advance(4)
    eighth()
    m_conv.third()
    advance(2)
    m_red.second()
    ninth(0, examples // 2)
    m_conv.fourth()
    m_red.third()
    advance(2)
    ninth(examples // 2, examples)
    m_red.fourth()
    finish()
    advance(len(queue))
    m_exp.arrived()
    m_conv.arrived()
    m_red.arrived()
    for m in moves:
        m.drain()
    for s in adds + [vec_sum]:
        s.drain()
    lax.fori_loop(0, examples, lambda i, _: (leave_feats(i).wait(), 0)[1], 0)


def stem_backward(A, B, dact, feats, red, conv, expand, params, stats, w_red, w_conv, w_exp, smalls, sizes, grads, parts, inside, cid):
    A2, Z, count = A // 2, B // 2, A * B
    examples, patches, channels = feats.shape
    narrow = red.shape[2]
    near = [w_red, w_conv, w_exp]
    near_rows = [w.shape[0] // count for w in near]
    packed = [(tile_rows(r), w.shape[1]) for r, w in zip(near_rows, near)]
    cuts = cut([(g.shape[1], q) for g, q in zip(grads, parts)] + [(p[1], 1) for p in reversed(packed) if inside])
    shapes = [(g.shape[0] // count, g.shape[1]) for g in grads] + packed[::-1]
    outs = [jax.ShapeDtypeStruct(feats.shape, bf16), jax.ShapeDtypeStruct((16, 128), f32)]
    outs += [jax.ShapeDtypeStruct(s, f32) for s in shapes[: len(grads)]]
    outs += [jax.ShapeDtypeStruct((r, w.shape[1]), f32) if inside else jax.ShapeDtypeStruct(w.shape, bf16) for r, w in zip(near_rows, near)]
    hbm, vm = pl.BlockSpec(memory_space=pl.ANY), pl.BlockSpec(memory_space=pltpu.VMEM)
    lead = (A2, 2, Z, 2)
    return pl.pallas_call(
        functools.partial(stem_back_kernel, A, B, cuts, near_rows, float(examples * count * patches), sizes, len(grads), inside),
        out_shape=outs,
        in_specs=[hbm] * 5 + [vm] * 9 + [hbm] * len(grads),
        out_specs=[hbm] + [vm] * (len(outs) - 1),
        scratch_shapes=[pltpu.VMEM(a.shape, a.dtype) for a in (dact, feats, expand, red, conv, feats)]
        + [
            DMA((4, examples)),
            DMA((2,)),
            pltpu.VMEM((examples, patches, channels), f32),
            pltpu.VMEM((examples, patches, narrow), f32),
            pltpu.VMEM((examples, patches, narrow), bf16),
            pltpu.VMEM((9, patches, patches), bf16),
        ]
        + [pltpu.VMEM(w.shape, f32) for w in near]
        + [pltpu.VMEM(lead + p if inside else (16, 128), bf16) for p in packed]
        + total_scratch(A, B, 3, (8, 256))
        + total_scratch(A, B, 1, (16, smalls[2].shape[1]))
        + (scatter_buffers(A, B, cuts, shapes) + scatter_sems(A, B, len(cuts)) if cuts else []),
        compiler_params=pltpu.CompilerParams(collective_id=cid, has_side_effects=True, vmem_limit_bytes=62 << 20),
        name="stem_back",
    )(dact, feats, red, conv, expand, params, stats, w_red, w_conv, w_exp, *smalls, *[split_rows(A, B, g) for g in grads])


def finish_kernel(n, *refs):
    shares, ins, outs, vecs = refs[0], refs[1 : 1 + n], refs[1 + n : 1 + 2 * n], refs[1 + 2 * n :]
    for a, b in zip(ins, outs):
        b[...] = a[...]
    for v, ref in enumerate(vecs):
        ref[...] = shares[v, : ref.shape[0]]


def finish(shares, sizes, arrays):
    vm = pl.BlockSpec(memory_space=pltpu.VMEM)
    n = len(arrays)
    outs = pl.pallas_call(
        functools.partial(finish_kernel, n),
        out_shape=[jax.ShapeDtypeStruct(a.shape, a.dtype) for a in arrays] + [jax.ShapeDtypeStruct((s,), f32) for s in sizes],
        in_specs=[vm] * (1 + n),
        out_specs=[vm] * (n + len(sizes)),
        compiler_params=pltpu.CompilerParams(vmem_limit_bytes=48 << 20),
        name="finish",
    )(shares, *arrays)
    return outs[:n], outs[n:]


AXES = ("dp", "fsdp")


def local(
    feats, text, lengths, cotangent,
    w_red, bn1_gain, bn1_bias, w_conv, bn2_gain, bn2_bias, w_exp, bn3_gain, bn3_bias, w_patch, b_patch,
    ln1_gain, ln1_bias, w_qkv, b_qv, w_out, b_out, ln2_gain, ln2_bias, w_up, b_up, w_down, b_down,
):
    A, B = lax.axis_size("dp"), lax.axis_size("fsdp")
    vecs = (bn1_gain, bn1_bias, bn2_gain, bn2_bias, bn3_gain, bn3_bias, b_patch, ln1_gain, ln1_bias, b_qv, b_out, ln2_gain, ln2_bias, b_up, b_down)
    sizes = [v.shape[0] for v in vecs]
    patches, slots = feats.shape[1], text.shape[1]
    far, near = stem_forward(A, B, feats, vecs, (w_red, w_conv, w_exp, w_patch, w_qkv, w_out, w_up, w_down), PATCH_PAD, (1, 3, 1, 4, 3), 0)
    full_patch, full_qkv, full_out, full_up, full_down = far
    act, red, conv, expand, params, stats, full_red, full_conv, full_exp = near
    x, h1, qkv, o, x2, h2 = attend(lengths, act, text, full_patch, full_qkv, full_out, params, patches, 2)
    output, dx2, g_up, g_down, small_b, small_f = ffn(lengths, h2, x2, cotangent, full_up, full_down, params, patches, 2, 512)
    inside = w_qkv.shape[0] >= 16
    first = [g_up, g_down] if inside else []
    dact, grad_text, g_qkv, g_out, g_patch, small_a, small_q, *sums = attend_back(
        A, B, lengths, dx2, x, h1, qkv, o, act, full_patch, full_qkv, full_out, params, first, (4, 3)[: len(first)], slots, patches, 1, 1
    )
    second = [g_qkv, g_out, g_patch] if inside else []
    grad_feats, shares, *more = stem_backward(
        A, B, dact, feats, red, conv, expand, params, stats, full_red, full_conv, full_exp, (small_f, small_b, small_a, small_q), sizes, second, (3, 1, 1)[: len(second)], inside, 2
    )
    if not inside:
        sums = [lax.psum_scatter(g.astype(f32), AXES, scatter_dimension=0, tiled=True) for g in (g_up, g_down)]
        more = [lax.psum_scatter(g.astype(f32), AXES, scatter_dimension=0, tiled=True) for g in (g_qkv, g_out, g_patch, *more)]
    (grad_feats, s_up, s_down, s_qkv, s_out, s_patch, s_red, s_conv, s_exp), vectors = finish(shares, sizes, [grad_feats, *sums, *more])
    (s_bn1_gain, s_bn1_bias, s_bn2_gain, s_bn2_bias, s_bn3_gain, s_bn3_bias, s_b_patch, s_ln1_gain, s_ln1_bias, s_b_qv, s_b_out, s_ln2_gain, s_ln2_bias, s_b_up, s_b_down) = vectors
    return (
        output, grad_feats, grad_text,
        s_red, s_bn1_gain, s_bn1_bias, s_conv, s_bn2_gain, s_bn2_bias, s_exp, s_bn3_gain, s_bn3_bias, s_patch, s_b_patch,
        s_ln1_gain, s_ln1_bias, s_qkv, s_b_qv, s_out, s_b_out, s_ln2_gain, s_ln2_bias, s_up, s_b_up, s_down, s_b_down,
    )


def solution(mesh):
    every = ("dp", "fsdp")
    v, m, t = P(every), P(every, None), P(every, None, None)
    weights = (m, v, v, m, v, v, m, v, v, m, v, v, v, m, v, m, v, v, v, m, v, m, v)
    return jax.shard_map(local, mesh=mesh, in_specs=(t, t, v, t) + weights, out_specs=(t, t, t) + weights, check_vma=False)
```

```python
import functools

import jax
import jax.numpy as jnp
from jax import lax
from jax.experimental import pallas as pl
from jax.experimental.pallas import tpu as pltpu
from jax.sharding import PartitionSpec as P
MESH = pl.DeviceIdType.MESH
DMA = pltpu.SemaphoreType.DMA


def rcopy(src, dst, send, recv, dev):
    return pltpu.make_async_remote_copy(
        src_ref=src, dst_ref=dst, send_sem=send, recv_sem=recv, device_id=dev, device_id_type=MESH
    )


class Place:
    def __init__(self, A, B):
        self.A, self.B, self.A2, self.Z = A, B, A // 2, B // 2
        a, b = lax.axis_index("dp"), lax.axis_index("fsdp")
        self.a, self.b = a, b
        self.y, self.x = a // 2, lax.rem(a, 2)
        self.z, self.c = b // 2, lax.rem(b, 2)
        self.zs = [lax.rem(self.z + k, self.Z) for k in range(1, self.Z)]
        self.ys = [lax.rem(self.y + k, self.A2) for k in range(1, self.A2)]
        self.zfrom = [lax.rem(self.z + self.Z - k, self.Z) for k in range(1, self.Z)]
        self.yfrom = [lax.rem(self.y + self.A2 - k, self.A2) for k in range(1, self.A2)]
        self.me = (a, b)
        self.core = (a, self.z * 2 + 1 - self.c)
        self.xpeer = (self.y * 2 + 1 - self.x, b)
        self.c1, self.x1 = 1 - self.c, 1 - self.x
        self.dpeers = [(lax.rem(a + k, A), b) for k in range(1, A)]
        self.zpeers = [(a, zz * 2 + self.c) for zz in self.zs]
        self.ypeers = [(yy * 2 + self.x, b) for yy in self.ys]

        self.bpeers = [(a, lax.rem(b + k, B)) for k in range(1, B)]

    def greet(self, totals=True):
        peers = self.dpeers + self.bpeers if totals else self.zpeers + self.ypeers + [self.xpeer, self.core]
        bar = pltpu.get_barrier_semaphore()
        for p in peers:
            pl.semaphore_signal(bar, inc=1, device_id=p, device_id_type=MESH)
        pl.semaphore_wait(bar, len(peers))


class GatherItem:
    def __init__(self, pc, i, cols, order, src, out, sems):
        self.pc, self.order, self.src_ref, self.out = pc, order, src, out
        self.cols = slice(None) if cols is None else pl.ds(*cols)
        self.loc, self.s1, self.r1, self.s2, self.r2, self.s3, self.r3, self.sc, self.rc = [s.at[i] for s in sems]
        self.here = False
        p = pc
        every = slice(None)
        self.got2 = [(p.y, p.x1)] if order == 0 else [(yy, p.x) for yy in p.yfrom]
        self.got3 = [(yy, every) for yy in p.yfrom] if order == 0 else [(every, p.x1)]
        self.to2 = [p.xpeer] if order == 0 else p.ypeers
        self.to3 = p.ypeers if order == 0 else [p.xpeer]
        self.crossed = [(p.y, p.x)] + self.got2 + self.got3

    def src(self):
        return self.src_ref.at[:, self.cols]

    def block(self, y, x, z, c):
        return self.out.at[y, x, z, c, :, self.cols]

    def local(self):
        p = self.pc
        return pltpu.make_async_copy(self.src(), self.block(p.y, p.x, p.z, p.c), self.loc)

    def send1(self, k):
        p = self.pc
        return rcopy(self.src(), self.block(p.y, p.x, p.z, p.c), self.s1.at[k], self.r1.at[k], p.zpeers[k])

    def send2(self, k):
        p = self.pc
        col = self.block(p.y, p.x, slice(None), p.c)
        return rcopy(col, col, self.s2.at[k], self.r2.at[k], self.to2[k])

    def send3(self, k):
        p, every = self.pc, slice(None)
        blk = self.block(p.y, every, every, p.c) if self.order == 0 else self.block(every, p.x, every, p.c)
        return rcopy(blk, blk, self.s3.at[k], self.r3.at[k], self.to3[k])

    def cross(self, j, c):
        blk = self.block(*self.crossed[j], slice(None), c)
        return rcopy(blk, blk, self.sc.at[j], self.rc.at[j], self.pc.core)

    def wait(self, got, send, recv):
        rcopy(got, got, send, recv, self.pc.me).wait_recv()

    def start(self):
        self.local().start()
        for k in range(len(self.pc.zpeers)):
            self.send1(k).start()

    def second(self):
        p = self.pc
        self.local().wait()
        for k, zz in enumerate(p.zfrom):
            self.wait(self.block(p.y, p.x, zz, p.c), self.s1.at[k], self.r1.at[k])
        for k in range(len(self.to2)):
            self.send2(k).start()
        self.cross(0, p.c).start()

    def third(self):
        p = self.pc
        for k, (yy, xx) in enumerate(self.got2):
            self.wait(self.block(yy, xx, slice(None), p.c), self.s2.at[k], self.r2.at[k])
        for k in range(len(self.to3)):
            self.send3(k).start()
        for k in range(len(self.got2)):
            self.cross(1 + k, p.c).start()

    def fourth(self):
        p = self.pc
        for k, (yy, xx) in enumerate(self.got3):
            self.wait(self.block(yy, xx, slice(None), p.c), self.s3.at[k], self.r3.at[k])
            self.cross(1 + len(self.got2) + k, p.c).start()

    def arrived(self):
        if self.here:
            return
        self.here = True
        for j in range(len(self.crossed)):
            self.cross(j, self.pc.c1).wait_recv()

    def drain(self):
        for k in range(len(self.pc.zpeers)):
            self.send1(k).wait_send()
        for k in range(len(self.to2)):
            self.send2(k).wait_send()
        for k in range(len(self.to3)):
            self.send3(k).wait_send()
        for j in range(len(self.crossed)):
            self.cross(j, self.pc.c).wait_send()


def gather_sems(A, B, n):
    A2, Z = A // 2, B // 2
    m = max(A2 - 1, 1)
    return [DMA((n,)), DMA((n, Z - 1)), DMA((n, Z - 1)), DMA((n, m)), DMA((n, m)), DMA((n, m)), DMA((n, m)), DMA((n, A2 + 1)), DMA((n, A2 + 1))]


def wave(items, lags, stages, hooks=None):
    hooks = hooks or {}
    last = max([len(items) + lags[-1]] + [t + 1 for t in hooks])
    for t in range(last):
        for lag, stage in zip(reversed(lags), reversed(stages)):
            if 0 <= t - lag < len(items):
                getattr(items[t - lag], stage)()
        for hook in hooks.get(t, ()):
            hook()


def wave_stages(items, lags, stages):
    out = []
    for t in range(len(items) + lags[-1]):
        for lag, stage in zip(reversed(lags), reversed(stages)):
            if 0 <= t - lag < len(items):
                out.append(getattr(items[t - lag], stage))
    return out


def cut(widths_parts):
    items, order = [], 0
    for i, (width, parts) in enumerate(widths_parts):
        for q in range(parts):
            items.append((i, None if parts == 1 else (q * (width // parts), width // parts), order))
            order = 1 - order
    return items


class ScatterItem:
    def __init__(self, pc, i, order, src, out, own, r0, r1, r2, r3, sems, cols=None):
        self.pc, self.order, self.src, self.out = pc, order, src, out
        self.cols = slice(None) if cols is None else pl.ds(*cols)
        self.own, self.r0, self.r1, self.r2, self.r3 = own, r0, r1, r2, r3
        self.loc, self.s0, self.q0, self.s1, self.q1, self.s2, self.q2, self.s3, self.q3 = [s.at[i] for s in sems]
        self.sends = []

    def go(self, copy):
        copy().start()
        self.sends.append(copy)

    def start(self):
        p = self.pc
        self.go(lambda: rcopy(self.src.at[:, :, :, p.c1, :, self.cols], self.r0, self.s0, self.q0, p.core))
        self.local().start()

    def local(self):
        return pltpu.make_async_copy(self.src.at[:, :, :, self.pc.c, :, self.cols], self.own, self.loc)

    def add(self, dst, others, lead):
        total = 1
        for d in lead:
            total *= d

        def body(t, _):
            idx, rest = [], t
            for d in reversed(lead):
                idx.append(lax.rem(rest, d))
                rest = rest // d
            idx = tuple(reversed(idx))
            v = dst[idx].astype(jnp.float32)
            for o in others:
                v = v + o[idx].astype(jnp.float32)
            dst[idx] = v.astype(jnp.bfloat16)
            return 0

        lax.fori_loop(0, total, body, 0)

    def second(self):
        p = self.pc
        self.local().wait()
        rcopy(self.r0, self.r0, self.s0, self.q0, p.me).wait_recv()
        self.add(self.own, [self.r0], (p.A2, 2, p.Z))
        if self.order == 0:
            self.go(lambda: rcopy(self.own.at[:, p.x1], self.r1.at[0], self.s1.at[0], self.q1.at[0], p.xpeer))
        else:
            for k, yy in enumerate(p.ys):
                self.go(lambda k=k, yy=yy: rcopy(self.own.at[yy], self.r1.at[k], self.s1.at[k], self.q1.at[k], p.ypeers[k]))

    def third(self):
        p = self.pc
        n1 = 1 if self.order == 0 else p.A2 - 1
        for k in range(n1):
            rcopy(self.r1.at[k], self.r1.at[k], self.s1.at[k], self.q1.at[k], p.me).wait_recv()
        mine = self.own.at[:, p.x] if self.order == 0 else self.own.at[p.y]
        self.add(mine, [self.r1.at[k] for k in range(n1)], (p.A2 if self.order == 0 else 2, p.Z))
        if self.order == 0:
            for k, yy in enumerate(p.ys):
                self.go(lambda k=k, yy=yy: rcopy(self.own.at[yy, p.x], self.r2.at[k], self.s2.at[k], self.q2.at[k], p.ypeers[k]))
        else:
            self.go(lambda: rcopy(self.own.at[p.y, p.x1], self.r2.at[0], self.s2.at[0], self.q2.at[0], p.xpeer))

    def fourth(self):
        p = self.pc
        n2 = p.A2 - 1 if self.order == 0 else 1
        for k in range(n2):
            rcopy(self.r2.at[k], self.r2.at[k], self.s2.at[k], self.q2.at[k], p.me).wait_recv()
        self.add(self.own.at[p.y, p.x], [self.r2.at[k] for k in range(n2)], (p.Z,))
        for k, zz in enumerate(p.zs):
            self.go(lambda k=k, zz=zz: rcopy(self.own.at[p.y, p.x, zz], self.r3.at[k], self.s3.at[k], self.q3.at[k], p.zpeers[k]))

    def arrived(self):
        p = self.pc
        for k in range(p.Z - 1):
            rcopy(self.r3.at[k], self.r3.at[k], self.s3.at[k], self.q3.at[k], p.me).wait_recv()
        v = self.own[p.y, p.x, p.z].astype(jnp.float32)
        for k in range(p.Z - 1):
            v = v + self.r3[k].astype(jnp.float32)
        self.out[:, self.cols] = v[: self.out.shape[0]]

    def drain(self):
        for copy in self.sends:
            copy().wait_send()


def scatter_sems(A, B, n):
    m, Z = max(A // 2 - 1, 1), B // 2
    return [DMA((n,)), DMA((n,)), DMA((n,)), DMA((n, m)), DMA((n, m)), DMA((n, m)), DMA((n, m)), DMA((n, Z - 1)), DMA((n, Z - 1))]


def scatter_scratch(A, B, shape, order):
    A2, Z = A // 2, B // 2
    n1 = (1, A2, Z) if order == 0 else (A2 - 1, 2, Z)
    n2 = (A2 - 1, Z) if order == 0 else (1, Z)
    return [pltpu.VMEM(s + shape, jnp.bfloat16) for s in ((A2, 2, Z), (A2, 2, Z), n1, n2, (Z - 1,))]


def scatter_items(pc, cuts, srcs, outs, bufs, sems, base=0):
    return [ScatterItem(pc, base + j, o, srcs[i], outs[i], *bufs[5 * j : 5 * j + 5], sems, cols) for j, (i, cols, o) in enumerate(cuts)]


def scatter_buffers(A, B, cuts, shapes):
    out = []
    for i, cols, order in cuts:
        out += scatter_scratch(A, B, (shapes[i][0], shapes[i][1] if cols is None else cols[1]), order)
    return out


def split_rows(A, B, g):
    return g.reshape((A // 2, 2, B // 2, 2, g.shape[0] // (A * B), g.shape[1]))


HEAD_DIM = 64
GRID = 14
ln_eps = 1e-06
bn_eps = 1e-05
gelu_coef = 0.7978845608028654
gelu_cube = gelu_coef * 0.044715
bf16, f32 = jnp.bfloat16, jnp.float32
PATCH_PAD = 208


def dot(left, right):
    return jnp.dot(left, right, preferred_element_type=f32)


def dot_nt(left, right):
    return lax.dot_general(left, right, (((1,), (1,)), ((), ())), preferred_element_type=f32)


def dot_tn(left, right):
    return lax.dot_general(left, right, (((0,), (0,)), ((), ())), preferred_element_type=f32)


def smooth(v):
    return (0.5 * v) * (1.0 + jnp.tanh(v * (gelu_coef + gelu_cube * (v * v))))


def smooth_both(v):
    sq = v * v
    t = jnp.tanh(v * (gelu_coef + gelu_cube * sq))
    half = 0.5 * v
    up = 1.0 + t
    return half * up, 0.5 * up + half * ((1.0 - t * t) * (gelu_coef + 3.0 * gelu_cube * sq))


def ln_parts(v):
    center = v - jnp.mean(v, -1, keepdims=True)
    inv = lax.rsqrt(jnp.mean(center * center, -1, keepdims=True) + ln_eps)
    return center * inv, inv


def ln_back(dy, hat, inv, gain):
    dh = dy * gain
    return inv * (dh - jnp.mean(dh, -1, keepdims=True) - hat * jnp.mean(dh * hat, -1, keepdims=True))


def colsum(v):
    return jnp.sum(v, 0, keepdims=True)


def iota(shape, dim):
    return lax.broadcasted_iota(jnp.int32, shape, dim)


def valid_of(position, length, patches):
    text = position - PATCH_PAD
    return jnp.where((position < patches) | ((text >= 0) & (text < length)), 1.0, 0.0).astype(f32)


def spread(rows, patches, seq):
    i, j = iota((rows, seq), 0), iota((rows, seq), 1)
    hit = ((i < patches) & (j == i)) | ((i >= PATCH_PAD) & (j == i - (PATCH_PAD - patches)))
    return jnp.where(hit, 1.0, 0.0).astype(bf16)


def gather_rows(seq, rows, patches):
    j, i = iota((seq, rows), 0), iota((seq, rows), 1)
    hit = ((i < patches) & (j == i)) | ((i >= PATCH_PAD) & (j == i - (PATCH_PAD - patches)))
    return jnp.where(hit, 1.0, 0.0).astype(bf16)


def lane_masks(width):
    lane = iota((1, 2 * width), 1)
    low = jnp.where(lane < width, 1.0, 0.0).astype(bf16)
    return low, (1.0 - low.astype(f32)).astype(bf16)


class Plan:
    def __init__(self, step, steps, points, stages):
        self.step, self.steps, self.points = step, steps, points
        total, n = steps * points, len(stages)
        self.due = [stages[n * q // total : n * (q + 1) // total] for q in range(total)]

    def __call__(self, point):
        for s in range(self.steps):
            stages = self.due[s * self.points + point]
            if stages:

                @pl.when(self.step == s)
                def _():
                    for stage in stages:
                        stage()


def attend_kernel(n, patches, len_ref, act, text, wp, wqkv, wout, params, x_o, h1_o, qkv_o, o_o, x2_o, h2_o):
    width = text.shape[2]
    slots = text.shape[1]
    rows = PATCH_PAD + slots
    step = pl.program_id(0)
    lows = lane_masks(HEAD_DIM)
    bp, g1, b1, bo, g2, b2 = (params[v : v + 1, :width] for v in (6, 7, 8, 10, 11, 12))
    bqkv = jnp.concatenate([params[9:10, :width], jnp.zeros((1, width), f32), params[9:10, width : 2 * width]], 1)
    patch = dot(act[...].reshape(n * PATCH_PAD, act.shape[2]), wp[...]) + bp
    for i in range(n):
        length = len_ref[step * n + i]
        keep = jnp.where(iota((slots, 1), 0) < length, 1.0, 0.0).astype(f32)
        x_o[i * rows : i * rows + PATCH_PAD] = patch[i * PATCH_PAD : (i + 1) * PATCH_PAD]
        x_o[i * rows + PATCH_PAD : (i + 1) * rows] = text[i].astype(f32) * keep
    hat, _ = ln_parts(x_o[...])
    h1 = (hat * g1 + b1).astype(bf16)
    h1_o[...] = h1
    qkv_o[...] = (dot(h1, wqkv[...]) + bqkv).astype(bf16)
    for i in range(n):
        at = slice(i * rows, (i + 1) * rows)
        bias = jnp.where(valid_of(iota((1, rows), 1), len_ref[step * n + i], patches) > 0.5, 0.0, -1e30)
        for j in range(width // (2 * HEAD_DIM)):
            cols = [slice(p * width + j * 128, p * width + (j + 1) * 128) for p in range(3)]
            q = qkv_o[at, cols[0]] * bf16(HEAD_DIM**-0.5)
            k, v = qkv_o[at, cols[1]], qkv_o[at, cols[2]]
            mixed = 0.0
            for low in lows:
                s = dot_nt(q * low, k) + bias
                e = jnp.exp(s - jnp.max(s, -1, keepdims=True))
                pr = (e * (1.0 / jnp.sum(e, -1, keepdims=True))).astype(bf16)
                mixed = mixed + dot(pr, v * low)
            o_o[at, cols[0]] = mixed.astype(bf16)
    x2 = x_o[...] + dot(o_o[...], wout[...]) + bo
    x2_o[...] = x2
    hat2, _ = ln_parts(x2)
    h2_o[...] = (hat2 * g2 + b2).astype(bf16)


def whole(shape):
    return pl.BlockSpec(shape, lambda *_: (0,) * len(shape), pipeline_mode=pl.Buffered(1))


def attend(lengths, act, text, wp, wqkv, wout, params, patches, n):
    examples, slots, width = text.shape
    rows = PATCH_PAD + slots
    steps = examples // n
    blk = lambda w: pl.BlockSpec((n * rows, w), lambda s: (s, 0))
    out = lambda w, t: jax.ShapeDtypeStruct((examples * rows, w), t)
    return pl.pallas_call(
        functools.partial(attend_kernel, n, patches),
        grid=(steps,),
        out_shape=[out(width, f32), out(width, bf16), out(3 * width, bf16), out(width, bf16), out(width, f32), out(width, bf16)],
        in_specs=[
            pl.BlockSpec(memory_space=pltpu.SMEM),
            pl.BlockSpec((n,) + act.shape[1:], lambda s: (s, 0, 0)),
            pl.BlockSpec((n,) + text.shape[1:], lambda s: (s, 0, 0)),
        ]
        + [whole(w.shape) for w in (wp, wqkv, wout, params)],
        out_specs=[blk(width), blk(width), blk(3 * width), blk(width), blk(width), blk(width)],
        compiler_params=pltpu.CompilerParams(vmem_limit_bytes=56 << 20),
        name="attend",
    )(lengths, act, text, wp, wqkv, wout, params)


def ffn_kernel(n, patches, len_ref, h2, x2_h, cot, wu, bu, wd, params, out_h, dx2_h, gup, gdown, gbu, small, g_s, h2t, acc, dh, m_s, du_s, x2, out, sems):
    c, last = pl.program_id(0), pl.num_programs(0) - 1
    examples, seq, width = cot.shape
    rows = PATCH_PAD + seq - patches
    blocks = examples // n
    load = pltpu.make_async_copy(x2_h, x2, sems.at[0, 0])

    def leave(i, at):
        return pltpu.make_async_copy(out.at[i], out_h.at[i], sems.at[1, i]), pltpu.make_async_copy(dh.at[at], dx2_h.at[at], sems.at[2, i])

    @pl.when(c == 0)
    def _():
        load.start()

        def body(i, _):
            at = pl.ds(pl.multiple_of(i * rows, 16), rows)
            valid = valid_of(iota((rows, 1), 0), len_ref[i], patches)
            g_s[at] = (dot(spread(rows, patches, seq), cot[i]) * valid).astype(bf16)
            acc[at] = jnp.zeros((rows, width), f32)
            dh[at] = jnp.zeros((rows, width), f32)
            return 0

        lax.fori_loop(0, examples, body, 0)
        h2t[...] = h2[...].T

    def block(r, sums):
        at = pl.ds(pl.multiple_of(r * (n * rows), 16), n * rows)
        m, slope = smooth_both(dot(h2[at], wu[...]) + bu[13:14])
        m = m.astype(bf16)
        m_s[at] = m
        acc[at] += dot(m, wd[...])
        du = dot_nt(g_s[at], wd[...]) * slope
        sums = sums + colsum(du)
        du = du.astype(bf16)
        du_s[at] = du
        dh[at] += dot_nt(du, wu[...])
        return sums

    gbu[...] = lax.fori_loop(0, blocks, block, jnp.zeros(gbu.shape, f32), unroll=True)
    gup[...] = dot(h2t[...], du_s[...]).astype(bf16)
    gdown[...] = dot_tn(m_s[...], g_s[...]).astype(bf16)

    @pl.when(c == last)
    def _():
        load.wait()

        def body(i, sums):
            at = pl.ds(pl.multiple_of(i * rows, 16), rows)
            valid = valid_of(iota((rows, 1), 0), len_ref[i], patches)
            result = (acc[at] + x2[at] + params[14:15, :width]) * valid
            out[i] = dot(gather_rows(seq, rows, patches), result.astype(bf16)).astype(bf16)
            hat, inv = ln_parts(x2[at])
            g = g_s[at].astype(f32)
            dy = dh[at]
            dh[at] = g + ln_back(dy, hat, inv, params[11:12, :width])
            for copy in leave(i, at):
                copy.start()
            return sums[0] + colsum(g), sums[1] + colsum(dy * hat), sums[2] + colsum(dy)

        zero = jnp.zeros((1, width), f32)
        a, b, d = lax.fori_loop(0, examples, body, (zero, zero, zero))
        small[0:1], small[1:2], small[2:3] = a, b, d
        small[3:8] = jnp.zeros((5, width), f32)

        def wait(i, _):
            for copy in leave(i, pl.ds(pl.multiple_of(i * rows, 16), rows)):
                copy.wait()
            return 0

        lax.fori_loop(0, examples, wait, 0)


def ffn(lengths, h2, x2, cot, wu, wd, params, patches, n, chunk):
    examples, seq, width = cot.shape
    total, hidden = h2.shape[0], wu.shape[1]
    col = lambda rows: pl.BlockSpec((rows, chunk), lambda c: (0, c))
    row = pl.BlockSpec((chunk, width), lambda c: (c, 0))
    return pl.pallas_call(
        functools.partial(ffn_kernel, n, patches),
        grid=(hidden // chunk,),
        out_shape=[
            jax.ShapeDtypeStruct(cot.shape, bf16),
            jax.ShapeDtypeStruct((total, width), f32),
            jax.ShapeDtypeStruct((width, hidden), bf16),
            jax.ShapeDtypeStruct((hidden, width), bf16),
            jax.ShapeDtypeStruct((1, hidden), f32),
            jax.ShapeDtypeStruct((8, width), f32),
        ],
        in_specs=[pl.BlockSpec(memory_space=pltpu.SMEM), whole(h2.shape), pl.BlockSpec(memory_space=pl.ANY), whole(cot.shape), col(width), col(params.shape[0]), row, whole(params.shape)],
        out_specs=[pl.BlockSpec(memory_space=pl.ANY), pl.BlockSpec(memory_space=pl.ANY), col(width), row, col(1), whole((8, width))],
        scratch_shapes=[
            pltpu.VMEM((total, width), bf16),
            pltpu.VMEM((width, total), bf16),
            pltpu.VMEM((total, width), f32),
            pltpu.VMEM((total, width), f32),
            pltpu.VMEM((total, chunk), bf16),
            pltpu.VMEM((total, chunk), bf16),
            pltpu.VMEM((total, width), f32),
            pltpu.VMEM(cot.shape, bf16),
            DMA((3, examples)),
        ],
        compiler_params=pltpu.CompilerParams(vmem_limit_bytes=60 << 20),
        name="ffn",
    )(lengths, h2, x2, cot, wu, params, wd, params)


def attend_back_kernel(A, B, n, patches, slots, cuts, n_sc, *refs):
    (len_ref, dx2, x, h1, qkv, o, act, wp, wqkv, wout, params), refs = refs[:11], refs[11:]
    srcs, refs = refs[:n_sc], refs[n_sc:]
    (dact, gtext, gqkv, gout, gpatch, small, small3), refs = refs[:7], refs[7:]
    sums, refs = refs[:n_sc], refs[n_sc:]
    (aqkv, aout, apatch, do_s, dq_s), refs = refs[:5], refs[5:]
    step, last = pl.program_id(0), pl.num_programs(0) - 1
    width = x.shape[1]
    g1 = params[7:8, :width]
    rows = PATCH_PAD + slots
    lows = lane_masks(HEAD_DIM)
    scale = bf16(HEAD_DIM**-0.5)

    @pl.when(step == 0)
    def _():
        for ref in (aqkv, aout, apatch, small, small3):
            ref[...] = jnp.zeros(ref.shape, f32)

    moves, stages = [], []
    if n_sc:
        pc = Place(A, B)
        pl.when(step == 0)(lambda: pc.greet(False))
        moves = scatter_items(pc, cuts, srcs, sums, refs[: 5 * len(cuts)], refs[5 * len(cuts) :])
        stages = wave_stages(moves, (0, 2, 5, 8, 11), ["start", "second", "third", "fourth", "arrived"])
    progress = Plan(step, 6, 3, stages)
    progress(0)
    db = dx2[...].astype(bf16)
    do_s[...] = dot_nt(db, wout[...]).astype(bf16)
    aout[...] += dot_tn(o[...], db)
    for i in range(n):
        at = slice(i * rows, (i + 1) * rows)
        bias = jnp.where(valid_of(iota((rows, 1), 0), len_ref[step * n + i], patches) > 0.5, 0.0, -1e30)
        for j in range(width // (2 * HEAD_DIM)):
            cols = [slice(p * width + j * 128, p * width + (j + 1) * 128) for p in range(3)]
            q, k, v = qkv[at, cols[0]] * scale, qkv[at, cols[1]], qkv[at, cols[2]]
            ks = k * scale
            do = do_s[at, cols[0]]
            dq = dk = dv = 0.0
            for low in lows:
                s = dot_nt(k * low, q) + bias
                e = jnp.exp(s - jnp.max(s, 0, keepdims=True))
                p = e * (1.0 / jnp.sum(e, 0, keepdims=True))
                dv = dv + dot(p.astype(bf16), do * low)
                dp = dot_nt(v * low, do)
                ds = (p * (dp - jnp.sum(p * dp, 0, keepdims=True))).astype(bf16)
                dk = dk + dot(ds, q * low)
                dq = dq + dot_tn(ds, ks * low)
            dq_s[at, cols[0]], dq_s[at, cols[1]], dq_s[at, cols[2]] = dq.astype(bf16), dk.astype(bf16), dv.astype(bf16)
    progress(1)
    aqkv[...] += dot_tn(h1[...], dq_s[...])
    dh1 = dot_nt(dq_s[...], wqkv[...])
    hat, inv = ln_parts(x[...])
    dx = dx2[...] + ln_back(dh1, hat, inv, g1)
    progress(2)
    dps = []
    for i in range(n):
        keep = jnp.where(iota((slots, 1), 0) < len_ref[step * n + i], 1.0, 0.0).astype(f32)
        gtext[i] = (dx[i * rows + PATCH_PAD : (i + 1) * rows] * keep).astype(bf16)
        inside = iota((PATCH_PAD, 1), 0) < patches
        dps.append(jnp.where(inside, dx[i * rows : i * rows + PATCH_PAD], 0.0).astype(bf16))
    dp = jnp.concatenate(dps, 0)
    dact[...] = dot_nt(dp, wp[...]).reshape(dact.shape)
    apatch[...] += dot_tn(act[...].reshape(n * PATCH_PAD, act.shape[2]), dp)
    small[0:1] += colsum(dh1 * hat)
    small[1:2] += colsum(dh1)
    small[2:3] += colsum(db.astype(f32))
    small[3:4] += colsum(dp.astype(f32))
    small3[0:1] += colsum(dq_s[...].astype(f32))

    @pl.when(step == last)
    def _():
        for m in moves:
            m.drain()
        gqkv[...], gout[...], gpatch[...] = aqkv[...].astype(bf16), aout[...].astype(bf16), apatch[...].astype(bf16)


def attend_back(A, B, lengths, dx2, x, h1, qkv, o, act, wp, wqkv, wout, params, grads, parts, slots, patches, n, cid):
    examples, _, channels = act.shape
    width = x.shape[1]
    rows = PATCH_PAD + slots
    blk = lambda w: pl.BlockSpec((n * rows, w), lambda s: (s, 0))
    assert examples == 6 * n
    cuts = cut([(g.shape[1], q) for g, q in zip(grads, parts)])
    shapes = [(g.shape[0] // (A * B), g.shape[1]) for g in grads]
    hbm = pl.BlockSpec(memory_space=pl.ANY)
    remote = dict(collective_id=cid, has_side_effects=True) if grads else {}
    cube = lambda a, b: pl.BlockSpec((n, a, b), lambda s: (s, 0, 0))
    return pl.pallas_call(
        functools.partial(attend_back_kernel, A, B, n, patches, slots, cuts, len(grads)),
        grid=(examples // n,),
        out_shape=[
            jax.ShapeDtypeStruct(act.shape, f32),
            jax.ShapeDtypeStruct((examples, slots, width), bf16),
            jax.ShapeDtypeStruct(wqkv.shape, bf16),
            jax.ShapeDtypeStruct(wout.shape, bf16),
            jax.ShapeDtypeStruct(wp.shape, bf16),
            jax.ShapeDtypeStruct((8, width), f32),
            jax.ShapeDtypeStruct((8, 3 * width), f32),
        ]
        + [jax.ShapeDtypeStruct(s, f32) for s in shapes],
        in_specs=[pl.BlockSpec(memory_space=pltpu.SMEM), blk(width), blk(width), blk(width), blk(3 * width), blk(width), cube(PATCH_PAD, channels)]
        + [whole(w.shape) for w in (wp, wqkv, wout, params)]
        + [hbm] * len(grads),
        out_specs=[cube(PATCH_PAD, channels), cube(slots, width)] + [whole(s) for s in (wqkv.shape, wout.shape, wp.shape, (8, width), (8, 3 * width), *shapes)],
        scratch_shapes=[pltpu.VMEM(wqkv.shape, f32), pltpu.VMEM(wout.shape, f32), pltpu.VMEM(wp.shape, f32), pltpu.VMEM((n * rows, width), bf16), pltpu.VMEM((n * rows, 3 * width), bf16)]
        + (scatter_buffers(A, B, cuts, shapes) + scatter_sems(A, B, len(cuts)) if grads else []),
        compiler_params=pltpu.CompilerParams(vmem_limit_bytes=62 << 20, **remote),
        name="attend_back",
    )(lengths, dx2, x, h1, qkv, o, act, wp, wqkv, wout, params, *[split_rows(A, B, g) for g in grads])


class Total:
    def __init__(self, pc, j, send, recv, ssem, rsem):
        self.pc, self.send, self.recv = pc, send.at[j], recv.at[j]
        self.ssem, self.rsem = ssem.at[j], rsem.at[j]
        groups = [pc.bpeers, pc.dpeers]
        self.groups, at = [], 0
        for g in groups:
            self.groups.append([(at + k, dev) for k, dev in enumerate(g)])
            at += len(g)

    def copy(self, step, k, dev):
        return rcopy(self.send.at[step], self.recv.at[k], self.ssem.at[k], self.rsem.at[k], dev)

    def put(self, step, v):
        self.send[step] = v
        for k, dev in self.groups[step]:
            self.copy(step, k, dev).start()

    def take(self, step):
        v = self.send[step]
        for k, dev in self.groups[step]:
            self.copy(step, k, dev).wait_recv()
            v = v + self.recv[k]
        return v

    def begin(self, v):
        self.put(0, v)

    def middle(self):
        self.put(1, self.take(0))

    def end(self):
        return self.take(1)

    def drain(self):
        for step in range(2):
            for k, dev in self.groups[step]:
                self.copy(step, k, dev).wait_send()


def total_scratch(A, B, count, shape):
    peers = (B - 1) + (A - 1)
    return [pltpu.VMEM((count, 2) + shape, f32), pltpu.VMEM((count, peers) + shape, f32), DMA((count, peers)), DMA((count, peers))]


def tile_rows(rows):
    return -(-rows // 16) * 16


def together(rows):
    n = 1
    while n * rows % 16:
        n += 1
    return n


def unpack(src, dst, rows):
    padded, cols = src.shape[-2:]
    shards = dst.shape[0] // rows
    flat = src[...].reshape(shards * padded, cols)
    if padded == rows:
        dst[...] = flat
        return
    n = together(rows)
    pick = turn_rows((n * rows, n * padded), rows, padded)
    for t in range(shards // n):
        dst[t * n * rows : (t + 1) * n * rows] = dot(pick, flat[t * n * padded : (t + 1) * n * padded]).astype(bf16)


def turn_rows(shape, rows, padded):
    out, pos = iota(shape, 0), iota(shape, 1)
    shard = jnp.floor((out.astype(f32) + 0.5) * (1.0 / rows)).astype(jnp.int32)
    return jnp.where(pos == out + shard * (padded - rows), 1.0, 0.0).astype(bf16)


def pack(src, dst, rows):
    padded, cols = dst.shape[-2:]
    shards = src.shape[0] // rows
    if padded == rows:
        dst[...] = src.reshape(dst.shape)
        return
    n = together(rows)
    shape = (n * padded, n * rows)
    out, pos = iota(shape, 0), iota(shape, 1)
    shard = jnp.floor((out.astype(f32) + 0.5) * (1.0 / padded)).astype(jnp.int32)
    pick = jnp.where((pos == out - shard * (padded - rows)) & (out - shard * padded < rows), 1.0, 0.0).astype(bf16)
    parts = [dot(pick, src[t * n * rows : (t + 1) * n * rows]).astype(bf16) for t in range(shards // n)]
    dst[...] = jnp.concatenate(parts, 0).reshape(dst.shape)


def unpack_vectors(tab, out, sizes):
    shards = tab.shape[0] * tab.shape[1] * tab.shape[2] * tab.shape[3]
    flat = tab[...].reshape(shards, tab.shape[-2], tab.shape[-1])[:, 0, :]
    out[...] = jnp.zeros(out.shape, f32)
    for v, n in enumerate(sizes):
        wide = n * shards
        lane = iota((128, wide), 1)
        block = jnp.floor((lane.astype(f32) + 0.5) * (1.0 / n)).astype(jnp.int32)
        spot = jnp.where(iota((128, wide), 0) == lane - block * n, 1.0, 0.0).astype(bf16)
        rows = dot(flat[:, 128 * v : 128 * (v + 1)].astype(bf16), spot)
        owner = jnp.where(iota((shards, wide), 0) == block[:shards] if shards <= 128 else block, rows, 0.0)
        out[v : v + 1, :wide] = colsum(owner)


def make_taps(taps, grid):
    places = grid * grid
    i, j = iota((places, places), 0), iota((places, places), 1)
    col = i - grid * jnp.floor((i.astype(f32) + 0.5) * (1.0 / grid)).astype(jnp.int32)
    for t in range(9):
        dr, dc = t // 3 - 1, t % 3 - 1
        hit = (j == i + grid * dr + dc) & (col + dc >= 0) & (col + dc < grid)
        taps[t] = jnp.where(hit, 1.0, 0.0).astype(bf16)


def rows_of(vectors):
    rows = []
    for v in vectors:
        rows += [v[:, q : q + 256] for q in range(0, v.shape[1], 256)]
    if len(rows) < 8:
        rows.append(jnp.zeros((8 - len(rows), 256), f32))
    return jnp.concatenate(rows, 0)


def vectors_of(block, width):
    per = width // 256
    take = lambda k: jnp.concatenate([block[k * per + q : k * per + q + 1] for q in range(per)], 1)
    return take(0), take(1)


VECTORS = ("bn1_gain", "bn1_bias", "bn2_gain", "bn2_bias", "bn3_gain", "bn3_bias", "b_patch", "ln1_gain", "ln1_bias", "b_q", "b_v", "b_out", "ln2_gain", "ln2_bias", "b_up", "b_down")


def moments(s1, s2, total_rows, gain, bias):
    mean = s1 / total_rows
    inv = lax.rsqrt(s2 / total_rows - mean * mean + bn_eps)
    return mean, inv


def stem_kernel(A, B, items, n_mats, sizes, shard_rows, total_rows, *refs):
    n_vec = len(sizes)
    feats, vecs, refs = refs[0], refs[1 : 1 + n_vec], refs[1 + n_vec :]
    near, far_in, refs = refs[:3], refs[3 : n_mats - 1], refs[n_mats - 1 :]
    n_far = n_mats - 4
    far, refs = refs[:n_far], refs[n_far:]
    (act_h, r_h, c_h, e_h, params, stats, w_red, w_conv, w_exp), refs = refs[:9], refs[9:]
    (act, r_o, c_o, e_o, out_sems), refs = refs[:5], refs[5:]
    (p_red, tab, p_conv, p_exp, taps, cols), refs = refs[:6], refs[6:]
    mine, refs = refs[:4], refs[4:]
    sums, sems = refs[:4], refs[4:]
    pc = Place(A, B)
    for src, dst in zip(near, (mine[0], mine[2], mine[3])):
        dst[...] = dot(jnp.where(iota((dst.shape[0], src.shape[0]), 0) == iota((dst.shape[0], src.shape[0]), 1), 1.0, 0.0).astype(bf16), src[...]).astype(bf16)
    mine[1][...] = jnp.zeros(mine[1].shape, f32)
    for v, ref in enumerate(vecs):
        mine[1][:, 128 * v : 128 * v + sizes[v]] = ref[...].astype(f32)
    shards = [*mine, *far_in]
    pc.greet()
    dsts = [p_red, tab, p_conv, p_exp, *far]
    moves = [GatherItem(pc, j, c, order, shards[i], dsts[i], sems) for j, (i, c, order) in enumerate(items)]
    adds = [Total(pc, j, *sums) for j in range(3)]
    examples, patches, channels = feats.shape
    grid = GRID
    vec = lambda v, width: params[v : v + 1, :width]

    def each(fn, width):
        zero = jnp.zeros((1, width), f32)

        def body(i, s):
            v = fn(i)
            return s[0] + colsum(v), s[1] + colsum(v * v)

        return lax.fori_loop(0, examples, body, (zero, zero), unroll=3)

    def norm(v, j, width):
        return (v - stats[2 * j : 2 * j + 1, :width]) * stats[2 * j + 1 : 2 * j + 2, :width] * vec(2 * j, width) + vec(2 * j + 1, width)

    def keep(j, width):
        s1, s2 = vectors_of(adds[j].end(), width)
        mean, inv = moments(s1, s2, total_rows, None, None)
        stats[2 * j : 2 * j + 1, :width] = mean
        stats[2 * j + 1 : 2 * j + 2, :width] = inv

    narrow = r_o.shape[2]

    def first():
        moves[0].arrived()
        unpack(p_red, w_red, shard_rows[0])

        def one(i):
            v = dot(feats[i], w_red[...])
            r_o[i] = v
            return v

        adds[0].begin(rows_of(each(one, narrow)))

    def vectors():
        moves[1].arrived()
        unpack_vectors(tab, params, sizes)

    def second():
        keep(0, narrow)

        def one(i):
            ra = smooth(norm(r_o[i], 0, narrow)).astype(bf16)
            for t in range(9):
                cols[:, t * narrow : (t + 1) * narrow] = dot(taps[t], ra).astype(bf16)
            v = dot(cols[...], w_conv[...])
            c_o[i] = v
            return v

        adds[1].begin(rows_of(each(one, narrow)))

    def third():
        keep(1, narrow)

        def one(i):
            ca = smooth(norm(c_o[i], 1, narrow)).astype(bf16)
            v = dot(ca, w_exp[...])
            e_o[i] = v
            return v

        adds[2].begin(rows_of(each(one, channels)))

    def act_copy(i):
        return pltpu.make_async_copy(act.at[i], act_h.at[i], out_sems.at[3 + i])

    def fourth():
        keep(2, channels)
        wide = spread(act.shape[1], patches, patches)

        def body(i, _):
            v = norm(e_o[i], 2, channels) + feats[i].astype(f32)
            act[i] = dot(wide, smooth(v).astype(bf16)).astype(bf16)
            act_copy(i).start()
            return 0

        lax.fori_loop(0, examples, body, 0, unroll=3)

    saved = [pltpu.make_async_copy(v, h, out_sems.at[k]) for k, (v, h) in enumerate(((r_o, r_h), (c_o, c_h), (e_o, e_h)))]
    make_taps(taps, grid)
    stats[...] = jnp.zeros(stats.shape, f32)

    def ready_conv():
        moves[2].arrived()
        unpack(p_conv, w_conv, shard_rows[1])
        vectors()

    def ready_exp():
        moves[3].arrived()
        unpack(p_exp, w_exp, shard_rows[2])

    hooks = {8: [first], 10: [adds[0].middle, saved[0].start, ready_conv], 12: [second], 14: [adds[1].middle, saved[1].start, ready_exp], 16: [third], 18: [adds[2].middle, saved[2].start], 20: [fourth]}
    wave(moves, (0, 2, 4, 6), ["start", "second", "third", "fourth"], hooks)
    for m in moves:
        m.arrived()
    for m in moves:
        m.drain()
    for t in adds:
        t.drain()
    for t in saved:
        t.wait()
    lax.fori_loop(0, examples, lambda i, _: (act_copy(i).wait(), 0)[1], 0)


def stem_forward(A, B, feats, vecs, mats, pad_rows, parts, cid):
    A2, Z, count = A // 2, B // 2, A * B
    examples, patches, channels = feats.shape
    near, far = mats[:3], mats[3:]
    sizes = [v.shape[0] for v in vecs]
    shard_rows = [m.shape[0] for m in near]
    pads = [jax.ShapeDtypeStruct((tile_rows(m.shape[0]), m.shape[1]), bf16) for m in near]
    shards = [pads[0], jax.ShapeDtypeStruct((1, 128 * len(vecs)), f32), pads[1], pads[2], *far]
    items = cut([(s.shape[1], q) for s, q in zip(shards, (1, 1, 1, 1) + parts)])
    shape = lambda s: (A2, 2, Z, 2) + s.shape
    narrow = near[0].shape[1]
    hbm, vm = pl.BlockSpec(memory_space=pl.ANY), pl.BlockSpec(memory_space=pltpu.VMEM)
    full = [(m.shape[0] * count, m.shape[1]) for m in near]
    outs = pl.pallas_call(
        functools.partial(stem_kernel, A, B, items, len(shards), sizes, shard_rows, float(examples * count * patches)),
        out_shape=[jax.ShapeDtypeStruct(shape(s), s.dtype) for s in far]
        + [
            jax.ShapeDtypeStruct((examples, pad_rows, channels), bf16),
            jax.ShapeDtypeStruct((examples, patches, narrow), f32),
            jax.ShapeDtypeStruct((examples, patches, narrow), f32),
            jax.ShapeDtypeStruct((examples, patches, channels), f32),
            jax.ShapeDtypeStruct((16, sizes[13] * count), f32),
            jax.ShapeDtypeStruct((8, channels), f32),
        ]
        + [jax.ShapeDtypeStruct(s, bf16) for s in full],
        in_specs=[vm] * (1 + len(vecs) + 3) + [hbm] * len(far),
        out_specs=[hbm] * (len(far) + 4) + [vm] * 5,
        scratch_shapes=[
            pltpu.VMEM((examples, pad_rows, channels), bf16),
            pltpu.VMEM((examples, patches, narrow), f32),
            pltpu.VMEM((examples, patches, narrow), f32),
            pltpu.VMEM((examples, patches, channels), f32),
            DMA((3 + examples,)),
        ]
        + [pltpu.VMEM(shape(s), s.dtype) for s in shards[:4]]
        + [pltpu.VMEM((9, patches, patches), bf16), pltpu.VMEM((patches, full[1][0]), bf16)]
        + [pltpu.VMEM(s.shape, s.dtype) for s in shards[:4]]
        + total_scratch(A, B, 3, (8, 256))
        + gather_sems(A, B, len(items)),
        compiler_params=pltpu.CompilerParams(collective_id=cid, has_side_effects=True, vmem_limit_bytes=60 << 20),
        name="stem",
    )(feats, *[v[None] for v in vecs], *near, *far)
    return [g.reshape(-1, g.shape[-1]) for g in outs[: len(far)]], outs[len(far) :]


class Run:
    pass


class Written:
    def __init__(self, out):
        self.out = out

    def second(self):
        pass

    third = fourth = arrived = second


def stem_back_kernel(A, B, cuts, near_rows, total_rows, sizes, n_far, inside, *refs):
    (dact_h, feats_h, red_h, conv_h, expand_h, params, stats, w_red, w_conv, w_exp, small_f, small_b, small_a, small_q), refs = refs[:14], refs[14:]
    far, refs = refs[:n_far], refs[n_far:]
    (gfeats_h, shares), refs = refs[:2], refs[2:]
    far_out, near_out, refs = refs[:n_far], refs[n_far : n_far + 3], refs[n_far + 3 :]
    (dact, feats, expand, red, conv, gfeats, ex_sems, in_sems), refs = refs[:8], refs[8:]
    (ds_s, dy_s, ca_s, taps, gred, gconv, gexp, k_red, k_conv, k_exp), refs = refs[:10], refs[10:]
    sums, vsum, refs = refs[:4], refs[4:8], refs[8:]
    bufs, sems = refs[: 5 * len(cuts)], refs[5 * len(cuts) :]
    def load(k, i):
        src, dst = ((dact_h, dact), (feats_h, feats), (expand_h, expand))[k]
        return pltpu.make_async_copy(src.at[i], dst.at[i], ex_sems.at[k, i])

    def leave_feats(i):
        return pltpu.make_async_copy(gfeats.at[i], gfeats_h.at[i], ex_sems.at[3, i])

    load_conv, load_red = (pltpu.make_async_copy(a, b, in_sems.at[k]) for k, (a, b) in enumerate(((conv_h, conv), (red_h, red))))
    for i in range(feats.shape[0]):
        for k in range(3):
            load(k, i).start()
    load_conv.start()
    load_red.start()
    pc = Place(A, B)
    pc.greet()
    moves = scatter_items(pc, cuts, [*far, k_exp, k_conv, k_red], [*far_out, near_out[2], near_out[1], near_out[0]], bufs, sems)
    big, late = (moves[:-3], moves[-3:]) if inside else (moves, [Written(o) for o in (near_out[2], near_out[1], near_out[0])])
    m_exp, m_conv, m_red = late

    def leave(move, grad, packed, rows):
        if inside:
            pack(grad[...].astype(bf16), packed, rows)
            move.start()
        else:
            move.out[...] = grad[...].astype(bf16)

    adds = [Total(pc, j, *sums) for j in range(3)]
    vec_sum = Total(pc, 0, *vsum)
    examples, patches, channels = feats.shape
    narrow, width = red.shape[2], small_a.shape[1]
    for m in big:
        m.start()
    rows = [small_a[3:4], small_a[0:1], small_a[1:2], small_q[0:1, :width], small_q[0:1, 2 * width :], small_a[2:3], small_f[1:2], small_f[2:3]]
    rows += [small_b[:, q : q + width] for q in range(0, small_b.shape[1], width)]
    rows += [small_f[0:1]]
    vec_sum.begin(jnp.concatenate(rows + [jnp.zeros((16 - len(rows), width), f32)], 0))
    make_taps(taps, GRID)

    def hat_of(ref, i, j, w):
        return (ref[i] - stats[2 * j : 2 * j + 1, :w]) * stats[2 * j + 1 : 2 * j + 2, :w]

    def point(hat, j, w):
        return hat * params[2 * j : 2 * j + 1, :w] + params[2 * j + 1 : 2 * j + 2, :w]

    def each(fn, w):
        zero = jnp.zeros((1, w), f32)

        def body(i, s):
            dy, hat = fn(i)
            return s[0] + colsum(dy), s[1] + colsum(dy * hat)

        return lax.fori_loop(0, examples, body, (zero, zero), unroll=3)

    def norm_back(dy, hat, j, w, totals):
        scale = stats[2 * j + 1 : 2 * j + 2, :w] * params[2 * j : 2 * j + 1, :w]
        return (scale * (dy - totals[0] * (1.0 / total_rows) - hat * (totals[1] * (1.0 / total_rows)))).astype(bf16)

    run = Run()

    def fifth():
        def one(i):
            for k in range(3):
                load(k, i).wait()
            hat = hat_of(expand, i, 2, channels)
            _, slope = smooth_both(point(hat, 2, channels) + feats[i].astype(f32))
            dy = dact[i, :patches] * slope
            ds_s[i] = dy
            return dy, hat

        adds[2].begin(rows_of(each(one, channels)))

    def sixth():
        load_conv.wait()
        run.t3 = vectors_of(adds[2].end(), channels)
        gexp[...] = jnp.zeros(gexp.shape, f32)

        def one(i):
            de = norm_back(ds_s[i], hat_of(expand, i, 2, channels), 2, channels, run.t3)
            hat = hat_of(conv, i, 1, narrow)
            ca, slope = smooth_both(point(hat, 1, narrow))
            gexp[...] += dot_tn(ca.astype(bf16), de)
            dy = dot_nt(de, w_exp[...]) * slope
            dy_s[i] = dy
            return dy, hat

        adds[1].begin(rows_of(each(one, narrow)))
        leave(m_exp, gexp, k_exp, near_rows[2])

    def seventh():
        load_red.wait()
        run.t2 = vectors_of(adds[1].end(), narrow)
        gconv[...] = jnp.zeros(gconv.shape, f32)

        def one(i):
            dc = norm_back(dy_s[i], hat_of(conv, i, 1, narrow), 1, narrow, run.t2)
            hat = hat_of(red, i, 0, narrow)
            ra, slope = smooth_both(point(hat, 0, narrow))
            turned = ra.T.astype(bf16)
            dra = jnp.zeros((patches, narrow), f32)
            for t in range(9):
                moved = dot(taps[8 - t], dc).astype(bf16)
                at = slice(t * narrow, (t + 1) * narrow)
                gconv[at] += dot(turned, moved)
                dra = dra + dot_nt(moved, w_conv[at])
            dy = dra * slope
            dy_s[i] = dy
            return dy, hat

        adds[0].begin(rows_of(each(one, narrow)))
        leave(m_conv, gconv, k_conv, near_rows[1])

    def eighth():
        run.t1 = vectors_of(adds[0].end(), narrow)
        gred[...] = jnp.zeros(gred.shape, f32)

        def body(i, _):
            dr = norm_back(dy_s[i], hat_of(red, i, 0, narrow), 0, narrow, run.t1)
            ca_s[i] = dr
            gred[...] += dot_tn(feats[i], dr)
            return 0

        lax.fori_loop(0, examples, body, 0)
        leave(m_red, gred, k_red, near_rows[0])

    def ninth(lo, hi):
        def body(i, _):
            gfeats[i] = (ds_s[i] + dot_nt(ca_s[i], w_red[...])).astype(bf16)
            leave_feats(i).start()
            return 0

        lax.fori_loop(lo, hi, body, 0)

    def finish():
        v = vec_sum.end()
        me = pc.a * B + pc.b
        one = lambda k: v[k : k + 1]
        rows = [run.t1[1], run.t1[0], run.t2[1], run.t2[0], run.t3[1], run.t3[0], one(0), one(1), one(2), jnp.concatenate([one(3), one(4)], 1)]
        rows += [one(5), one(6), one(7), jnp.concatenate([one(k) for k in range(8, 8 + small_b.shape[1] // width)], 1), one(8 + small_b.shape[1] // width)]
        for k, row in enumerate(rows):
            wide = row.shape[1]
            turn = lax.rem(wide - me * sizes[k], wide)
            shares[k : k + 1] = pltpu.roll(jnp.broadcast_to(row, (8, wide)), turn, 1)[0:1, :128]
        shares[15:16] = jnp.zeros((1, 128), f32)

    queue = wave_stages(big, (0, 2, 4, 6), ["second", "third", "fourth", "arrived"])

    def advance(count):
        for _ in range(min(count, len(queue))):
            queue.pop(0)()

    fifth()
    advance(2)
    adds[2].middle()
    vec_sum.middle()
    advance(4)
    sixth()
    advance(2)
    adds[1].middle()
    m_exp.second()
    advance(4)
    seventh()
    m_exp.third()
    advance(2)
    adds[0].middle()
    m_conv.second()
    m_exp.fourth()
    advance(4)
    eighth()
    m_conv.third()
    advance(2)
    m_red.second()
    ninth(0, examples // 2)
    m_conv.fourth()
    m_red.third()
    advance(2)
    ninth(examples // 2, examples)
    m_red.fourth()
    finish()
    advance(len(queue))
    m_exp.arrived()
    m_conv.arrived()
    m_red.arrived()
    for m in moves:
        m.drain()
    for s in adds + [vec_sum]:
        s.drain()
    lax.fori_loop(0, examples, lambda i, _: (leave_feats(i).wait(), 0)[1], 0)


def stem_backward(A, B, dact, feats, red, conv, expand, params, stats, w_red, w_conv, w_exp, smalls, sizes, grads, parts, inside, cid):
    A2, Z, count = A // 2, B // 2, A * B
    examples, patches, channels = feats.shape
    narrow = red.shape[2]
    near = [w_red, w_conv, w_exp]
    near_rows = [w.shape[0] // count for w in near]
    packed = [(tile_rows(r), w.shape[1]) for r, w in zip(near_rows, near)]
    cuts = cut([(g.shape[1], q) for g, q in zip(grads, parts)] + [(p[1], 1) for p in reversed(packed) if inside])
    shapes = [(g.shape[0] // count, g.shape[1]) for g in grads] + packed[::-1]
    outs = [jax.ShapeDtypeStruct(feats.shape, bf16), jax.ShapeDtypeStruct((16, 128), f32)]
    outs += [jax.ShapeDtypeStruct(s, f32) for s in shapes[: len(grads)]]
    outs += [jax.ShapeDtypeStruct((r, w.shape[1]), f32) if inside else jax.ShapeDtypeStruct(w.shape, bf16) for r, w in zip(near_rows, near)]
    hbm, vm = pl.BlockSpec(memory_space=pl.ANY), pl.BlockSpec(memory_space=pltpu.VMEM)
    lead = (A2, 2, Z, 2)
    return pl.pallas_call(
        functools.partial(stem_back_kernel, A, B, cuts, near_rows, float(examples * count * patches), sizes, len(grads), inside),
        out_shape=outs,
        in_specs=[hbm] * 5 + [vm] * 9 + [hbm] * len(grads),
        out_specs=[hbm] + [vm] * (len(outs) - 1),
        scratch_shapes=[pltpu.VMEM(a.shape, a.dtype) for a in (dact, feats, expand, red, conv, feats)]
        + [
            DMA((4, examples)),
            DMA((2,)),
            pltpu.VMEM((examples, patches, channels), f32),
            pltpu.VMEM((examples, patches, narrow), f32),
            pltpu.VMEM((examples, patches, narrow), bf16),
            pltpu.VMEM((9, patches, patches), bf16),
        ]
        + [pltpu.VMEM(w.shape, f32) for w in near]
        + [pltpu.VMEM(lead + p if inside else (16, 128), bf16) for p in packed]
        + total_scratch(A, B, 3, (8, 256))
        + total_scratch(A, B, 1, (16, smalls[2].shape[1]))
        + (scatter_buffers(A, B, cuts, shapes) + scatter_sems(A, B, len(cuts)) if cuts else []),
        compiler_params=pltpu.CompilerParams(collective_id=cid, has_side_effects=True, vmem_limit_bytes=62 << 20),
        name="stem_back",
    )(dact, feats, red, conv, expand, params, stats, w_red, w_conv, w_exp, *smalls, *[split_rows(A, B, g) for g in grads])


def finish_kernel(n, *refs):
    shares, ins, outs, refs = refs[0], refs[1 : 1 + n], refs[1 + n : 1 + 2 * n], refs[1 + 2 * n :]
    vecs, bufs, sems = refs[: -n - 1], refs[-n - 1 : -1], refs[-1]
    loads = [pltpu.make_async_copy(a, b, sems.at[0, k]) for k, (a, b) in enumerate(zip(ins, bufs))]
    stores = [pltpu.make_async_copy(a, b, sems.at[1, k]) for k, (a, b) in enumerate(zip(bufs, outs))]
    for c in loads:
        c.start()
    for v, ref in enumerate(vecs):
        ref[...] = shares[v, : ref.shape[0]]
    for load, store in zip(loads, stores):
        load.wait()
        store.start()
    for c in stores:
        c.wait()


def finish(shares, sizes, arrays):
    hbm, vm = pl.BlockSpec(memory_space=pl.ANY), pl.BlockSpec(memory_space=pltpu.VMEM)
    n = len(arrays)
    outs = pl.pallas_call(
        functools.partial(finish_kernel, n),
        out_shape=[jax.ShapeDtypeStruct(a.shape, a.dtype) for a in arrays] + [jax.ShapeDtypeStruct((s,), f32) for s in sizes],
        in_specs=[vm] + [hbm] * n,
        out_specs=[hbm] * n + [vm] * len(sizes),
        scratch_shapes=[pltpu.VMEM(a.shape, a.dtype) for a in arrays] + [DMA((2, n))],
        compiler_params=pltpu.CompilerParams(vmem_limit_bytes=60 << 20),
        name="finish",
    )(shares, *arrays)
    return outs[:n], outs[n:]


AXES = ("dp", "fsdp")


def local(
    feats, text, lengths, cotangent,
    w_red, bn1_gain, bn1_bias, w_conv, bn2_gain, bn2_bias, w_exp, bn3_gain, bn3_bias, w_patch, b_patch,
    ln1_gain, ln1_bias, w_qkv, b_qv, w_out, b_out, ln2_gain, ln2_bias, w_up, b_up, w_down, b_down,
):
    A, B = lax.axis_size("dp"), lax.axis_size("fsdp")
    vecs = (bn1_gain, bn1_bias, bn2_gain, bn2_bias, bn3_gain, bn3_bias, b_patch, ln1_gain, ln1_bias, b_qv, b_out, ln2_gain, ln2_bias, b_up, b_down)
    sizes = [v.shape[0] for v in vecs]
    patches, slots = feats.shape[1], text.shape[1]
    far, near = stem_forward(A, B, feats, vecs, (w_red, w_conv, w_exp, w_patch, w_qkv, w_out, w_up, w_down), PATCH_PAD, (1, 3, 1, 4, 3), 0)
    full_patch, full_qkv, full_out, full_up, full_down = far
    act, red, conv, expand, params, stats, full_red, full_conv, full_exp = near
    x, h1, qkv, o, x2, h2 = attend(lengths, act, text, full_patch, full_qkv, full_out, params, patches, 2)
    output, dx2, g_up, g_down, small_b, small_f = ffn(lengths, h2, x2, cotangent, full_up, full_down, params, patches, 2, 512)
    inside = w_qkv.shape[0] >= 16
    first = [g_up, g_down] if inside else []
    dact, grad_text, g_qkv, g_out, g_patch, small_a, small_q, *sums = attend_back(
        A, B, lengths, dx2, x, h1, qkv, o, act, full_patch, full_qkv, full_out, params, first, (4, 3)[: len(first)], slots, patches, 1, 1
    )
    second = [g_qkv, g_out, g_patch] if inside else []
    grad_feats, shares, *more = stem_backward(
        A, B, dact, feats, red, conv, expand, params, stats, full_red, full_conv, full_exp, (small_f, small_b, small_a, small_q), sizes, second, (3, 1, 1)[: len(second)], inside, 2
    )
    if not inside:
        sums = [lax.psum_scatter(g.astype(f32), AXES, scatter_dimension=0, tiled=True) for g in (g_up, g_down)]
        more = [lax.psum_scatter(g.astype(f32), AXES, scatter_dimension=0, tiled=True) for g in (g_qkv, g_out, g_patch, *more)]
    (grad_feats, grad_text, s_up, s_down, s_qkv, s_out, s_patch, s_red, s_conv, s_exp), vectors = finish(shares, sizes, [grad_feats, grad_text, *sums, *more])
    (s_bn1_gain, s_bn1_bias, s_bn2_gain, s_bn2_bias, s_bn3_gain, s_bn3_bias, s_b_patch, s_ln1_gain, s_ln1_bias, s_b_qv, s_b_out, s_ln2_gain, s_ln2_bias, s_b_up, s_b_down) = vectors
    return (
        output, grad_feats, grad_text,
        s_red, s_bn1_gain, s_bn1_bias, s_conv, s_bn2_gain, s_bn2_bias, s_exp, s_bn3_gain, s_bn3_bias, s_patch, s_b_patch,
        s_ln1_gain, s_ln1_bias, s_qkv, s_b_qv, s_out, s_b_out, s_ln2_gain, s_ln2_bias, s_up, s_b_up, s_down, s_b_down,
    )


def solution(mesh):
    every = ("dp", "fsdp")
    v, m, t = P(every), P(every, None), P(every, None, None)
    weights = (m, v, v, m, v, v, m, v, v, m, v, v, v, m, v, m, v, v, v, m, v, m, v)
    return jax.shard_map(local, mesh=mesh, in_specs=(t, t, v, t) + weights, out_specs=(t, t, t) + weights, check_vma=False)
```

```python
import functools

import jax
import jax.numpy as jnp
from jax import lax
from jax.experimental import pallas as pl
from jax.experimental.pallas import tpu as pltpu
from jax.sharding import PartitionSpec as P
MESH = pl.DeviceIdType.MESH
DMA = pltpu.SemaphoreType.DMA


def rcopy(src, dst, send, recv, dev):
    return pltpu.make_async_remote_copy(
        src_ref=src, dst_ref=dst, send_sem=send, recv_sem=recv, device_id=dev, device_id_type=MESH
    )


class Place:
    def __init__(self, A, B):
        self.A, self.B, self.A2, self.Z = A, B, A // 2, B // 2
        a, b = lax.axis_index("dp"), lax.axis_index("fsdp")
        self.a, self.b = a, b
        self.y, self.x = a // 2, lax.rem(a, 2)
        self.z, self.c = b // 2, lax.rem(b, 2)
        self.zs = [lax.rem(self.z + k, self.Z) for k in range(1, self.Z)]
        self.ys = [lax.rem(self.y + k, self.A2) for k in range(1, self.A2)]
        self.zfrom = [lax.rem(self.z + self.Z - k, self.Z) for k in range(1, self.Z)]
        self.yfrom = [lax.rem(self.y + self.A2 - k, self.A2) for k in range(1, self.A2)]
        self.me = (a, b)
        self.core = (a, self.z * 2 + 1 - self.c)
        self.xpeer = (self.y * 2 + 1 - self.x, b)
        self.c1, self.x1 = 1 - self.c, 1 - self.x
        self.dpeers = [(lax.rem(a + k, A), b) for k in range(1, A)]
        self.zpeers = [(a, zz * 2 + self.c) for zz in self.zs]
        self.ypeers = [(yy * 2 + self.x, b) for yy in self.ys]

        self.bpeers = [(a, lax.rem(b + k, B)) for k in range(1, B)]

    def greet(self, totals=True):
        peers = self.dpeers + self.bpeers if totals else self.zpeers + self.ypeers + [self.xpeer, self.core]
        bar = pltpu.get_barrier_semaphore()
        for p in peers:
            pl.semaphore_signal(bar, inc=1, device_id=p, device_id_type=MESH)
        pl.semaphore_wait(bar, len(peers))


class GatherItem:
    def __init__(self, pc, i, cols, order, src, out, sems):
        self.pc, self.order, self.src_ref, self.out = pc, order, src, out
        self.cols = slice(None) if cols is None else pl.ds(*cols)
        self.loc, self.s1, self.r1, self.s2, self.r2, self.s3, self.r3, self.sc, self.rc = [s.at[i] for s in sems]
        self.here = False
        p = pc
        every = slice(None)
        self.got2 = [(p.y, p.x1)] if order == 0 else [(yy, p.x) for yy in p.yfrom]
        self.got3 = [(yy, every) for yy in p.yfrom] if order == 0 else [(every, p.x1)]
        self.to2 = [p.xpeer] if order == 0 else p.ypeers
        self.to3 = p.ypeers if order == 0 else [p.xpeer]
        self.crossed = [(p.y, p.x)] + self.got2 + self.got3

    def src(self):
        return self.src_ref.at[:, self.cols]

    def block(self, y, x, z, c):
        return self.out.at[y, x, z, c, :, self.cols]

    def local(self):
        p = self.pc
        return pltpu.make_async_copy(self.src(), self.block(p.y, p.x, p.z, p.c), self.loc)

    def send1(self, k):
        p = self.pc
        return rcopy(self.src(), self.block(p.y, p.x, p.z, p.c), self.s1.at[k], self.r1.at[k], p.zpeers[k])

    def send2(self, k):
        p = self.pc
        col = self.block(p.y, p.x, slice(None), p.c)
        return rcopy(col, col, self.s2.at[k], self.r2.at[k], self.to2[k])

    def send3(self, k):
        p, every = self.pc, slice(None)
        blk = self.block(p.y, every, every, p.c) if self.order == 0 else self.block(every, p.x, every, p.c)
        return rcopy(blk, blk, self.s3.at[k], self.r3.at[k], self.to3[k])

    def cross(self, j, c):
        blk = self.block(*self.crossed[j], slice(None), c)
        return rcopy(blk, blk, self.sc.at[j], self.rc.at[j], self.pc.core)

    def wait(self, got, send, recv):
        rcopy(got, got, send, recv, self.pc.me).wait_recv()

    def start(self):
        self.local().start()
        for k in range(len(self.pc.zpeers)):
            self.send1(k).start()

    def second(self):
        p = self.pc
        self.local().wait()
        for k, zz in enumerate(p.zfrom):
            self.wait(self.block(p.y, p.x, zz, p.c), self.s1.at[k], self.r1.at[k])
        for k in range(len(self.to2)):
            self.send2(k).start()
        self.cross(0, p.c).start()

    def third(self):
        p = self.pc
        for k, (yy, xx) in enumerate(self.got2):
            self.wait(self.block(yy, xx, slice(None), p.c), self.s2.at[k], self.r2.at[k])
        for k in range(len(self.to3)):
            self.send3(k).start()
        for k in range(len(self.got2)):
            self.cross(1 + k, p.c).start()

    def fourth(self):
        p = self.pc
        for k, (yy, xx) in enumerate(self.got3):
            self.wait(self.block(yy, xx, slice(None), p.c), self.s3.at[k], self.r3.at[k])
            self.cross(1 + len(self.got2) + k, p.c).start()

    def arrived(self):
        if self.here:
            return
        self.here = True
        for j in range(len(self.crossed)):
            self.cross(j, self.pc.c1).wait_recv()

    def drain(self):
        for k in range(len(self.pc.zpeers)):
            self.send1(k).wait_send()
        for k in range(len(self.to2)):
            self.send2(k).wait_send()
        for k in range(len(self.to3)):
            self.send3(k).wait_send()
        for j in range(len(self.crossed)):
            self.cross(j, self.pc.c).wait_send()


def gather_sems(A, B, n):
    A2, Z = A // 2, B // 2
    m = max(A2 - 1, 1)
    return [DMA((n,)), DMA((n, Z - 1)), DMA((n, Z - 1)), DMA((n, m)), DMA((n, m)), DMA((n, m)), DMA((n, m)), DMA((n, A2 + 1)), DMA((n, A2 + 1))]


def wave(items, lags, stages, hooks=None):
    hooks = hooks or {}
    last = max([len(items) + lags[-1]] + [t + 1 for t in hooks])
    for t in range(last):
        for lag, stage in zip(reversed(lags), reversed(stages)):
            if 0 <= t - lag < len(items):
                getattr(items[t - lag], stage)()
        for hook in hooks.get(t, ()):
            hook()


def wave_stages(items, lags, stages):
    out = []
    for t in range(len(items) + lags[-1]):
        for lag, stage in zip(reversed(lags), reversed(stages)):
            if 0 <= t - lag < len(items):
                out.append(getattr(items[t - lag], stage))
    return out


def cut(widths_parts):
    items, order = [], 0
    for i, (width, parts) in enumerate(widths_parts):
        for q in range(parts):
            items.append((i, None if parts == 1 else (q * (width // parts), width // parts), order))
            order = 1 - order
    return items


class ScatterItem:
    def __init__(self, pc, i, order, src, out, own, r0, r1, r2, r3, sems, cols=None):
        self.pc, self.order, self.src, self.out = pc, order, src, out
        self.cols = slice(None) if cols is None else pl.ds(*cols)
        self.own, self.r0, self.r1, self.r2, self.r3 = own, r0, r1, r2, r3
        self.loc, self.s0, self.q0, self.s1, self.q1, self.s2, self.q2, self.s3, self.q3 = [s.at[i] for s in sems]
        self.sends = []

    def go(self, copy):
        copy().start()
        self.sends.append(copy)

    def start(self):
        p = self.pc
        self.go(lambda: rcopy(self.src.at[:, :, :, p.c1, :, self.cols], self.r0, self.s0, self.q0, p.core))
        self.local().start()

    def local(self):
        return pltpu.make_async_copy(self.src.at[:, :, :, self.pc.c, :, self.cols], self.own, self.loc)

    def add(self, dst, others, lead):
        total = 1
        for d in lead:
            total *= d

        def body(t, _):
            idx, rest = [], t
            for d in reversed(lead):
                idx.append(lax.rem(rest, d))
                rest = rest // d
            idx = tuple(reversed(idx))
            v = dst[idx].astype(jnp.float32)
            for o in others:
                v = v + o[idx].astype(jnp.float32)
            dst[idx] = v.astype(jnp.bfloat16)
            return 0

        lax.fori_loop(0, total, body, 0)

    def second(self):
        p = self.pc
        self.local().wait()
        rcopy(self.r0, self.r0, self.s0, self.q0, p.me).wait_recv()
        self.add(self.own, [self.r0], (p.A2, 2, p.Z))
        if self.order == 0:
            self.go(lambda: rcopy(self.own.at[:, p.x1], self.r1.at[0], self.s1.at[0], self.q1.at[0], p.xpeer))
        else:
            for k, yy in enumerate(p.ys):
                self.go(lambda k=k, yy=yy: rcopy(self.own.at[yy], self.r1.at[k], self.s1.at[k], self.q1.at[k], p.ypeers[k]))

    def third(self):
        p = self.pc
        n1 = 1 if self.order == 0 else p.A2 - 1
        for k in range(n1):
            rcopy(self.r1.at[k], self.r1.at[k], self.s1.at[k], self.q1.at[k], p.me).wait_recv()
        mine = self.own.at[:, p.x] if self.order == 0 else self.own.at[p.y]
        self.add(mine, [self.r1.at[k] for k in range(n1)], (p.A2 if self.order == 0 else 2, p.Z))
        if self.order == 0:
            for k, yy in enumerate(p.ys):
                self.go(lambda k=k, yy=yy: rcopy(self.own.at[yy, p.x], self.r2.at[k], self.s2.at[k], self.q2.at[k], p.ypeers[k]))
        else:
            self.go(lambda: rcopy(self.own.at[p.y, p.x1], self.r2.at[0], self.s2.at[0], self.q2.at[0], p.xpeer))

    def fourth(self):
        p = self.pc
        n2 = p.A2 - 1 if self.order == 0 else 1
        for k in range(n2):
            rcopy(self.r2.at[k], self.r2.at[k], self.s2.at[k], self.q2.at[k], p.me).wait_recv()
        self.add(self.own.at[p.y, p.x], [self.r2.at[k] for k in range(n2)], (p.Z,))
        for k, zz in enumerate(p.zs):
            self.go(lambda k=k, zz=zz: rcopy(self.own.at[p.y, p.x, zz], self.r3.at[k], self.s3.at[k], self.q3.at[k], p.zpeers[k]))

    def arrived(self):
        p = self.pc
        for k in range(p.Z - 1):
            rcopy(self.r3.at[k], self.r3.at[k], self.s3.at[k], self.q3.at[k], p.me).wait_recv()
        v = self.own[p.y, p.x, p.z].astype(jnp.float32)
        for k in range(p.Z - 1):
            v = v + self.r3[k].astype(jnp.float32)
        self.out[:, self.cols] = v[: self.out.shape[0]]

    def drain(self):
        for copy in self.sends:
            copy().wait_send()


def scatter_sems(A, B, n):
    m, Z = max(A // 2 - 1, 1), B // 2
    return [DMA((n,)), DMA((n,)), DMA((n,)), DMA((n, m)), DMA((n, m)), DMA((n, m)), DMA((n, m)), DMA((n, Z - 1)), DMA((n, Z - 1))]


def scatter_scratch(A, B, shape, order):
    A2, Z = A // 2, B // 2
    n1 = (1, A2, Z) if order == 0 else (A2 - 1, 2, Z)
    n2 = (A2 - 1, Z) if order == 0 else (1, Z)
    return [pltpu.VMEM(s + shape, jnp.bfloat16) for s in ((A2, 2, Z), (A2, 2, Z), n1, n2, (Z - 1,))]


def scatter_items(pc, cuts, srcs, outs, bufs, sems, base=0):
    return [ScatterItem(pc, base + j, o, srcs[i], outs[i], *bufs[5 * j : 5 * j + 5], sems, cols) for j, (i, cols, o) in enumerate(cuts)]


def scatter_buffers(A, B, cuts, shapes):
    out = []
    for i, cols, order in cuts:
        out += scatter_scratch(A, B, (shapes[i][0], shapes[i][1] if cols is None else cols[1]), order)
    return out


def split_rows(A, B, g):
    return g.reshape((A // 2, 2, B // 2, 2, g.shape[0] // (A * B), g.shape[1]))


HEAD_DIM = 64
GRID = 14
ln_eps = 1e-06
bn_eps = 1e-05
gelu_coef = 0.7978845608028654
gelu_cube = gelu_coef * 0.044715
bf16, f32 = jnp.bfloat16, jnp.float32
PATCH_PAD = 208


def dot(left, right):
    return jnp.dot(left, right, preferred_element_type=f32)


def dot_nt(left, right):
    return lax.dot_general(left, right, (((1,), (1,)), ((), ())), preferred_element_type=f32)


def dot_tn(left, right):
    return lax.dot_general(left, right, (((0,), (0,)), ((), ())), preferred_element_type=f32)


def smooth(v):
    return (0.5 * v) * (1.0 + jnp.tanh(v * (gelu_coef + gelu_cube * (v * v))))


def smooth_both(v):
    sq = v * v
    t = jnp.tanh(v * (gelu_coef + gelu_cube * sq))
    half = 0.5 * v
    up = 1.0 + t
    return half * up, 0.5 * up + half * ((1.0 - t * t) * (gelu_coef + 3.0 * gelu_cube * sq))


def ln_parts(v):
    center = v - jnp.mean(v, -1, keepdims=True)
    inv = lax.rsqrt(jnp.mean(center * center, -1, keepdims=True) + ln_eps)
    return center * inv, inv


def ln_back(dy, hat, inv, gain):
    dh = dy * gain
    return inv * (dh - jnp.mean(dh, -1, keepdims=True) - hat * jnp.mean(dh * hat, -1, keepdims=True))


def colsum(v):
    return jnp.sum(v, 0, keepdims=True)


def iota(shape, dim):
    return lax.broadcasted_iota(jnp.int32, shape, dim)


def valid_of(position, length, patches):
    text = position - PATCH_PAD
    return jnp.where((position < patches) | ((text >= 0) & (text < length)), 1.0, 0.0).astype(f32)


def spread(rows, patches, seq):
    i, j = iota((rows, seq), 0), iota((rows, seq), 1)
    hit = ((i < patches) & (j == i)) | ((i >= PATCH_PAD) & (j == i - (PATCH_PAD - patches)))
    return jnp.where(hit, 1.0, 0.0).astype(bf16)


def gather_rows(seq, rows, patches):
    j, i = iota((seq, rows), 0), iota((seq, rows), 1)
    hit = ((i < patches) & (j == i)) | ((i >= PATCH_PAD) & (j == i - (PATCH_PAD - patches)))
    return jnp.where(hit, 1.0, 0.0).astype(bf16)


def lane_masks(width):
    lane = iota((1, 2 * width), 1)
    low = jnp.where(lane < width, 1.0, 0.0).astype(bf16)
    return low, (1.0 - low.astype(f32)).astype(bf16)


class Plan:
    def __init__(self, step, steps, points, stages):
        self.step, self.steps, self.points = step, steps, points
        total, n = steps * points, len(stages)
        self.due = [stages[n * q // total : n * (q + 1) // total] for q in range(total)]

    def __call__(self, point):
        for s in range(self.steps):
            stages = self.due[s * self.points + point]
            if stages:

                @pl.when(self.step == s)
                def _():
                    for stage in stages:
                        stage()


def attend_kernel(n, patches, len_ref, act, text, wp, wqkv, wout, params, x_o, h1_o, qkv_o, o_o, x2_o, h2_o):
    width = text.shape[2]
    slots = text.shape[1]
    rows = PATCH_PAD + slots
    step = pl.program_id(0)
    lows = lane_masks(HEAD_DIM)
    bp, g1, b1, bo, g2, b2 = (params[v : v + 1, :width] for v in (6, 7, 8, 10, 11, 12))
    bqkv = jnp.concatenate([params[9:10, :width], jnp.zeros((1, width), f32), params[9:10, width : 2 * width]], 1)
    patch = dot(act[...].reshape(n * PATCH_PAD, act.shape[2]), wp[...]) + bp
    for i in range(n):
        length = len_ref[step * n + i]
        keep = jnp.where(iota((slots, 1), 0) < length, 1.0, 0.0).astype(f32)
        x_o[i * rows : i * rows + PATCH_PAD] = patch[i * PATCH_PAD : (i + 1) * PATCH_PAD]
        x_o[i * rows + PATCH_PAD : (i + 1) * rows] = text[i].astype(f32) * keep
    hat, _ = ln_parts(x_o[...])
    h1 = (hat * g1 + b1).astype(bf16)
    h1_o[...] = h1
    qkv_o[...] = (dot(h1, wqkv[...]) + bqkv).astype(bf16)
    for i in range(n):
        at = slice(i * rows, (i + 1) * rows)
        bias = jnp.where(valid_of(iota((1, rows), 1), len_ref[step * n + i], patches) > 0.5, 0.0, -1e30)
        for j in range(width // (2 * HEAD_DIM)):
            cols = [slice(p * width + j * 128, p * width + (j + 1) * 128) for p in range(3)]
            q = qkv_o[at, cols[0]] * bf16(HEAD_DIM**-0.5)
            k, v = qkv_o[at, cols[1]], qkv_o[at, cols[2]]
            mixed = 0.0
            for low in lows:
                s = dot_nt(q * low, k) + bias
                e = jnp.exp(s - jnp.max(s, -1, keepdims=True))
                pr = (e * (1.0 / jnp.sum(e, -1, keepdims=True))).astype(bf16)
                mixed = mixed + dot(pr, v * low)
            o_o[at, cols[0]] = mixed.astype(bf16)
    x2 = x_o[...] + dot(o_o[...], wout[...]) + bo
    x2_o[...] = x2
    hat2, _ = ln_parts(x2)
    h2_o[...] = (hat2 * g2 + b2).astype(bf16)


def whole(shape):
    return pl.BlockSpec(shape, lambda *_: (0,) * len(shape), pipeline_mode=pl.Buffered(1))


def attend(lengths, act, text, wp, wqkv, wout, params, patches, n):
    examples, slots, width = text.shape
    rows = PATCH_PAD + slots
    steps = examples // n
    blk = lambda w: pl.BlockSpec((n * rows, w), lambda s: (s, 0))
    out = lambda w, t: jax.ShapeDtypeStruct((examples * rows, w), t)
    return pl.pallas_call(
        functools.partial(attend_kernel, n, patches),
        grid=(steps,),
        out_shape=[out(width, f32), out(width, bf16), out(3 * width, bf16), out(width, bf16), out(width, f32), out(width, bf16)],
        in_specs=[
            pl.BlockSpec(memory_space=pltpu.SMEM),
            pl.BlockSpec((n,) + act.shape[1:], lambda s: (s, 0, 0)),
            pl.BlockSpec((n,) + text.shape[1:], lambda s: (s, 0, 0)),
        ]
        + [whole(w.shape) for w in (wp, wqkv, wout, params)],
        out_specs=[blk(width), blk(width), blk(3 * width), blk(width), blk(width), blk(width)],
        compiler_params=pltpu.CompilerParams(vmem_limit_bytes=56 << 20),
        name="attend",
    )(lengths, act, text, wp, wqkv, wout, params)


def ffn_kernel(n, patches, len_ref, h2, x2_h, cot, wu, bu, wd, params, out_h, dx2_h, gup, gdown, gbu, small, g_s, h2t, acc, dh, m_s, du_s, x2, out, sems):
    c, last = pl.program_id(0), pl.num_programs(0) - 1
    examples, seq, width = cot.shape
    rows = PATCH_PAD + seq - patches
    blocks = examples // n
    load = pltpu.make_async_copy(x2_h, x2, sems.at[0, 0])

    def leave(i, at):
        return pltpu.make_async_copy(out.at[i], out_h.at[i], sems.at[1, i]), pltpu.make_async_copy(dh.at[at], dx2_h.at[at], sems.at[2, i])

    @pl.when(c == 0)
    def _():
        load.start()

        def body(i, _):
            at = pl.ds(pl.multiple_of(i * rows, 16), rows)
            valid = valid_of(iota((rows, 1), 0), len_ref[i], patches)
            g_s[at] = (dot(spread(rows, patches, seq), cot[i]) * valid).astype(bf16)
            acc[at] = jnp.zeros((rows, width), f32)
            dh[at] = jnp.zeros((rows, width), f32)
            return 0

        lax.fori_loop(0, examples, body, 0, unroll=2)
        h2t[...] = h2[...].T

    def block(r, sums):
        at = pl.ds(pl.multiple_of(r * (n * rows), 16), n * rows)
        m, slope = smooth_both(dot(h2[at], wu[...]) + bu[13:14])
        m = m.astype(bf16)
        m_s[at] = m
        acc[at] += dot(m, wd[...])
        du = dot_nt(g_s[at], wd[...]) * slope
        sums = sums + colsum(du)
        du = du.astype(bf16)
        du_s[at] = du
        dh[at] += dot_nt(du, wu[...])
        return sums

    gbu[...] = lax.fori_loop(0, blocks, block, jnp.zeros(gbu.shape, f32), unroll=True)
    gup[...] = dot(h2t[...], du_s[...]).astype(bf16)
    gdown[...] = dot_tn(m_s[...], g_s[...]).astype(bf16)

    @pl.when(c == last)
    def _():
        load.wait()

        def body(i, sums):
            at = pl.ds(pl.multiple_of(i * rows, 16), rows)
            valid = valid_of(iota((rows, 1), 0), len_ref[i], patches)
            result = (acc[at] + x2[at] + params[14:15, :width]) * valid
            out[i] = dot(gather_rows(seq, rows, patches), result.astype(bf16)).astype(bf16)
            hat, inv = ln_parts(x2[at])
            g = g_s[at].astype(f32)
            dy = dh[at]
            dh[at] = g + ln_back(dy, hat, inv, params[11:12, :width])
            for copy in leave(i, at):
                copy.start()
            return sums[0] + colsum(g), sums[1] + colsum(dy * hat), sums[2] + colsum(dy)

        zero = jnp.zeros((1, width), f32)
        a, b, d = lax.fori_loop(0, examples, body, (zero, zero, zero), unroll=2)
        small[0:1], small[1:2], small[2:3] = a, b, d
        small[3:8] = jnp.zeros((5, width), f32)

        def wait(i, _):
            for copy in leave(i, pl.ds(pl.multiple_of(i * rows, 16), rows)):
                copy.wait()
            return 0

        lax.fori_loop(0, examples, wait, 0)


def ffn(lengths, h2, x2, cot, wu, wd, params, patches, n, chunk):
    examples, seq, width = cot.shape
    total, hidden = h2.shape[0], wu.shape[1]
    col = lambda rows: pl.BlockSpec((rows, chunk), lambda c: (0, c))
    row = pl.BlockSpec((chunk, width), lambda c: (c, 0))
    return pl.pallas_call(
        functools.partial(ffn_kernel, n, patches),
        grid=(hidden // chunk,),
        out_shape=[
            jax.ShapeDtypeStruct(cot.shape, bf16),
            jax.ShapeDtypeStruct((total, width), f32),
            jax.ShapeDtypeStruct((width, hidden), bf16),
            jax.ShapeDtypeStruct((hidden, width), bf16),
            jax.ShapeDtypeStruct((1, hidden), f32),
            jax.ShapeDtypeStruct((8, width), f32),
        ],
        in_specs=[pl.BlockSpec(memory_space=pltpu.SMEM), whole(h2.shape), pl.BlockSpec(memory_space=pl.ANY), whole(cot.shape), col(width), col(params.shape[0]), row, whole(params.shape)],
        out_specs=[pl.BlockSpec(memory_space=pl.ANY), pl.BlockSpec(memory_space=pl.ANY), col(width), row, col(1), whole((8, width))],
        scratch_shapes=[
            pltpu.VMEM((total, width), bf16),
            pltpu.VMEM((width, total), bf16),
            pltpu.VMEM((total, width), f32),
            pltpu.VMEM((total, width), f32),
            pltpu.VMEM((total, chunk), bf16),
            pltpu.VMEM((total, chunk), bf16),
            pltpu.VMEM((total, width), f32),
            pltpu.VMEM(cot.shape, bf16),
            DMA((3, examples)),
        ],
        compiler_params=pltpu.CompilerParams(vmem_limit_bytes=60 << 20),
        name="ffn",
    )(lengths, h2, x2, cot, wu, params, wd, params)


def attend_back_kernel(A, B, n, patches, slots, cuts, n_sc, *refs):
    (len_ref, dx2, x, h1, qkv, o, act, wp, wqkv, wout, params), refs = refs[:11], refs[11:]
    srcs, refs = refs[:n_sc], refs[n_sc:]
    (dact, gtext, gqkv, gout, gpatch, small, small3), refs = refs[:7], refs[7:]
    sums, refs = refs[:n_sc], refs[n_sc:]
    (aqkv, aout, apatch, do_s, dq_s), refs = refs[:5], refs[5:]
    step, last = pl.program_id(0), pl.num_programs(0) - 1
    width = x.shape[1]
    g1 = params[7:8, :width]
    rows = PATCH_PAD + slots
    lows = lane_masks(HEAD_DIM)
    scale = bf16(HEAD_DIM**-0.5)

    @pl.when(step == 0)
    def _():
        for ref in (aqkv, aout, apatch, small, small3):
            ref[...] = jnp.zeros(ref.shape, f32)

    moves, stages = [], []
    if n_sc:
        pc = Place(A, B)
        pl.when(step == 0)(lambda: pc.greet(False))
        moves = scatter_items(pc, cuts, srcs, sums, refs[: 5 * len(cuts)], refs[5 * len(cuts) :])
        stages = wave_stages(moves, (0, 2, 5, 8, 11), ["start", "second", "third", "fourth", "arrived"])
    progress = Plan(step, 6, 3, stages)
    progress(0)
    db = dx2[...].astype(bf16)
    do_s[...] = dot_nt(db, wout[...]).astype(bf16)
    aout[...] += dot_tn(o[...], db)
    for i in range(n):
        at = slice(i * rows, (i + 1) * rows)
        bias = jnp.where(valid_of(iota((rows, 1), 0), len_ref[step * n + i], patches) > 0.5, 0.0, -1e30)
        for j in range(width // (2 * HEAD_DIM)):
            cols = [slice(p * width + j * 128, p * width + (j + 1) * 128) for p in range(3)]
            q, k, v = qkv[at, cols[0]] * scale, qkv[at, cols[1]], qkv[at, cols[2]]
            ks = k * scale
            do = do_s[at, cols[0]]
            dq = dk = dv = 0.0
            for low in lows:
                s = dot_nt(k * low, q) + bias
                e = jnp.exp(s - jnp.max(s, 0, keepdims=True))
                p = e * (1.0 / jnp.sum(e, 0, keepdims=True))
                dv = dv + dot(p.astype(bf16), do * low)
                dp = dot_nt(v * low, do)
                ds = (p * (dp - jnp.sum(p * dp, 0, keepdims=True))).astype(bf16)
                dk = dk + dot(ds, q * low)
                dq = dq + dot_tn(ds, ks * low)
            dq_s[at, cols[0]], dq_s[at, cols[1]], dq_s[at, cols[2]] = dq.astype(bf16), dk.astype(bf16), dv.astype(bf16)
    progress(1)
    aqkv[...] += dot_tn(h1[...], dq_s[...])
    dh1 = dot_nt(dq_s[...], wqkv[...])
    hat, inv = ln_parts(x[...])
    dx = dx2[...] + ln_back(dh1, hat, inv, g1)
    progress(2)
    dps = []
    for i in range(n):
        keep = jnp.where(iota((slots, 1), 0) < len_ref[step * n + i], 1.0, 0.0).astype(f32)
        gtext[i] = (dx[i * rows + PATCH_PAD : (i + 1) * rows] * keep).astype(bf16)
        inside = iota((PATCH_PAD, 1), 0) < patches
        dps.append(jnp.where(inside, dx[i * rows : i * rows + PATCH_PAD], 0.0).astype(bf16))
    dp = jnp.concatenate(dps, 0)
    dact[...] = dot_nt(dp, wp[...]).reshape(dact.shape)
    apatch[...] += dot_tn(act[...].reshape(n * PATCH_PAD, act.shape[2]), dp)
    small[0:1] += colsum(dh1 * hat)
    small[1:2] += colsum(dh1)
    small[2:3] += colsum(db.astype(f32))
    small[3:4] += colsum(dp.astype(f32))
    small3[0:1] += colsum(dq_s[...].astype(f32))

    @pl.when(step == last)
    def _():
        for m in moves:
            m.drain()
        gqkv[...], gout[...], gpatch[...] = aqkv[...].astype(bf16), aout[...].astype(bf16), apatch[...].astype(bf16)


def attend_back(A, B, lengths, dx2, x, h1, qkv, o, act, wp, wqkv, wout, params, grads, parts, slots, patches, n, cid):
    examples, _, channels = act.shape
    width = x.shape[1]
    rows = PATCH_PAD + slots
    blk = lambda w: pl.BlockSpec((n * rows, w), lambda s: (s, 0))
    assert examples == 6 * n
    cuts = cut([(g.shape[1], q) for g, q in zip(grads, parts)])
    shapes = [(g.shape[0] // (A * B), g.shape[1]) for g in grads]
    hbm = pl.BlockSpec(memory_space=pl.ANY)
    remote = dict(collective_id=cid, has_side_effects=True) if grads else {}
    cube = lambda a, b: pl.BlockSpec((n, a, b), lambda s: (s, 0, 0))
    return pl.pallas_call(
        functools.partial(attend_back_kernel, A, B, n, patches, slots, cuts, len(grads)),
        grid=(examples // n,),
        out_shape=[
            jax.ShapeDtypeStruct(act.shape, f32),
            jax.ShapeDtypeStruct((examples, slots, width), bf16),
            jax.ShapeDtypeStruct(wqkv.shape, bf16),
            jax.ShapeDtypeStruct(wout.shape, bf16),
            jax.ShapeDtypeStruct(wp.shape, bf16),
            jax.ShapeDtypeStruct((8, width), f32),
            jax.ShapeDtypeStruct((8, 3 * width), f32),
        ]
        + [jax.ShapeDtypeStruct(s, f32) for s in shapes],
        in_specs=[pl.BlockSpec(memory_space=pltpu.SMEM), blk(width), blk(width), blk(width), blk(3 * width), blk(width), cube(PATCH_PAD, channels)]
        + [whole(w.shape) for w in (wp, wqkv, wout, params)]
        + [hbm] * len(grads),
        out_specs=[cube(PATCH_PAD, channels), cube(slots, width)] + [whole(s) for s in (wqkv.shape, wout.shape, wp.shape, (8, width), (8, 3 * width), *shapes)],
        scratch_shapes=[pltpu.VMEM(wqkv.shape, f32), pltpu.VMEM(wout.shape, f32), pltpu.VMEM(wp.shape, f32), pltpu.VMEM((n * rows, width), bf16), pltpu.VMEM((n * rows, 3 * width), bf16)]
        + (scatter_buffers(A, B, cuts, shapes) + scatter_sems(A, B, len(cuts)) if grads else []),
        compiler_params=pltpu.CompilerParams(vmem_limit_bytes=62 << 20, **remote),
        name="attend_back",
    )(lengths, dx2, x, h1, qkv, o, act, wp, wqkv, wout, params, *[split_rows(A, B, g) for g in grads])


class Total:
    def __init__(self, pc, j, send, recv, ssem, rsem):
        self.pc, self.send, self.recv = pc, send.at[j], recv.at[j]
        self.ssem, self.rsem = ssem.at[j], rsem.at[j]
        groups = [pc.bpeers, pc.dpeers]
        self.groups, at = [], 0
        for g in groups:
            self.groups.append([(at + k, dev) for k, dev in enumerate(g)])
            at += len(g)

    def copy(self, step, k, dev):
        return rcopy(self.send.at[step], self.recv.at[k], self.ssem.at[k], self.rsem.at[k], dev)

    def put(self, step, v):
        self.send[step] = v
        for k, dev in self.groups[step]:
            self.copy(step, k, dev).start()

    def take(self, step):
        v = self.send[step]
        for k, dev in self.groups[step]:
            self.copy(step, k, dev).wait_recv()
            v = v + self.recv[k]
        return v

    def begin(self, v):
        self.put(0, v)

    def middle(self):
        self.put(1, self.take(0))

    def end(self):
        return self.take(1)

    def drain(self):
        for step in range(2):
            for k, dev in self.groups[step]:
                self.copy(step, k, dev).wait_send()


def total_scratch(A, B, count, shape):
    peers = (B - 1) + (A - 1)
    return [pltpu.VMEM((count, 2) + shape, f32), pltpu.VMEM((count, peers) + shape, f32), DMA((count, peers)), DMA((count, peers))]


def tile_rows(rows):
    return -(-rows // 16) * 16


def together(rows):
    n = 1
    while n * rows % 16:
        n += 1
    return n


def unpack(src, dst, rows):
    padded, cols = src.shape[-2:]
    shards = dst.shape[0] // rows
    flat = src[...].reshape(shards * padded, cols)
    if padded == rows:
        dst[...] = flat
        return
    n = together(rows)
    pick = turn_rows((n * rows, n * padded), rows, padded)
    for t in range(shards // n):
        dst[t * n * rows : (t + 1) * n * rows] = dot(pick, flat[t * n * padded : (t + 1) * n * padded]).astype(bf16)


def turn_rows(shape, rows, padded):
    out, pos = iota(shape, 0), iota(shape, 1)
    shard = jnp.floor((out.astype(f32) + 0.5) * (1.0 / rows)).astype(jnp.int32)
    return jnp.where(pos == out + shard * (padded - rows), 1.0, 0.0).astype(bf16)


def pack(src, dst, rows):
    padded, cols = dst.shape[-2:]
    shards = src.shape[0] // rows
    if padded == rows:
        dst[...] = src.reshape(dst.shape)
        return
    n = together(rows)
    shape = (n * padded, n * rows)
    out, pos = iota(shape, 0), iota(shape, 1)
    shard = jnp.floor((out.astype(f32) + 0.5) * (1.0 / padded)).astype(jnp.int32)
    pick = jnp.where((pos == out - shard * (padded - rows)) & (out - shard * padded < rows), 1.0, 0.0).astype(bf16)
    parts = [dot(pick, src[t * n * rows : (t + 1) * n * rows]).astype(bf16) for t in range(shards // n)]
    dst[...] = jnp.concatenate(parts, 0).reshape(dst.shape)


def unpack_vectors(tab, out, sizes):
    shards = tab.shape[0] * tab.shape[1] * tab.shape[2] * tab.shape[3]
    flat = tab[...].reshape(shards, tab.shape[-2], tab.shape[-1])[:, 0, :]
    out[...] = jnp.zeros(out.shape, f32)
    for v, n in enumerate(sizes):
        wide = n * shards
        lane = iota((128, wide), 1)
        block = jnp.floor((lane.astype(f32) + 0.5) * (1.0 / n)).astype(jnp.int32)
        spot = jnp.where(iota((128, wide), 0) == lane - block * n, 1.0, 0.0).astype(bf16)
        rows = dot(flat[:, 128 * v : 128 * (v + 1)].astype(bf16), spot)
        owner = jnp.where(iota((shards, wide), 0) == block[:shards] if shards <= 128 else block, rows, 0.0)
        out[v : v + 1, :wide] = colsum(owner)


def make_taps(taps, grid):
    places = grid * grid
    i, j = iota((places, places), 0), iota((places, places), 1)
    col = i - grid * jnp.floor((i.astype(f32) + 0.5) * (1.0 / grid)).astype(jnp.int32)
    for t in range(9):
        dr, dc = t // 3 - 1, t % 3 - 1
        hit = (j == i + grid * dr + dc) & (col + dc >= 0) & (col + dc < grid)
        taps[t] = jnp.where(hit, 1.0, 0.0).astype(bf16)


def rows_of(vectors):
    rows = []
    for v in vectors:
        rows += [v[:, q : q + 256] for q in range(0, v.shape[1], 256)]
    if len(rows) < 8:
        rows.append(jnp.zeros((8 - len(rows), 256), f32))
    return jnp.concatenate(rows, 0)


def vectors_of(block, width):
    per = width // 256
    take = lambda k: jnp.concatenate([block[k * per + q : k * per + q + 1] for q in range(per)], 1)
    return take(0), take(1)


VECTORS = ("bn1_gain", "bn1_bias", "bn2_gain", "bn2_bias", "bn3_gain", "bn3_bias", "b_patch", "ln1_gain", "ln1_bias", "b_q", "b_v", "b_out", "ln2_gain", "ln2_bias", "b_up", "b_down")


def moments(s1, s2, total_rows, gain, bias):
    mean = s1 / total_rows
    inv = lax.rsqrt(s2 / total_rows - mean * mean + bn_eps)
    return mean, inv


def stem_kernel(A, B, items, n_mats, sizes, shard_rows, total_rows, *refs):
    n_vec = len(sizes)
    feats, vecs, refs = refs[0], refs[1 : 1 + n_vec], refs[1 + n_vec :]
    near, far_in, refs = refs[:3], refs[3 : n_mats - 1], refs[n_mats - 1 :]
    n_far = n_mats - 4
    far, refs = refs[:n_far], refs[n_far:]
    (act_h, r_h, c_h, e_h, params, stats, w_red, w_conv, w_exp), refs = refs[:9], refs[9:]
    (act, r_o, c_o, e_o, out_sems), refs = refs[:5], refs[5:]
    (p_red, tab, p_conv, p_exp, taps, cols), refs = refs[:6], refs[6:]
    mine, refs = refs[:4], refs[4:]
    sums, sems = refs[:4], refs[4:]
    pc = Place(A, B)
    for src, dst in zip(near, (mine[0], mine[2], mine[3])):
        dst[...] = dot(jnp.where(iota((dst.shape[0], src.shape[0]), 0) == iota((dst.shape[0], src.shape[0]), 1), 1.0, 0.0).astype(bf16), src[...]).astype(bf16)
    mine[1][...] = jnp.zeros(mine[1].shape, f32)
    for v, ref in enumerate(vecs):
        mine[1][:, 128 * v : 128 * v + sizes[v]] = ref[...].astype(f32)
    shards = [*mine, *far_in]
    pc.greet()
    dsts = [p_red, tab, p_conv, p_exp, *far]
    moves = [GatherItem(pc, j, c, order, shards[i], dsts[i], sems) for j, (i, c, order) in enumerate(items)]
    adds = [Total(pc, j, *sums) for j in range(3)]
    examples, patches, channels = feats.shape
    grid = GRID
    vec = lambda v, width: params[v : v + 1, :width]

    def each(fn, width):
        zero = jnp.zeros((1, width), f32)

        def body(i, s):
            v = fn(i)
            return s[0] + colsum(v), s[1] + colsum(v * v)

        return lax.fori_loop(0, examples, body, (zero, zero), unroll=3)

    def norm(v, j, width):
        return (v - stats[2 * j : 2 * j + 1, :width]) * stats[2 * j + 1 : 2 * j + 2, :width] * vec(2 * j, width) + vec(2 * j + 1, width)

    def keep(j, width):
        s1, s2 = vectors_of(adds[j].end(), width)
        mean, inv = moments(s1, s2, total_rows, None, None)
        stats[2 * j : 2 * j + 1, :width] = mean
        stats[2 * j + 1 : 2 * j + 2, :width] = inv

    narrow = r_o.shape[2]

    def first():
        moves[0].arrived()
        unpack(p_red, w_red, shard_rows[0])

        def one(i):
            v = dot(feats[i], w_red[...])
            r_o[i] = v
            return v

        adds[0].begin(rows_of(each(one, narrow)))

    def vectors():
        moves[1].arrived()
        unpack_vectors(tab, params, sizes)

    def second():
        keep(0, narrow)

        def one(i):
            ra = smooth(norm(r_o[i], 0, narrow)).astype(bf16)
            for t in range(9):
                cols[:, t * narrow : (t + 1) * narrow] = dot(taps[t], ra).astype(bf16)
            v = dot(cols[...], w_conv[...])
            c_o[i] = v
            return v

        adds[1].begin(rows_of(each(one, narrow)))

    def third():
        keep(1, narrow)

        def one(i):
            ca = smooth(norm(c_o[i], 1, narrow)).astype(bf16)
            v = dot(ca, w_exp[...])
            e_o[i] = v
            return v

        adds[2].begin(rows_of(each(one, channels)))

    def act_copy(i):
        return pltpu.make_async_copy(act.at[i], act_h.at[i], out_sems.at[3 + i])

    def fourth():
        keep(2, channels)
        wide = spread(act.shape[1], patches, patches)

        def body(i, _):
            v = norm(e_o[i], 2, channels) + feats[i].astype(f32)
            act[i] = dot(wide, smooth(v).astype(bf16)).astype(bf16)
            act_copy(i).start()
            return 0

        lax.fori_loop(0, examples, body, 0, unroll=3)

    saved = [pltpu.make_async_copy(v, h, out_sems.at[k]) for k, (v, h) in enumerate(((r_o, r_h), (c_o, c_h), (e_o, e_h)))]
    make_taps(taps, grid)
    stats[...] = jnp.zeros(stats.shape, f32)

    def ready_conv():
        moves[2].arrived()
        unpack(p_conv, w_conv, shard_rows[1])
        vectors()

    def ready_exp():
        moves[3].arrived()
        unpack(p_exp, w_exp, shard_rows[2])

    hooks = {8: [first], 10: [adds[0].middle, saved[0].start, ready_conv], 12: [second], 14: [adds[1].middle, saved[1].start, ready_exp], 16: [third], 18: [adds[2].middle, saved[2].start], 20: [fourth]}
    wave(moves, (0, 2, 4, 6), ["start", "second", "third", "fourth"], hooks)
    for m in moves:
        m.arrived()
    for m in moves:
        m.drain()
    for t in adds:
        t.drain()
    for t in saved:
        t.wait()
    lax.fori_loop(0, examples, lambda i, _: (act_copy(i).wait(), 0)[1], 0)


def stem_forward(A, B, feats, vecs, mats, pad_rows, parts, cid):
    A2, Z, count = A // 2, B // 2, A * B
    examples, patches, channels = feats.shape
    near, far = mats[:3], mats[3:]
    sizes = [v.shape[0] for v in vecs]
    shard_rows = [m.shape[0] for m in near]
    pads = [jax.ShapeDtypeStruct((tile_rows(m.shape[0]), m.shape[1]), bf16) for m in near]
    shards = [pads[0], jax.ShapeDtypeStruct((1, 128 * len(vecs)), f32), pads[1], pads[2], *far]
    items = cut([(s.shape[1], q) for s, q in zip(shards, (1, 1, 1, 1) + parts)])
    shape = lambda s: (A2, 2, Z, 2) + s.shape
    narrow = near[0].shape[1]
    hbm, vm = pl.BlockSpec(memory_space=pl.ANY), pl.BlockSpec(memory_space=pltpu.VMEM)
    full = [(m.shape[0] * count, m.shape[1]) for m in near]
    outs = pl.pallas_call(
        functools.partial(stem_kernel, A, B, items, len(shards), sizes, shard_rows, float(examples * count * patches)),
        out_shape=[jax.ShapeDtypeStruct(shape(s), s.dtype) for s in far]
        + [
            jax.ShapeDtypeStruct((examples, pad_rows, channels), bf16),
            jax.ShapeDtypeStruct((examples, patches, narrow), f32),
            jax.ShapeDtypeStruct((examples, patches, narrow), f32),
            jax.ShapeDtypeStruct((examples, patches, channels), f32),
            jax.ShapeDtypeStruct((16, sizes[13] * count), f32),
            jax.ShapeDtypeStruct((8, channels), f32),
        ]
        + [jax.ShapeDtypeStruct(s, bf16) for s in full],
        in_specs=[vm] * (1 + len(vecs) + 3) + [hbm] * len(far),
        out_specs=[hbm] * (len(far) + 4) + [vm] * 5,
        scratch_shapes=[
            pltpu.VMEM((examples, pad_rows, channels), bf16),
            pltpu.VMEM((examples, patches, narrow), f32),
            pltpu.VMEM((examples, patches, narrow), f32),
            pltpu.VMEM((examples, patches, channels), f32),
            DMA((3 + examples,)),
        ]
        + [pltpu.VMEM(shape(s), s.dtype) for s in shards[:4]]
        + [pltpu.VMEM((9, patches, patches), bf16), pltpu.VMEM((patches, full[1][0]), bf16)]
        + [pltpu.VMEM(s.shape, s.dtype) for s in shards[:4]]
        + total_scratch(A, B, 3, (8, 256))
        + gather_sems(A, B, len(items)),
        compiler_params=pltpu.CompilerParams(collective_id=cid, has_side_effects=True, vmem_limit_bytes=60 << 20),
        name="stem",
    )(feats, *[v[None] for v in vecs], *near, *far)
    return [g.reshape(-1, g.shape[-1]) for g in outs[: len(far)]], outs[len(far) :]


class Run:
    pass


class Written:
    def __init__(self, out):
        self.out = out

    def second(self):
        pass

    third = fourth = arrived = second


def stem_back_kernel(A, B, cuts, near_rows, total_rows, sizes, n_far, inside, *refs):
    (dact_h, feats_h, red_h, conv_h, expand_h, params, stats, w_red, w_conv, w_exp, small_f, small_b, small_a, small_q), refs = refs[:14], refs[14:]
    far, refs = refs[:n_far], refs[n_far:]
    (gfeats_h, shares), refs = refs[:2], refs[2:]
    far_out, near_out, refs = refs[:n_far], refs[n_far : n_far + 3], refs[n_far + 3 :]
    (dact, feats, expand, red, conv, gfeats, ex_sems, in_sems), refs = refs[:8], refs[8:]
    (ds_s, dy_s, ca_s, taps, gred, gconv, gexp, k_red, k_conv, k_exp), refs = refs[:10], refs[10:]
    sums, vsum, refs = refs[:4], refs[4:8], refs[8:]
    bufs, sems = refs[: 5 * len(cuts)], refs[5 * len(cuts) :]
    def load(k, i):
        src, dst = ((dact_h, dact), (feats_h, feats), (expand_h, expand))[k]
        return pltpu.make_async_copy(src.at[i], dst.at[i], ex_sems.at[k, i])

    def leave_feats(i):
        return pltpu.make_async_copy(gfeats.at[i], gfeats_h.at[i], ex_sems.at[3, i])

    load_conv, load_red = (pltpu.make_async_copy(a, b, in_sems.at[k]) for k, (a, b) in enumerate(((conv_h, conv), (red_h, red))))
    for i in range(feats.shape[0]):
        for k in range(3):
            load(k, i).start()
    load_conv.start()
    load_red.start()
    pc = Place(A, B)
    pc.greet()
    moves = scatter_items(pc, cuts, [*far, k_exp, k_conv, k_red], [*far_out, near_out[2], near_out[1], near_out[0]], bufs, sems)
    big, late = (moves[:-3], moves[-3:]) if inside else (moves, [Written(o) for o in (near_out[2], near_out[1], near_out[0])])
    m_exp, m_conv, m_red = late

    def leave(move, grad, packed, rows):
        if inside:
            pack(grad[...].astype(bf16), packed, rows)
            move.start()
        else:
            move.out[...] = grad[...].astype(bf16)

    adds = [Total(pc, j, *sums) for j in range(3)]
    vec_sum = Total(pc, 0, *vsum)
    examples, patches, channels = feats.shape
    narrow, width = red.shape[2], small_a.shape[1]
    for m in big:
        m.start()
    rows = [small_a[3:4], small_a[0:1], small_a[1:2], small_q[0:1, :width], small_q[0:1, 2 * width :], small_a[2:3], small_f[1:2], small_f[2:3]]
    rows += [small_b[:, q : q + width] for q in range(0, small_b.shape[1], width)]
    rows += [small_f[0:1]]
    vec_sum.begin(jnp.concatenate(rows + [jnp.zeros((16 - len(rows), width), f32)], 0))
    make_taps(taps, GRID)

    def hat_of(ref, i, j, w):
        return (ref[i] - stats[2 * j : 2 * j + 1, :w]) * stats[2 * j + 1 : 2 * j + 2, :w]

    def point(hat, j, w):
        return hat * params[2 * j : 2 * j + 1, :w] + params[2 * j + 1 : 2 * j + 2, :w]

    def each(fn, w):
        zero = jnp.zeros((1, w), f32)

        def body(i, s):
            dy, hat = fn(i)
            return s[0] + colsum(dy), s[1] + colsum(dy * hat)

        return lax.fori_loop(0, examples, body, (zero, zero), unroll=3)

    def norm_back(dy, hat, j, w, totals):
        scale = stats[2 * j + 1 : 2 * j + 2, :w] * params[2 * j : 2 * j + 1, :w]
        return (scale * (dy - totals[0] * (1.0 / total_rows) - hat * (totals[1] * (1.0 / total_rows)))).astype(bf16)

    run = Run()

    def fifth():
        def one(i):
            for k in range(3):
                load(k, i).wait()
            hat = hat_of(expand, i, 2, channels)
            _, slope = smooth_both(point(hat, 2, channels) + feats[i].astype(f32))
            dy = dact[i, :patches] * slope
            ds_s[i] = dy
            return dy, hat

        adds[2].begin(rows_of(each(one, channels)))

    def sixth():
        load_conv.wait()
        run.t3 = vectors_of(adds[2].end(), channels)
        gexp[...] = jnp.zeros(gexp.shape, f32)

        def one(i):
            de = norm_back(ds_s[i], hat_of(expand, i, 2, channels), 2, channels, run.t3)
            hat = hat_of(conv, i, 1, narrow)
            ca, slope = smooth_both(point(hat, 1, narrow))
            gexp[...] += dot_tn(ca.astype(bf16), de)
            dy = dot_nt(de, w_exp[...]) * slope
            dy_s[i] = dy
            return dy, hat

        adds[1].begin(rows_of(each(one, narrow)))
        leave(m_exp, gexp, k_exp, near_rows[2])

    def seventh():
        load_red.wait()
        run.t2 = vectors_of(adds[1].end(), narrow)
        gconv[...] = jnp.zeros(gconv.shape, f32)

        def one(i):
            dc = norm_back(dy_s[i], hat_of(conv, i, 1, narrow), 1, narrow, run.t2)
            hat = hat_of(red, i, 0, narrow)
            ra, slope = smooth_both(point(hat, 0, narrow))
            turned = ra.T.astype(bf16)
            dra = jnp.zeros((patches, narrow), f32)
            for t in range(9):
                moved = dot(taps[8 - t], dc).astype(bf16)
                at = slice(t * narrow, (t + 1) * narrow)
                gconv[at] += dot(turned, moved)
                dra = dra + dot_nt(moved, w_conv[at])
            dy = dra * slope
            dy_s[i] = dy
            return dy, hat

        adds[0].begin(rows_of(each(one, narrow)))
        leave(m_conv, gconv, k_conv, near_rows[1])

    def eighth():
        run.t1 = vectors_of(adds[0].end(), narrow)
        gred[...] = jnp.zeros(gred.shape, f32)

        def body(i, _):
            dr = norm_back(dy_s[i], hat_of(red, i, 0, narrow), 0, narrow, run.t1)
            ca_s[i] = dr
            gred[...] += dot_tn(feats[i], dr)
            return 0

        lax.fori_loop(0, examples, body, 0, unroll=3)
        leave(m_red, gred, k_red, near_rows[0])

    def ninth(lo, hi):
        def body(i, _):
            gfeats[i] = (ds_s[i] + dot_nt(ca_s[i], w_red[...])).astype(bf16)
            leave_feats(i).start()
            return 0

        lax.fori_loop(lo, hi, body, 0, unroll=True)

    def finish():
        v = vec_sum.end()
        me = pc.a * B + pc.b
        one = lambda k: v[k : k + 1]
        rows = [run.t1[1], run.t1[0], run.t2[1], run.t2[0], run.t3[1], run.t3[0], one(0), one(1), one(2), jnp.concatenate([one(3), one(4)], 1)]
        rows += [one(5), one(6), one(7), jnp.concatenate([one(k) for k in range(8, 8 + small_b.shape[1] // width)], 1), one(8 + small_b.shape[1] // width)]
        for k, row in enumerate(rows):
            wide = row.shape[1]
            turn = lax.rem(wide - me * sizes[k], wide)
            shares[k : k + 1] = pltpu.roll(jnp.broadcast_to(row, (8, wide)), turn, 1)[0:1, :128]
        shares[15:16] = jnp.zeros((1, 128), f32)

    queue = wave_stages(big, (0, 2, 4, 6), ["second", "third", "fourth", "arrived"])

    def advance(count):
        for _ in range(min(count, len(queue))):
            queue.pop(0)()

    fifth()
    advance(2)
    adds[2].middle()
    vec_sum.middle()
    advance(4)
    sixth()
    advance(2)
    adds[1].middle()
    m_exp.second()
    advance(4)
    seventh()
    m_exp.third()
    advance(2)
    adds[0].middle()
    m_conv.second()
    m_exp.fourth()
    advance(4)
    eighth()
    m_conv.third()
    advance(2)
    m_red.second()
    ninth(0, examples // 2)
    m_conv.fourth()
    m_red.third()
    advance(2)
    ninth(examples // 2, examples)
    m_red.fourth()
    finish()
    advance(len(queue))
    m_exp.arrived()
    m_conv.arrived()
    m_red.arrived()
    for m in moves:
        m.drain()
    for s in adds + [vec_sum]:
        s.drain()
    lax.fori_loop(0, examples, lambda i, _: (leave_feats(i).wait(), 0)[1], 0)


def stem_backward(A, B, dact, feats, red, conv, expand, params, stats, w_red, w_conv, w_exp, smalls, sizes, grads, parts, inside, cid):
    A2, Z, count = A // 2, B // 2, A * B
    examples, patches, channels = feats.shape
    narrow = red.shape[2]
    near = [w_red, w_conv, w_exp]
    near_rows = [w.shape[0] // count for w in near]
    packed = [(tile_rows(r), w.shape[1]) for r, w in zip(near_rows, near)]
    cuts = cut([(g.shape[1], q) for g, q in zip(grads, parts)] + [(p[1], 1) for p in reversed(packed) if inside])
    shapes = [(g.shape[0] // count, g.shape[1]) for g in grads] + packed[::-1]
    outs = [jax.ShapeDtypeStruct(feats.shape, bf16), jax.ShapeDtypeStruct((16, 128), f32)]
    outs += [jax.ShapeDtypeStruct(s, f32) for s in shapes[: len(grads)]]
    outs += [jax.ShapeDtypeStruct((r, w.shape[1]), f32) if inside else jax.ShapeDtypeStruct(w.shape, bf16) for r, w in zip(near_rows, near)]
    hbm, vm = pl.BlockSpec(memory_space=pl.ANY), pl.BlockSpec(memory_space=pltpu.VMEM)
    lead = (A2, 2, Z, 2)
    return pl.pallas_call(
        functools.partial(stem_back_kernel, A, B, cuts, near_rows, float(examples * count * patches), sizes, len(grads), inside),
        out_shape=outs,
        in_specs=[hbm] * 5 + [vm] * 9 + [hbm] * len(grads),
        out_specs=[hbm] + [vm] * (len(outs) - 1),
        scratch_shapes=[pltpu.VMEM(a.shape, a.dtype) for a in (dact, feats, expand, red, conv, feats)]
        + [
            DMA((4, examples)),
            DMA((2,)),
            pltpu.VMEM((examples, patches, channels), f32),
            pltpu.VMEM((examples, patches, narrow), f32),
            pltpu.VMEM((examples, patches, narrow), bf16),
            pltpu.VMEM((9, patches, patches), bf16),
        ]
        + [pltpu.VMEM(w.shape, f32) for w in near]
        + [pltpu.VMEM(lead + p if inside else (16, 128), bf16) for p in packed]
        + total_scratch(A, B, 3, (8, 256))
        + total_scratch(A, B, 1, (16, smalls[2].shape[1]))
        + (scatter_buffers(A, B, cuts, shapes) + scatter_sems(A, B, len(cuts)) if cuts else []),
        compiler_params=pltpu.CompilerParams(collective_id=cid, has_side_effects=True, vmem_limit_bytes=62 << 20),
        name="stem_back",
    )(dact, feats, red, conv, expand, params, stats, w_red, w_conv, w_exp, *smalls, *[split_rows(A, B, g) for g in grads])


def finish_kernel(n, *refs):
    shares, ins, outs, refs = refs[0], refs[1 : 1 + n], refs[1 + n : 1 + 2 * n], refs[1 + 2 * n :]
    vecs, bufs, sems = refs[: -n - 1], refs[-n - 1 : -1], refs[-1]
    loads = [pltpu.make_async_copy(a, b, sems.at[0, k]) for k, (a, b) in enumerate(zip(ins, bufs))]
    stores = [pltpu.make_async_copy(a, b, sems.at[1, k]) for k, (a, b) in enumerate(zip(bufs, outs))]
    for c in loads:
        c.start()
    for v, ref in enumerate(vecs):
        ref[...] = shares[v, : ref.shape[0]]
    for load, store in zip(loads, stores):
        load.wait()
        store.start()
    for c in stores:
        c.wait()


def finish(shares, sizes, arrays):
    hbm, vm = pl.BlockSpec(memory_space=pl.ANY), pl.BlockSpec(memory_space=pltpu.VMEM)
    n = len(arrays)
    outs = pl.pallas_call(
        functools.partial(finish_kernel, n),
        out_shape=[jax.ShapeDtypeStruct(a.shape, a.dtype) for a in arrays] + [jax.ShapeDtypeStruct((s,), f32) for s in sizes],
        in_specs=[vm] + [hbm] * n,
        out_specs=[hbm] * n + [vm] * len(sizes),
        scratch_shapes=[pltpu.VMEM(a.shape, a.dtype) for a in arrays] + [DMA((2, n))],
        compiler_params=pltpu.CompilerParams(vmem_limit_bytes=60 << 20),
        name="finish",
    )(shares, *arrays)
    return outs[:n], outs[n:]


AXES = ("dp", "fsdp")


def local(
    feats, text, lengths, cotangent,
    w_red, bn1_gain, bn1_bias, w_conv, bn2_gain, bn2_bias, w_exp, bn3_gain, bn3_bias, w_patch, b_patch,
    ln1_gain, ln1_bias, w_qkv, b_qv, w_out, b_out, ln2_gain, ln2_bias, w_up, b_up, w_down, b_down,
):
    A, B = lax.axis_size("dp"), lax.axis_size("fsdp")
    vecs = (bn1_gain, bn1_bias, bn2_gain, bn2_bias, bn3_gain, bn3_bias, b_patch, ln1_gain, ln1_bias, b_qv, b_out, ln2_gain, ln2_bias, b_up, b_down)
    sizes = [v.shape[0] for v in vecs]
    patches, slots = feats.shape[1], text.shape[1]
    far, near = stem_forward(A, B, feats, vecs, (w_red, w_conv, w_exp, w_patch, w_qkv, w_out, w_up, w_down), PATCH_PAD, (1, 3, 1, 4, 3), 0)
    full_patch, full_qkv, full_out, full_up, full_down = far
    act, red, conv, expand, params, stats, full_red, full_conv, full_exp = near
    x, h1, qkv, o, x2, h2 = attend(lengths, act, text, full_patch, full_qkv, full_out, params, patches, 2)
    output, dx2, g_up, g_down, small_b, small_f = ffn(lengths, h2, x2, cotangent, full_up, full_down, params, patches, 2, 1024)
    inside = w_qkv.shape[0] >= 16
    first = [g_up, g_down] if inside else []
    dact, grad_text, g_qkv, g_out, g_patch, small_a, small_q, *sums = attend_back(
        A, B, lengths, dx2, x, h1, qkv, o, act, full_patch, full_qkv, full_out, params, first, (4, 3)[: len(first)], slots, patches, 1, 1
    )
    second = [g_qkv, g_out, g_patch] if inside else []
    grad_feats, shares, *more = stem_backward(
        A, B, dact, feats, red, conv, expand, params, stats, full_red, full_conv, full_exp, (small_f, small_b, small_a, small_q), sizes, second, (3, 1, 1)[: len(second)], inside, 2
    )
    if not inside:
        sums = [lax.psum_scatter(g.astype(f32), AXES, scatter_dimension=0, tiled=True) for g in (g_up, g_down)]
        more = [lax.psum_scatter(g.astype(f32), AXES, scatter_dimension=0, tiled=True) for g in (g_qkv, g_out, g_patch, *more)]
    (grad_feats, grad_text, s_up, s_down, s_qkv, s_out, s_patch, s_red, s_conv, s_exp), vectors = finish(shares, sizes, [grad_feats, grad_text, *sums, *more])
    (s_bn1_gain, s_bn1_bias, s_bn2_gain, s_bn2_bias, s_bn3_gain, s_bn3_bias, s_b_patch, s_ln1_gain, s_ln1_bias, s_b_qv, s_b_out, s_ln2_gain, s_ln2_bias, s_b_up, s_b_down) = vectors
    return (
        output, grad_feats, grad_text,
        s_red, s_bn1_gain, s_bn1_bias, s_conv, s_bn2_gain, s_bn2_bias, s_exp, s_bn3_gain, s_bn3_bias, s_patch, s_b_patch,
        s_ln1_gain, s_ln1_bias, s_qkv, s_b_qv, s_out, s_b_out, s_ln2_gain, s_ln2_bias, s_up, s_b_up, s_down, s_b_down,
    )


def solution(mesh):
    every = ("dp", "fsdp")
    v, m, t = P(every), P(every, None), P(every, None, None)
    weights = (m, v, v, m, v, v, m, v, v, m, v, v, v, m, v, m, v, v, v, m, v, m, v)
    return jax.shard_map(local, mesh=mesh, in_specs=(t, t, v, t) + weights, out_specs=(t, t, t) + weights, check_vma=False)
```
